32 devices in a mesh: dp: 2 (over x), blk: 8 (over z, core), ulysses: 2 (over y).
Axes of the slice: x: 2, y: 2, z: 4, core: 2. Of those that a mesh axis runs over, the one named last changes fastest.
Arguments:
- x_in: bfloat16 [2, 2048, 768], P('dp', ('blk', 'ulysses')), may hold values from -6 to 6
- block_ids: int32 [2, 2048], P('dp'), may hold values from 0 to 15, never falling along the last dimension, each value on 1 to 256 neighbouring positions
- expert_ids: int32 [2, 2048, 2], P('dp', ('blk', 'ulysses')), may hold values from 0 to 15, all different within a row; in each aligned block of 128 rows (0 to 127, 128 to 255, ..., all dimensions but the last counted through in order) at most 21 rows name the same one
- cotangent: bfloat16 [2, 2048, 768], P('dp', ('blk', 'ulysses')), may hold values from -6 to 6
- gain_attn: bfloat16 [2, 768], P(None, ('dp', 'blk', 'ulysses')), may hold values from 0.5 to 1.5
- w_qkv: bfloat16 [2, 768, 2304], P(None, ('dp', 'blk', 'ulysses')), may hold values from -0.21875 to 0.21875
- w_out: bfloat16 [2, 768, 768], P(None, ('dp', 'blk', 'ulysses')), may hold values from -2 to 2
- gain_ffn: bfloat16 [2, 768], P(None, ('dp', 'blk', 'ulysses')), may hold values from 0.5 to 1.5
- w_router: bfloat16 [2, 768, 16], P(None, ('dp', 'blk', 'ulysses')), may hold values from -0.15625 to 0.15625
- shared_gate_up: bfloat16 [2, 768, 4096], P(None, ('dp', 'blk', 'ulysses')), may hold values from -0.21875 to 0.21875
- shared_down: bfloat16 [2, 2048, 768], P(None, ('dp', 'blk', 'ulysses')), may hold values from -0.125 to 0.125
- expert_gate_up: bfloat16 [2, 16, 768, 4096], P(None, ('blk', 'ulysses')), may hold values from -0.21875 to 0.21875
- expert_down: bfloat16 [2, 16, 2048, 768], P(None, ('blk', 'ulysses')), may hold values from -0.125 to 0.125
Outputs:
- y_out: bfloat16 [2, 2048, 768], P('dp', ('blk', 'ulysses'))
- grad_x: bfloat16 [2, 2048, 768], P('dp', ('blk', 'ulysses'))
- grad_gain_attn: float32 [2, 768], P(None, ('dp', 'blk', 'ulysses'))
- grad_qkv: float32 [2, 768, 2304], P(None, ('dp', 'blk', 'ulysses'))
- grad_out: float32 [2, 768, 768], P(None, ('dp', 'blk', 'ulysses'))
- grad_gain_ffn: float32 [2, 768], P(None, ('dp', 'blk', 'ulysses'))
- grad_router: float32 [2, 768, 16], P(None, ('dp', 'blk', 'ulysses'))
- grad_shared_gate_up: float32 [2, 768, 4096], P(None, ('dp', 'blk', 'ulysses'))
- grad_shared_down: float32 [2, 2048, 768], P(None, ('dp', 'blk', 'ulysses'))
- grad_expert_gate_up: float32 [2, 16, 768, 4096], P(None, ('blk', 'ulysses'))
- grad_expert_down: float32 [2, 16, 2048, 768], P(None, ('blk', 'ulysses'))
The draws below stay inside these ranges and needn't reach their ends.
Inputs may be any that keep to these rules, and one draw needn't show every extreme that they name: `block_ids`: block numbers never fall along a sequence; each block is 1 to 256 positions long and some block is exactly 256 long. `expert_ids`: the two experts of a position differ. Within each aligned run of 128 positions of one sequence (the rows of one device) no expert is named more than 21 times, a bound that some block reaches.
All inputs are finite; a program needn't handle non-finite values.
Results may differ from the reference program's by a relative error of at most 0.023.
Values may be sent and summed in bfloat16 or wider, within the bound.
No kernel may reach another device: no remote copies, remote signals or barrier semaphores. Data moves between devices by JAX's collectives and lax.ppermute only.
A program may use at most 320 MiB of HBM per device.

```python
import math
import jax
import jax.numpy as jnp
import numpy as np
from jax import lax

D = 768
HEADS = 12
HEAD = 64
FF = 2048
EXPERTS = 16
LAYERS = 2
BLOCK = 256
STRETCH = 128
MOST = 21
LENGTH = 2048
SEQS = 2
SPLIT = 1
FF_PART = 2048


def levels(own_key, dims, cuts, least, largest):
    def one(axis_at, blocks):
        heights = jax.random.uniform(jax.random.fold_in(jax.random.fold_in(own_key, 6), axis_at), (blocks,), jnp.float32, least / len(cuts), largest / len(cuts))
        return jnp.repeat(jnp.exp(heights), dims[axis_at] // blocks).reshape((-1,) + (1,) * (len(dims) - axis_at - 1))

    factor_of = one(*cuts[0])
    for cut in cuts[1:]:
        factor_of = factor_of * one(*cut)
    return factor_of


def profile(amount, total, reach, lean):
    loads = [(1 << 20) // math.isqrt(rank ** lean) + 1 for rank in range(2, amount + 1)]
    surplus, counts = total - reach - (amount - 1), [1] * (amount - 1)
    while surplus > 0:
        movable = [i for i in range(amount - 1) if counts[i] < reach]
        whole, remaining = sum([loads[i] for i in movable]), surplus
        for i in movable:
            extra = min(reach - counts[i], max(1, remaining * loads[i] // whole), surplus)
            counts[i] = counts[i] + extra
            surplus = surplus - extra
    return np.array([reach] + counts)


def uneven_parts(stream_key, number_of, total, most, skew):
    if number_of == 2:
        one = jax.random.randint(stream_key, (), max(1, total - most), min(most, total - 1) + 1)
        return jnp.stack([one, total - one])
    tallies = jnp.asarray(profile(number_of, total, most, skew), jnp.int32)
    pairs = (number_of - 1) // 2
    source_of, taker = tallies[1:1 + 2 * pairs:2], tallies[2:2 + 2 * pairs:2]
    margin = jnp.minimum(source_of - 1, most - taker)
    moved = jax.random.randint(jax.random.fold_in(stream_key, 1), (pairs,), 0, 1 << 20) % (margin + 1)
    tallies = tallies.at[1:1 + 2 * pairs:2].set(source_of - moved).at[2:2 + 2 * pairs:2].set(taker + moved)
    return tallies[jax.random.permutation(jax.random.fold_in(stream_key, 2), number_of)]


def assign_block(own_key, own, number, rows, count, top, reach, lean):
    sequence = jax.random.permutation(own_key, count)
    packed, common = portions_of(count, rows * top, reach, lean, True), portions_of(count, rows * top, reach, lean, False)
    places = jnp.arange(count)

    def named(tallies, turn):
        used = int((tallies > 0).sum())
        fixed = max(1, used // 4)
        moved = fixed + (places - fixed + turn * (used - fixed)) % max(1, count - fixed)
        return jnp.zeros((count,), jnp.int32).at[sequence[jnp.where(places < fixed, places, moved)]].set(jnp.asarray(tallies, jnp.int32))

    tallies = jnp.where(number % 4 == 0, named(packed, number // 4), named(common, number - number // 4 - 1))
    mixed = jax.random.permutation(jax.random.fold_in(own, 3), count)
    giver, taker = mixed[0:count // 2 * 2:2], mixed[1:count // 2 * 2:2]
    margin = jnp.minimum(tallies[giver] - 1, reach - tallies[taker]) // 2
    margin = jnp.where((giver == sequence[0]) | (taker == sequence[0]) | (tallies[taker] == 0), 0, jnp.maximum(margin, 0))
    moved = jax.random.randint(jax.random.fold_in(own, 4), (count // 2,), 0, 1 << 20) % (margin + 1)
    tallies = tallies.at[giver].add(-moved).at[taker].add(moved)
    labels = jnp.searchsorted(jnp.cumsum(tallies), jnp.arange(rows * top), side="right").astype(jnp.int32)
    listing = labels.reshape(top, rows).T
    listing = listing[jax.random.permutation(jax.random.fold_in(own, 1), rows)]
    turn = jax.random.randint(jax.random.fold_in(own, 2), (rows, 1), 0, top)
    return jnp.take_along_axis(listing, (jnp.arange(top)[None, :] + turn) % top, axis=1)


def portions_of(amount, total, limit, lean, full):
    loads = [(1 << 20) // math.isqrt(standing ** lean) + 1 for standing in range(1, amount + 1)]
    largest = limit if full else min(limit, max(-(-total // amount), total * loads[0] // sum(loads)))
    least = 1 if total - largest >= amount - 1 else 0
    counts, surplus = [largest] + [least] * (amount - 1), total - largest - least * (amount - 1)
    while surplus > 0:
        movable = [i for i in range(1, amount) if counts[i] < largest] or [i for i in range(1, amount) if counts[i] < limit]
        mass, left = sum([loads[i] for i in movable]), surplus
        for i in movable:
            extra = min(limit - counts[i], max(1, left * loads[i] // mass), surplus)
            counts[i] = counts[i] + extra
            surplus = surplus - extra
    return np.array(counts)


def bell_draw(stream_key, dims, width, reach, cuts=(), kind=jnp.bfloat16):
    entries = jax.random.normal(stream_key, dims, jnp.float32) * width
    if len(cuts) > 0:
        entries = levels(stream_key, dims, cuts, -0.22, 0.18) * entries
    return jnp.clip(entries, min=-reach, max=reach).astype(kind)


def setup_inputs(seed: int = 0) -> dict:
    arg_keys = jax.random.split(jax.random.key(seed), 14)
    x_in = bell_draw(arg_keys[0], (SEQS, LENGTH, D), 1.0, 6.0, ((0, 2), (1, 16)))
    block_ids = jax.vmap(lambda own: jnp.searchsorted(jnp.cumsum(uneven_parts(own, LENGTH // (BLOCK // 2), LENGTH, BLOCK, 0)), jnp.arange(LENGTH), side="right"))(jax.random.split(arg_keys[1], SEQS)).reshape((SEQS, LENGTH)).astype(jnp.int32)
    expert_ids_keys = jax.random.split(jax.random.fold_in(arg_keys[2], 1), SEQS * LENGTH // STRETCH)
    expert_ids_turns = jax.random.permutation(jax.random.fold_in(arg_keys[2], 3), SEQS * LENGTH // STRETCH)
    expert_ids = jax.vmap(lambda own, number: assign_block(jax.random.fold_in(arg_keys[2], 2), own, number, STRETCH, EXPERTS, 2, MOST, 0))(expert_ids_keys, expert_ids_turns).reshape((SEQS, LENGTH, 2))
    cotangent = bell_draw(arg_keys[3], (SEQS, LENGTH, D), 1.0, 6.0, ((0, 2), (1, 16)))
    gain_attn = jnp.clip(1.0 + 0.1 * jax.random.normal(arg_keys[4], (LAYERS, D), jnp.float32), 0.5, 1.5).astype(jnp.bfloat16)
    w_qkv = bell_draw(arg_keys[5], (LAYERS, D, 3 * D), D ** -0.5, 0.21875, ((1, 32),))
    w_out = bell_draw(arg_keys[6], (LAYERS, D, D), (max(1, D // 96)) ** -0.5, 2.0, ((1, 32),))
    gain_ffn = jnp.clip(1.0 + 0.1 * jax.random.normal(arg_keys[7], (LAYERS, D), jnp.float32), 0.5, 1.5).astype(jnp.bfloat16)
    w_router = bell_draw(arg_keys[8], (LAYERS, D, EXPERTS), (2 * D) ** -0.5, 0.15625, ((1, 32),))
    shared_gate_up = bell_draw(arg_keys[9], (LAYERS, D, 2 * FF), D ** -0.5, 0.21875, ((1, 32),))
    shared_down = bell_draw(arg_keys[10], (LAYERS, FF, D), FF ** -0.5, 0.125, ((1, 32),))
    expert_gate_up = bell_draw(arg_keys[11], (LAYERS, EXPERTS * SPLIT, D, 2 * FF_PART), D ** -0.5, 0.21875, ((1, 16),))
    expert_down = bell_draw(arg_keys[12], (LAYERS, EXPERTS * SPLIT, FF_PART, D), FF ** -0.5, 0.125, ((1, 16),))
    return dict(x_in=x_in, block_ids=block_ids, expert_ids=expert_ids, cotangent=cotangent, gain_attn=gain_attn, w_qkv=w_qkv, w_out=w_out, gain_ffn=gain_ffn, w_router=w_router, shared_gate_up=shared_gate_up, shared_down=shared_down, expert_gate_up=expert_gate_up, expert_down=expert_down)


NORM_EPS = 1e-06
NEG_BIG = -1e+30
PRECISE = lax.Precision.HIGHEST

@jax.custom_vjp
def low(v):
    return lax.optimization_barrier(v.astype(jnp.bfloat16)).astype(jnp.float32)

@jax.custom_vjp
def low_back(v):
    return v

def low_keep(v):
    return (low(v), None)

def low_pass(kept, grad):
    return (grad,)

def back_keep(v):
    return (v, None)

def back_low(kept, grad):
    return (low(grad),)
low.defvjp(low_keep, low_pass)
low_back.defvjp(back_keep, back_low)

def rms_norm(stream, gain):
    factor = lax.rsqrt(lax.optimization_barrier(jnp.mean(stream * stream, axis=-1, keepdims=True)) + NORM_EPS)
    return stream * factor * gain

def rotate(vectors, positions):
    half_size = HEAD // 2
    spacing = 10000.0 ** (-jnp.arange(half_size).astype(jnp.float32) * 2.0 / HEAD)
    angles = positions.astype(jnp.float32)[:, None] * spacing[None, :]
    cosine = jnp.cos(angles)[:, None, :]
    sine_part = jnp.sin(angles)[:, None, :]
    leading = vectors[..., :half_size]
    trailing = vectors[..., half_size:]
    return jnp.concatenate([leading * cosine - trailing * sine_part, trailing * cosine + leading * sine_part], axis=-1)

def attention(queries, key_rows, values, block_row):
    block_span = math.gcd(LENGTH, 512)
    score_scale = HEAD ** (-0.5)

    def query_block(block_index):
        offset = block_index * block_span
        query_part = lax.dynamic_slice_in_dim(queries, offset, block_span, 0)
        query_ids = lax.dynamic_slice_in_dim(block_row, offset, block_span, 0)
        scores = low_back(jnp.einsum('qhd,khd->hqk', query_part, key_rows, precision=PRECISE) * score_scale)
        allowed = block_row[None, None, :] <= query_ids[None, :, None]
        attn_probs = low(jax.nn.softmax(jnp.where(allowed, scores, NEG_BIG), axis=-1))
        return jnp.einsum('hqk,khd->qhd', attn_probs, values, precision=PRECISE)
    stacked = lax.map(jax.checkpoint(query_block), jnp.arange(LENGTH // block_span, dtype=jnp.int32))
    return stacked.reshape(LENGTH, HEADS, HEAD)

def expert_mix(normed, gate_values, targets, route_masks, joint_all, down_all):
    rows_total = targets.shape[1] // STRETCH * MOST
    joint_all = joint_all.reshape(EXPERTS, SPLIT, D, 2 * FF_PART)
    down_all = down_all.reshape(EXPERTS, SPLIT * FF_PART, D)

    def one_expert(running, pieces):
        joint_w, down_w, target, route_mask = pieces
        gate_w = jnp.transpose(joint_w[:, :, :FF_PART], (1, 0, 2)).reshape(D, FF)
        up_w = jnp.transpose(joint_w[:, :, FF_PART:], (1, 0, 2)).reshape(D, FF)
        buffer = jnp.zeros((rows_total + 1, D), jnp.float32).at[target].add(normed)
        gate_part = low_back(jnp.dot(buffer, gate_w, precision=PRECISE))
        up_part = low_back(jnp.dot(buffer, up_w, precision=PRECISE))
        hidden = low(low_back(jax.nn.silu(gate_part) * up_part))
        result = low_back(jnp.dot(hidden, down_w, precision=PRECISE))
        weight = lax.optimization_barrier(jnp.sum(gate_values * route_mask, axis=1, keepdims=True))
        return (running + result[target] * weight, None)
    initial = jnp.zeros_like(normed)
    return lax.scan(jax.checkpoint(one_expert), initial, (joint_all, down_all, targets, route_masks))[0]

def block_layer(stream, positions, block_ids, route_ids, targets, route_masks, weights):
    gain_one, qkv_w, out_w, gain_two, router_w, shared_w, shared_down_w, joint_all, down_all = weights
    tokens_all = stream.shape[0]
    normed_attn = low(rms_norm(stream, gain_one))
    projected = jnp.dot(normed_attn, qkv_w, precision=PRECISE)
    queries = low(low_back(rotate(low_back(projected[:, :D]).reshape(tokens_all, HEADS, HEAD), positions)))
    key_rows = low(low_back(rotate(low_back(projected[:, D:2 * D]).reshape(tokens_all, HEADS, HEAD), positions)))
    values = low(low_back(projected[:, 2 * D:])).reshape(tokens_all, HEADS, HEAD)
    pieces = []
    for seq_index in range(SEQS):
        first_row = seq_index * LENGTH
        pieces.append(attention(queries[first_row:first_row + LENGTH], key_rows[first_row:first_row + LENGTH], values[first_row:first_row + LENGTH], block_ids[seq_index]))
    mixed_heads = low(low_back(jnp.concatenate(pieces, axis=0).reshape(tokens_all, D)))
    middle = stream + low_back(jnp.dot(mixed_heads, out_w, precision=PRECISE))
    normed_ffn = low(rms_norm(middle, gain_two))
    logits = jnp.dot(normed_ffn, router_w, precision=PRECISE)
    gate_values = jax.nn.softmax(jnp.take_along_axis(logits, route_ids, axis=1), axis=-1)
    shared_joint = jnp.dot(normed_ffn, shared_w, precision=PRECISE)
    gate_part = low_back(shared_joint[:, :FF])
    up_part = low_back(shared_joint[:, FF:])
    shared_hidden = low(low_back(jax.nn.silu(gate_part) * up_part))
    shared_out = low_back(jnp.dot(shared_hidden, shared_down_w, precision=PRECISE))
    routed_out = expert_mix(normed_ffn, gate_values, targets, route_masks, joint_all, down_all)
    return middle + shared_out + routed_out

def reference(x_in, block_ids, expert_ids, cotangent, gain_attn, w_qkv, w_out, gain_ffn, w_router, shared_gate_up, shared_down, expert_gate_up, expert_down):
    tokens_all = SEQS * LENGTH
    route_ids = expert_ids.reshape(tokens_all, 2).astype(jnp.int32)
    route_hits = (route_ids[:, :, None] == jnp.arange(EXPERTS, dtype=jnp.int32)[None, None, :]).astype(jnp.int32)
    slot_order = jnp.cumsum(route_hits.reshape(tokens_all // STRETCH, 2 * STRETCH, EXPERTS), axis=1).reshape(tokens_all, 2, EXPERTS) - 1
    slot_index = lax.optimization_barrier(jnp.sum(route_hits * slot_order, axis=1))
    chosen_any = lax.optimization_barrier(jnp.sum(route_hits, axis=1))
    block_base = jnp.arange(tokens_all, dtype=jnp.int32) // STRETCH * MOST
    dump_row = tokens_all // STRETCH * MOST
    targets = jnp.where(chosen_any > 0, block_base[:, None] + slot_index, dump_row).T.astype(jnp.int32)
    route_masks = jnp.transpose(route_hits, (2, 0, 1)).astype(jnp.float32)
    positions = jnp.tile(jnp.arange(LENGTH, dtype=jnp.int32), SEQS)
    block_rows = block_ids.astype(jnp.int32)

    def forward(stream, gain_a, qkv_w, out_w, gain_f, router_w, shared_w, shared_down_w, joint_all, down_all):
        for layer_index in range(LAYERS):
            stream = block_layer(stream, positions, block_rows, route_ids, targets, route_masks, (gain_a[layer_index], qkv_w[layer_index], out_w[layer_index], gain_f[layer_index], router_w[layer_index], shared_w[layer_index], shared_down_w[layer_index], joint_all[layer_index], down_all[layer_index]))
        return stream
    inputs = (x_in.reshape(tokens_all, D).astype(jnp.float32), gain_attn.astype(jnp.float32), w_qkv.astype(jnp.float32), w_out.astype(jnp.float32), gain_ffn.astype(jnp.float32), w_router.astype(jnp.float32), shared_gate_up.astype(jnp.float32), shared_down.astype(jnp.float32), expert_gate_up.astype(jnp.float32), expert_down.astype(jnp.float32))
    result, pullback = jax.vjp(forward, *inputs)
    gradients = pullback(cotangent.reshape(tokens_all, D).astype(jnp.float32))
    return (result.reshape(SEQS, LENGTH, D).astype(jnp.bfloat16), gradients[0].reshape(SEQS, LENGTH, D).astype(jnp.bfloat16), gradients[1], gradients[2], gradients[3], gradients[4], gradients[5], gradients[6], gradients[7], gradients[8], gradients[9])
```

```python
import functools

import jax
import jax.numpy as jnp
from jax import lax
from jax.experimental import pallas as pl
from jax.experimental.pallas import tpu as pltpu
from jax.sharding import Mesh
from jax.sharding import PartitionSpec as P

D = 768
HEADS = 12
HEAD = 64
FF = 2048
EXPERTS = 16
LAYERS = 2
MOST = 21
TEAM_SIZE = 4
TEAM_HEADS = HEADS // TEAM_SIZE

ALL = ("dp", "z", "core", "ulysses")
SEQ = ("z", "core", "ulysses")
TEAM = ("core", "ulysses")
REST = ("dp", "z")

NORM_EPS = 1e-06
NEG_BIG = -1e30
PRECISE = lax.Precision.HIGHEST
F32 = jnp.float32
BF16 = jnp.bfloat16
QUERY_TILE = 256
VMEM_LIMIT = 48 * 1024 * 1024


def contract(left, right, left_dim, right_dim):
    return lax.dot_general(
        left, right, (((left_dim,), (right_dim,)), ((), ())), preferred_element_type=F32
    )


def exchange(rows, axes):
    return lax.all_to_all(rows, axes, split_axis=0, concat_axis=0, tiled=True)


SWAP = [(0, 1), (1, 0)]


def from_member(rows, turn):
    if turn == 1:
        return lax.ppermute(rows, "ulysses", SWAP)
    if turn == 2:
        return lax.ppermute(rows, "core", SWAP)
    return lax.ppermute(rows, TEAM, [(i, 3 - i) for i in range(4)])


def team_gather(rows):
    return jnp.stack([rows] + [from_member(rows, turn) for turn in (1, 2, 3)])


def in_order(stacked, member):
    turns = [jnp.equal(member, i) for i in range(4)]
    pieces = []
    for k in range(4):
        piece = stacked[k ^ 3]
        for i in range(3):
            piece = jnp.where(turns[i], stacked[k ^ i], piece)
        pieces.append(piece)
    return jnp.stack(pieces)


def team_sum(parts):
    total = parts[0].astype(F32)
    for turn in (1, 2, 3):
        total = total + from_member(parts[turn].astype(BF16), turn).astype(F32)
    return total


def rms_factor(stream):
    return lax.rsqrt(jnp.mean(stream * stream, axis=-1, keepdims=True) + NORM_EPS)


def norm_back(stream, gain, factor, upstream):
    weighted = upstream * gain
    inner_mean = jnp.mean(weighted * stream, axis=-1, keepdims=True)
    grad_stream = factor * weighted - stream * factor * factor * factor * inner_mean
    grad_gain = jnp.sum(upstream * stream * factor, axis=0)
    return (grad_stream, grad_gain)


def attention_kernel(full_ref, some_ref, base_ref, rows_ref, limit_ref, out_ref, wide_ref, log_ref, keys):
    span = rows_ref.shape[2]
    step = pl.program_id(0)
    per_block = span // QUERY_TILE

    @pl.when(step == 0)
    def _():
        for s in range(rows_ref.shape[0]):
            keys[s] = rows_ref[s, HEAD : 2 * HEAD, :].T

    tile = base_ref[0] + step
    lanes = pl.ds(pl.multiple_of((tile % per_block) * QUERY_TILE, QUERY_TILE), QUERY_TILE)
    queries = rows_ref[tile // per_block, 0:HEAD, lanes] * BF16(HEAD**-0.5)
    limit = limit_ref[...]
    key_index = lax.broadcasted_iota(jnp.int32, (span, QUERY_TILE), 0)

    def sweep(s, state, masked):
        highest, total, running = state
        scores = jnp.dot(keys[s], queries, preferred_element_type=F32)
        if masked:
            scores = jnp.where(key_index < limit - s * span, scores, NEG_BIG)
        raised = jnp.maximum(highest, jnp.max(scores, axis=0, keepdims=True))
        terms = jnp.exp(scores - raised)
        shrink = jnp.exp(highest - raised)
        total = total * shrink + jnp.sum(terms, axis=0, keepdims=True)
        running = running * shrink + jnp.dot(
            rows_ref[s, 2 * HEAD :, :], terms.astype(BF16), preferred_element_type=F32
        )
        return (raised, total, running)

    state = (
        jnp.full((1, QUERY_TILE), NEG_BIG, F32),
        jnp.zeros((1, QUERY_TILE), F32),
        jnp.zeros((HEAD, QUERY_TILE), F32),
    )
    state = lax.fori_loop(0, full_ref[step], lambda s, c: sweep(s, c, False), state)
    state = lax.fori_loop(full_ref[step], some_ref[step], lambda s, c: sweep(s, c, True), state)
    highest, total, running = state
    result = running / total
    log_ref[...] = highest + jnp.log(total)
    wide_ref[...] = result
    stretch = out_ref.shape[2]
    for i in range(QUERY_TILE // stretch):
        out_ref[i] = result[:, i * stretch : (i + 1) * stretch].astype(BF16)


def attention_back_kernel(
    full_ref, some_ref, base_ref, rows_ref, limit_ref, grad_ref, wide_ref, log_ref, out_ref, keys, values, key_sum, value_sum
):
    span = rows_ref.shape[2]
    blocks = rows_ref.shape[0]
    step = pl.program_id(0)
    per_block = span // QUERY_TILE

    @pl.when(step == 0)
    def _():
        for s in range(blocks):
            keys[s] = rows_ref[s, HEAD : 2 * HEAD, :].T
            values[s] = rows_ref[s, 2 * HEAD :, :].T
        key_sum[...] = jnp.zeros_like(key_sum)
        value_sum[...] = jnp.zeros_like(value_sum)
        out_ref[...] = jnp.zeros_like(out_ref)

    tile = base_ref[0] + step
    lanes = pl.ds(pl.multiple_of((tile % per_block) * QUERY_TILE, QUERY_TILE), QUERY_TILE)
    queries = rows_ref[tile // per_block, 0:HEAD, lanes] * BF16(HEAD**-0.5)
    limit = limit_ref[...]
    key_index = lax.broadcasted_iota(jnp.int32, (span, QUERY_TILE), 0)
    grads = jnp.concatenate([grad_ref[i] for i in range(grad_ref.shape[0])], axis=1)
    delta = jnp.sum(grads.astype(F32) * wide_ref[...], axis=0, keepdims=True)
    logs = log_ref[...]

    def sweep(s, query_grad, masked):
        scores = jnp.dot(keys[s], queries, preferred_element_type=F32)
        probs = jnp.exp(scores - logs)
        if masked:
            probs = jnp.where(key_index < limit - s * span, probs, 0.0)
        prob_grad = jnp.dot(values[s], grads, preferred_element_type=F32)
        score_grad = (probs * (prob_grad - delta)).astype(BF16)
        value_sum[s] += contract(grads, probs.astype(BF16), 1, 1)
        key_sum[s] += contract(queries, score_grad, 1, 1)
        return query_grad + jnp.dot(
            rows_ref[s, HEAD : 2 * HEAD, :], score_grad, preferred_element_type=F32
        )

    query_grad = jnp.zeros((HEAD, QUERY_TILE), F32)
    query_grad = lax.fori_loop(0, full_ref[step], lambda s, c: sweep(s, c, False), query_grad)
    query_grad = lax.fori_loop(
        full_ref[step], some_ref[step], lambda s, c: sweep(s, c, True), query_grad
    )
    out_ref[tile // per_block, 0:HEAD, lanes] = (query_grad * HEAD**-0.5).astype(BF16)

    @pl.when(step == pl.num_programs(0) - 1)
    def _():
        out_ref[:, HEAD : 2 * HEAD, :] = key_sum[...].astype(BF16)
        out_ref[:, 2 * HEAD :, :] = value_sum[...].astype(BF16)


def whole(shape):
    return pl.BlockSpec(shape, lambda step, *_: (0,) * len(shape))


def tile_at(step, full, some, base):
    return (0, base[0] + step)


def attention_cost(rows, tiles, dots):
    span = rows.shape[0] * rows.shape[2]
    return pl.CostEstimate(
        flops=dots * 4 * tiles * QUERY_TILE * span * HEAD,
        bytes_accessed=rows.size * 4,
        transcendentals=tiles * QUERY_TILE * span,
    )


def attention(rows, spans, stretch):
    full, some, base, limit, tiles = spans
    blocks, _, span = rows.shape
    length = tiles * QUERY_TILE
    return pl.pallas_call(
        attention_kernel,
        grid_spec=pltpu.PrefetchScalarGridSpec(
            num_scalar_prefetch=3,
            grid=(tiles,),
            in_specs=[whole(rows.shape), pl.BlockSpec((1, QUERY_TILE), tile_at)],
            out_specs=[
                pl.BlockSpec((QUERY_TILE // stretch, HEAD, stretch), lambda step, *_: (step, 0, 0)),
                pl.BlockSpec((HEAD, QUERY_TILE), lambda step, *_: (0, step)),
                pl.BlockSpec((1, QUERY_TILE), lambda step, *_: (0, step)),
            ],
            scratch_shapes=[pltpu.VMEM((blocks, span, HEAD), BF16)],
        ),
        out_shape=[
            jax.ShapeDtypeStruct((length // stretch, HEAD, stretch), BF16),
            jax.ShapeDtypeStruct((HEAD, length), F32),
            jax.ShapeDtypeStruct((1, length), F32),
        ],
        compiler_params=pltpu.CompilerParams(vmem_limit_bytes=VMEM_LIMIT),
        cost_estimate=attention_cost(rows, tiles, 1),
        name="attend",
    )(full, some, base, rows, limit)


def attention_back(rows, spans, grads, wide, logs):
    full, some, base, limit, tiles = spans
    blocks, _, span = rows.shape
    stretch = grads.shape[2]
    return pl.pallas_call(
        attention_back_kernel,
        grid_spec=pltpu.PrefetchScalarGridSpec(
            num_scalar_prefetch=3,
            grid=(tiles,),
            in_specs=[
                whole(rows.shape),
                pl.BlockSpec((1, QUERY_TILE), tile_at),
                pl.BlockSpec((QUERY_TILE // stretch, HEAD, stretch), lambda step, *_: (step, 0, 0)),
                pl.BlockSpec((HEAD, QUERY_TILE), lambda step, *_: (0, step)),
                pl.BlockSpec((1, QUERY_TILE), lambda step, *_: (0, step)),
            ],
            out_specs=whole(rows.shape),
            scratch_shapes=[
                pltpu.VMEM((blocks, span, HEAD), BF16),
                pltpu.VMEM((blocks, span, HEAD), BF16),
                pltpu.VMEM((blocks, HEAD, span), F32),
                pltpu.VMEM((blocks, HEAD, span), F32),
            ],
        ),
        out_shape=jax.ShapeDtypeStruct(rows.shape, BF16),
        compiler_params=pltpu.CompilerParams(vmem_limit_bytes=VMEM_LIMIT),
        cost_estimate=attention_cost(rows, tiles, 3),
        name="attend_back",
    )(full, some, base, rows, limit, grads, wide, logs)


def turn_heads(parts, cosine, sine, direction):
    first, second = parts[:, :2, 0], parts[:, :2, 1]
    turned = jnp.stack(
        [
            first * cosine - direction * (second * sine),
            second * cosine + direction * (first * sine),
        ],
        axis=2,
    )
    return jnp.concatenate([turned, parts[:, 2:]], axis=1)


def swiglu_back(gate_pre, up_pre, hidden_grad):
    sigmoid_gate = jax.nn.sigmoid(gate_pre)
    silu_gate = gate_pre * sigmoid_gate
    gate_grad = hidden_grad * up_pre * (sigmoid_gate + silu_gate * (1.0 - sigmoid_gate))
    up_grad = hidden_grad * silu_gate
    return (gate_grad.astype(BF16), up_grad.astype(BF16))


def expert_grad_kernel(has_before, rows_ref, grads_ref, gate_ref, up_ref, down_ref, *refs):
    joint_out, down_out, up_hold = refs[-3:]

    @pl.when(pl.program_id(1) == 0)
    def _():
        rows = rows_ref[...]
        grads = grads_ref[...]
        gate_pre = jnp.dot(rows, gate_ref[0, 0], preferred_element_type=F32)
        up_pre = jnp.dot(rows, up_ref[0, 0], preferred_element_type=F32)
        hidden_grad = contract(grads, down_ref[0, 0], 1, 1).astype(BF16).astype(F32)
        hidden = (gate_pre * jax.nn.sigmoid(gate_pre) * up_pre).astype(BF16)
        gate_grad, up_grad = swiglu_back(gate_pre, up_pre, hidden_grad)
        up_hold[...] = up_grad
        down_out[0, 0] = contract(hidden, grads, 0, 0)
        joint_out[0, 0] = contract(rows, gate_grad, 0, 0)

    @pl.when(pl.program_id(1) == 1)
    def _():
        joint_out[0, 0] = contract(rows_ref[...], up_hold[...], 0, 0)


def expert_grads(layer, rows, grads, joint, down, before):
    half = joint.shape[3] // 2
    chunk = min(512, half)
    chunks = half // chunk
    count = rows.shape[0]
    in_specs = [
        pl.BlockSpec((count, D), lambda i, h: (0, 0)),
        pl.BlockSpec((count, D), lambda i, h: (0, 0)),
        pl.BlockSpec((1, 1, D, chunk), lambda i, h: (layer, 0, 0, i)),
        pl.BlockSpec((1, 1, D, chunk), lambda i, h: (layer, 0, 0, chunks + i)),
        pl.BlockSpec((1, 1, chunk, D), lambda i, h: (layer, 0, i, 0)),
    ]
    operands = [rows, grads, joint, joint, down]
    aliases = {}
    if before is not None:
        in_specs += [pl.BlockSpec(memory_space=pl.ANY)] * 2
        operands += list(before)
        aliases = {5: 0, 6: 1}
    return pl.pallas_call(
        functools.partial(expert_grad_kernel, before is not None),
        grid=(chunks, 2),
        in_specs=in_specs,
        out_specs=[
            pl.BlockSpec((1, 1, D, chunk), lambda i, h: (layer, 0, 0, h * chunks + i)),
            pl.BlockSpec((1, 1, chunk, D), lambda i, h: (layer, 0, i, 0)),
        ],
        out_shape=[
            jax.ShapeDtypeStruct(joint.shape, F32),
            jax.ShapeDtypeStruct(down.shape, F32),
        ],
        scratch_shapes=[pltpu.VMEM((count, chunk), BF16)],
        input_output_aliases=aliases,
        compiler_params=pltpu.CompilerParams(vmem_limit_bytes=VMEM_LIMIT),
        cost_estimate=pl.CostEstimate(
            flops=12 * count * D * half,
            bytes_accessed=18 * D * half,
            transcendentals=count * half,
        ),
        name="expert_grads",
    )(*operands)


def route_tables(route_ids):
    stretch_rows = route_ids.shape[0]
    experts_row = jnp.arange(EXPERTS, dtype=jnp.int32)
    route_hits = (route_ids[:, :, None] == experts_row[None, None, :]).astype(jnp.int32)
    running = (
        jnp.cumsum(route_hits.reshape(2 * stretch_rows, EXPERTS), axis=0).reshape(
            stretch_rows, 2, EXPERTS
        )
        - 1
    )
    slot_index = jnp.sum(route_hits * running, axis=2)
    route_rows = route_ids * MOST + slot_index
    all_rows = jnp.arange(EXPERTS * MOST, dtype=jnp.int32)
    tables = [
        (route_rows[:, c, None] == all_rows[None, :]).astype(BF16) for c in range(2)
    ]
    return (tables, route_hits.astype(F32))


def send_rows(outgoing, split_count):
    outgoing = outgoing.reshape(EXPERTS, MOST, D)
    if split_count > 1:
        outgoing = jnp.repeat(outgoing, split_count, axis=0)
    arrived = exchange(outgoing, SEQ)
    return arrived.reshape(-1, D)


def return_rows(rows, split_count):
    returned = exchange(rows.astype(BF16).reshape(-1, MOST, D), SEQ)
    if split_count > 1:
        returned = (
            returned.reshape(EXPERTS, split_count, MOST, D).astype(F32).sum(axis=1)
        ).astype(BF16)
    return returned.reshape(EXPERTS * MOST, D)


def forward_layer(layer, stream, first_rows, weights, experts, context):
    gain_one, qkv_weight, out_weight, gain_two, router_weight, joint_weight, down_weight = weights
    expert_joint, expert_down = experts
    stretch = stream.shape[0]
    group = TEAM_SIZE * stretch
    member = context["member"]
    factor_one = rms_factor(stream)
    if first_rows is not None:
        wide_rows = first_rows.astype(F32)
        normed_team = (wide_rows * rms_factor(wide_rows) * gain_one).astype(BF16)
    else:
        normed = (stream * factor_one * gain_one).astype(BF16)
        normed_team = in_order(team_gather(normed), member).reshape(group, D)
    projected = contract(qkv_weight, normed_team, 0, 1)
    turned = turn_heads(
        projected.reshape(TEAM_HEADS, 3, 2, HEAD // 2, group),
        context["cosine"],
        context["sine"],
        1.0,
    )
    heads = turned.astype(BF16).reshape(TEAM_HEADS, 3 * HEAD, group)
    heads = jnp.concatenate([heads, jnp.zeros((1,) + heads.shape[1:], BF16)], axis=0)
    parts = context["parts"]
    if parts > 1:
        heads = jnp.repeat(heads, parts, axis=0)
    head_rows = exchange(heads, "z")
    attended, wide, logs = attention(head_rows, context["spans"], stretch)
    pieces = context["pieces"]
    if parts > 1:
        attended = lax.dynamic_update_slice_in_dim(
            jnp.zeros((pieces, HEAD, stretch), BF16),
            attended,
            context["part"] * (pieces // parts),
            0,
        )
    back = exchange(attended, SEQ)
    if parts > 1:
        back = (
            back.reshape(TEAM_SIZE, parts, TEAM_SIZE, HEAD, stretch).astype(F32).sum(axis=1)
        ).astype(BF16)
    back = back.reshape(TEAM_SIZE, TEAM_SIZE, HEAD, stretch)[:TEAM_HEADS]
    mixed = back.transpose(1, 0, 2, 3).reshape(D, stretch)
    middle = stream + contract(mixed, out_weight, 0, 0)
    factor_two = rms_factor(middle)
    normed_ffn = (middle * factor_two * gain_two).astype(BF16)

    table_one, table_two = context["tables"]
    table = table_one + table_two
    split_count = context["split_count"]
    arrived = send_rows(contract(table, normed_ffn, 0, 0).astype(BF16), split_count)
    ffn_team = team_gather(normed_ffn).reshape(group, D)
    logits = jnp.dot(normed_ffn, router_weight, preferred_element_type=F32)
    picked = jnp.sum(logits[:, None, :] * context["hits"], axis=2)
    gate_values = jax.nn.softmax(picked, axis=1)

    shared_joint = jnp.dot(ffn_team, joint_weight, preferred_element_type=F32)
    half = shared_joint.shape[1] // 2
    shared_hidden = (jax.nn.silu(shared_joint[:, :half]) * shared_joint[:, half:]).astype(BF16)
    shared_out = team_sum(
        jnp.dot(shared_hidden, down_weight, preferred_element_type=F32).reshape(
            TEAM_SIZE, stretch, D
        )
    )

    joint_pre = jnp.dot(arrived, expert_joint[layer, 0], preferred_element_type=F32)
    part_width = joint_pre.shape[1] // 2
    hidden = (jax.nn.silu(joint_pre[:, :part_width]) * joint_pre[:, part_width:]).astype(BF16)
    partial_out = jnp.dot(hidden, expert_down[layer, 0], preferred_element_type=F32)
    returned = return_rows(partial_out, split_count)
    choice_one = jnp.dot(table_one, returned, preferred_element_type=F32)
    choice_two = jnp.dot(table_two, returned, preferred_element_type=F32)
    output = (
        middle
        + shared_out
        + gate_values[:, 0:1] * choice_one
        + gate_values[:, 1:2] * choice_two
    )
    saved = dict(
        stream=stream,
        factor_one=factor_one,
        normed_team=normed_team,
        head_rows=head_rows,
        wide=wide,
        logs=logs,
        mixed=mixed,
        middle=middle,
        factor_two=factor_two,
        normed_ffn=normed_ffn,
        ffn_team=ffn_team,
        gate_values=gate_values,
        shared_joint=shared_joint,
        shared_hidden=shared_hidden,
        choices=(choice_one, choice_two),
        arrived=arrived,
        joint_pre=joint_pre,
    )
    return (output, saved)


def both_halves(rows):
    other = lax.ppermute(rows, "dp", SWAP)
    first = lax.axis_index("dp") == 0
    return jnp.concatenate([jnp.where(first, rows, other), jnp.where(first, other, rows)], axis=0)


def backward_layer(layer, upstream, weights, experts, context, saved, before):
    gain_one, qkv_weight, out_weight, gain_two, router_weight, joint_weight, down_weight = weights
    expert_joint, expert_down = experts
    stretch = upstream.shape[0]
    group = TEAM_SIZE * stretch
    member = context["member"]
    split_count = context["split_count"]
    table_one, table_two = context["tables"]
    gate_values = saved["gate_values"]

    outgoing = contract(table_one, (gate_values[:, 0:1] * upstream).astype(BF16), 0, 0) + contract(
        table_two, (gate_values[:, 1:2] * upstream).astype(BF16), 0, 0
    )
    arrived_grad = send_rows(outgoing.astype(BF16), split_count)
    joint_pre = saved["joint_pre"]
    part_width = joint_pre.shape[1] // 2
    hidden_grad = (
        contract(arrived_grad, expert_down[layer, 0], 1, 1).astype(BF16).astype(F32)
    )
    pre_grad = jnp.concatenate(
        swiglu_back(joint_pre[:, :part_width], joint_pre[:, part_width:], hidden_grad), axis=1
    )
    returned_grad = return_rows(contract(pre_grad, expert_joint[layer, 0], 1, 1), split_count)

    grad_team = team_gather(upstream.astype(BF16)).reshape(group, D)
    shared_joint = saved["shared_joint"]
    half = shared_joint.shape[1] // 2
    shared_hidden_grad = contract(grad_team, down_weight, 1, 1).astype(BF16).astype(F32)
    shared_joint_grad = jnp.concatenate(
        swiglu_back(shared_joint[:, :half], shared_joint[:, half:], shared_hidden_grad), axis=1
    )
    normed_grad = team_sum(
        contract(shared_joint_grad, joint_weight, 1, 1).reshape(TEAM_SIZE, stretch, D)
    )
    grad_down = contract(saved["shared_hidden"], grad_team, 0, 0).astype(BF16)
    grad_joint = contract(saved["ffn_team"], shared_joint_grad, 0, 0).astype(BF16)

    choice_one, choice_two = saved["choices"]
    lead_grad = (
        gate_values[:, 0:1]
        * gate_values[:, 1:2]
        * jnp.sum((choice_one - choice_two) * upstream, axis=1, keepdims=True)
    )
    hits = context["hits"]
    logit_grad = lead_grad * (hits[:, 0, :] - hits[:, 1, :])
    grad_router = jnp.dot(saved["normed_ffn"].astype(F32).T, logit_grad, precision=PRECISE)
    normed_grad = (
        normed_grad
        + jnp.dot(logit_grad, router_weight.astype(F32).T, precision=PRECISE)
        + jnp.dot(table_one + table_two, returned_grad, preferred_element_type=F32)
    )
    norm_grad_two, grad_gain_two = norm_back(
        saved["middle"], gain_two, saved["factor_two"], normed_grad
    )
    middle_grad = upstream + norm_grad_two

    attn_grad = middle_grad.astype(BF16)
    grad_out = jnp.dot(saved["mixed"], attn_grad, preferred_element_type=F32).astype(BF16)
    mixed_grad = contract(out_weight, attn_grad, 1, 1).astype(BF16)
    mixed_grad = mixed_grad.reshape(TEAM_SIZE, TEAM_HEADS, HEAD, stretch).transpose(1, 0, 2, 3)
    mixed_grad = jnp.concatenate(
        [mixed_grad, jnp.zeros((1,) + mixed_grad.shape[1:], BF16)], axis=0
    )
    parts = context["parts"]
    if parts > 1:
        mixed_grad = jnp.repeat(mixed_grad, parts, axis=0)
    pieces = context["pieces"]
    head_grad = exchange(mixed_grad.reshape(-1, HEAD, stretch), SEQ)
    if parts > 1:
        head_grad = lax.dynamic_slice_in_dim(
            head_grad, context["part"] * (pieces // parts), pieces // parts, 0
        )
    rows_grad = attention_back(
        saved["head_rows"], context["spans"], head_grad, saved["wide"], saved["logs"]
    )
    team_grad = exchange(rows_grad, "z")
    if parts > 1:
        team_grad = team_grad.reshape(TEAM_SIZE, parts, 3 * HEAD, group).astype(F32).sum(axis=1)
        team_grad = team_grad.astype(BF16)
    projected_grad = turn_heads(
        team_grad[:TEAM_HEADS].astype(F32).reshape(TEAM_HEADS, 3, 2, HEAD // 2, group),
        context["cosine"],
        context["sine"],
        -1.0,
    )
    projected_grad = projected_grad.astype(BF16).reshape(TEAM_HEADS * 3 * HEAD, group)
    grad_qkv = contract(saved["normed_team"], projected_grad, 0, 1).astype(BF16)
    team_part = contract(projected_grad, qkv_weight, 0, 1).astype(BF16)
    team_part = in_order(team_part.reshape(TEAM_SIZE, stretch, D), member)
    norm_grad_one, grad_gain_one = norm_back(
        saved["stream"], gain_one, saved["factor_one"], team_sum(team_part)
    )
    small = jnp.concatenate([grad_gain_one[:, None], grad_gain_two[:, None], grad_router], axis=1)

    expert_terms = expert_grads(
        layer,
        both_halves(saved["arrived"]),
        both_halves(arrived_grad),
        expert_joint,
        expert_down,
        before,
    )
    dense = dense_sums(grad_qkv, small, grad_out, grad_joint, grad_down)
    return (middle_grad + norm_grad_one, dense, expert_terms)


def dense_sums(grad_qkv, small, grad_out, grad_joint, grad_down):
    total = lax.axis_size(ALL)
    rest = total // TEAM_SIZE
    width = D // total
    qkv_width = grad_qkv.shape[1]
    packed = jnp.concatenate([grad_qkv, small.astype(BF16)], axis=1)
    packed = exchange(packed.reshape(total, width, -1), ALL).astype(F32)
    small_sum = packed[:, :, qkv_width:].sum(axis=0)
    qkv_sum = packed[:, :, :qkv_width].reshape(rest, TEAM_SIZE, width, qkv_width).sum(axis=0)
    qkv_sum = (
        qkv_sum.reshape(TEAM_SIZE, width, TEAM_HEADS, 3, HEAD)
        .transpose(1, 3, 0, 2, 4)
        .reshape(width, 3 * D)
    )
    out_sum = exchange(grad_out.reshape(total, width, D), ALL).astype(F32).sum(axis=0)
    joint_sum = exchange(grad_joint.reshape(total, width, -1), ALL).astype(F32)
    joint_sum = joint_sum.reshape(rest, TEAM_SIZE, width, -1).sum(axis=0)
    joint_sum = (
        joint_sum.reshape(TEAM_SIZE, width, 2, rest, FF // total)
        .transpose(1, 2, 3, 0, 4)
        .reshape(width, 2 * FF)
    )
    down_sum = exchange(grad_down.reshape(rest, FF // total, D), REST).astype(F32).sum(axis=0)
    return (
        small_sum[:, 0],
        qkv_sum,
        out_sum,
        small_sum[:, 1],
        small_sum[:, 2:],
        joint_sum,
        down_sum,
    )


def spread(rows):
    return lax.all_gather(rows, REST, axis=0, tiled=True)


def dense_weights(gain_attn, w_qkv, w_out, gain_ffn, w_router, shared_gate_up, shared_down):
    total = lax.axis_size(ALL)
    rest = total // TEAM_SIZE
    width = w_qkv.shape[1]
    small = jnp.concatenate(
        [gain_attn.T, gain_ffn.T, w_router.transpose(1, 0, 2).reshape(width, -1)], axis=1
    )
    small = jnp.broadcast_to(small[None], (TEAM_SIZE,) + small.shape)

    def qkv_columns(layer):
        blocks = w_qkv[layer].reshape(width, 3, TEAM_SIZE, TEAM_HEADS, HEAD)
        return blocks.transpose(2, 0, 3, 1, 4).reshape(TEAM_SIZE, width, -1)

    def joint_columns(layer):
        blocks = shared_gate_up[layer].reshape(width, 2, rest, TEAM_SIZE, FF // total)
        return blocks.transpose(3, 0, 1, 2, 4).reshape(TEAM_SIZE, width, -1)

    qkv_width = 3 * D // TEAM_SIZE
    first = exchange(jnp.concatenate([qkv_columns(0), small], axis=2), TEAM)
    first = spread(first.reshape(TEAM_SIZE * width, -1))
    qkv = [first[:, :qkv_width]]
    smalls = first[:, qkv_width:].astype(F32)
    out, joint, down = [], [], []
    for layer in range(LAYERS):
        if layer > 0:
            columns = exchange(qkv_columns(layer), TEAM)
            qkv.append(spread(columns.reshape(TEAM_SIZE * width, -1)))
        out.append(lax.all_gather(w_out[layer], ALL, axis=0, tiled=True))
        columns = exchange(joint_columns(layer), TEAM)
        joint.append(spread(columns.reshape(TEAM_SIZE * width, -1)))
        down.append(spread(shared_down[layer]))
    weights = []
    for layer in range(LAYERS):
        router = smalls[:, 2 * LAYERS + layer * EXPERTS : 2 * LAYERS + (layer + 1) * EXPERTS]
        weights.append(
            (
                smalls[:, layer],
                qkv[layer],
                out[layer],
                smalls[:, LAYERS + layer],
                router.astype(BF16),
                joint[layer],
                down[layer],
            )
        )
    return weights


def query_spans(block_row, group, part, parts):
    length = block_row.shape[0]
    limit = jnp.sum((block_row[None, :] <= block_row[:, None]).astype(jnp.int32), axis=1)
    tiles = length // QUERY_TILE // parts
    base = part * tiles
    ends = lax.dynamic_slice_in_dim(limit.reshape(-1, QUERY_TILE), base, tiles, 0)
    full = ends[:, 0] // group
    some = (ends[:, -1] + group - 1) // group
    base = jnp.full((1,), base, jnp.int32)
    return (full, some, base, limit[None, :], tiles)


def local(
    x_in,
    block_ids,
    expert_ids,
    cotangent,
    gain_attn,
    w_qkv,
    w_out,
    gain_ffn,
    w_router,
    shared_gate_up,
    shared_down,
    expert_gate_up,
    expert_down,
):
    stretch = x_in.shape[1]
    group = TEAM_SIZE * stretch
    deep = lax.axis_size("z")
    parts = max(1, deep // TEAM_SIZE)
    at = lax.axis_index("z")
    member = lax.axis_index("core") * lax.axis_size("ulysses") + lax.axis_index("ulysses")
    half_size = HEAD // 2
    spacing = 10000.0 ** (-jnp.arange(half_size).astype(F32) * 2.0 / HEAD)
    positions = (at * group + jnp.arange(group, dtype=jnp.int32)).astype(F32)
    angles = spacing[:, None] * positions[None, :]
    tables, hits = route_tables(expert_ids[0])
    part = at % parts
    context = dict(
        member=member,
        cosine=jnp.cos(angles),
        sine=jnp.sin(angles),
        tables=tables,
        hits=hits,
        parts=parts,
        part=part,
        pieces=deep * TEAM_SIZE,
        split_count=deep * TEAM_SIZE // EXPERTS,
        spans=query_spans(block_ids[0], group, part, parts),
    )
    experts = (expert_gate_up, expert_down)
    first_rows = in_order(team_gather(x_in[0]), member).reshape(group, D)
    weights = dense_weights(
        gain_attn, w_qkv, w_out, gain_ffn, w_router, shared_gate_up, shared_down
    )
    stream = x_in[0].astype(F32)
    records = []
    for layer in range(LAYERS):
        stream, saved = forward_layer(
            layer, stream, first_rows if layer == 0 else None, weights[layer], experts, context
        )
        records.append(saved)
    upstream = cotangent[0].astype(F32)
    dense = [None] * LAYERS
    expert_terms = None
    for layer in reversed(range(LAYERS)):
        upstream, dense[layer], expert_terms = backward_layer(
            layer, upstream, weights[layer], experts, context, records[layer], expert_terms
        )
    stacked = [jnp.stack([dense[layer][i] for layer in range(LAYERS)]) for i in range(7)]
    return (
        stream.astype(BF16)[None],
        upstream.astype(BF16)[None],
        *stacked,
        *expert_terms,
    )


def solution(mesh):
    dp, blk, ulysses = mesh.devices.shape
    grid = Mesh(mesh.devices.reshape(dp, blk // 2, 2, ulysses), ALL)
    rows = P("dp", SEQ, None)
    in_specs = (
        rows,
        P("dp", None),
        rows,
        rows,
        P(None, ALL),
        P(None, ALL, None),
        P(None, ALL, None),
        P(None, ALL),
        P(None, ALL, None),
        P(None, ALL, None),
        P(None, ALL, None),
        P(None, SEQ, None, None),
        P(None, SEQ, None, None),
    )
    out_specs = (
        rows,
        rows,
        P(None, ALL),
        P(None, ALL, None),
        P(None, ALL, None),
        P(None, ALL),
        P(None, ALL, None),
        P(None, ALL, None),
        P(None, ALL, None),
        P(None, SEQ, None, None),
        P(None, SEQ, None, None),
    )
    return jax.shard_map(local, mesh=grid, in_specs=in_specs, out_specs=out_specs, check_vma=False)
```

```python
import functools

import jax
import jax.numpy as jnp
from jax import lax
from jax.experimental import pallas as pl
from jax.experimental.pallas import tpu as pltpu
from jax.sharding import Mesh
from jax.sharding import PartitionSpec as P

D = 768
HEADS = 12
HEAD = 64
FF = 2048
EXPERTS = 16
LAYERS = 2
MOST = 21
SLOTS = -(-MOST // 8) * 8
TEAM_SIZE = 4
TEAM_HEADS = HEADS // TEAM_SIZE

ALL = ("dp", "z", "core", "ulysses")
SEQ = ("z", "core", "ulysses")
TEAM = ("core", "ulysses")
REST = ("dp", "z")

NORM_EPS = 1e-06
NEG_BIG = -1e30
PRECISE = lax.Precision.HIGHEST
F32 = jnp.float32
BF16 = jnp.bfloat16
QUERY_TILE = 256
VMEM_LIMIT = 48 * 1024 * 1024


def cost(flops, moved, steps=0):
    return pl.CostEstimate(flops=flops, bytes_accessed=moved, transcendentals=steps)


def contract(left, right, left_dim, right_dim):
    return lax.dot_general(
        left, right, (((left_dim,), (right_dim,)), ((), ())), preferred_element_type=F32
    )


def exchange(rows, axes):
    return lax.all_to_all(rows, axes, split_axis=0, concat_axis=0, tiled=True)


SWAP = [(0, 1), (1, 0)]


def from_member(rows, turn):
    if turn == 1:
        return lax.ppermute(rows, "ulysses", SWAP)
    if turn == 2:
        return lax.ppermute(rows, "core", SWAP)
    return lax.ppermute(rows, TEAM, [(i, 3 - i) for i in range(4)])


def team_gather(rows):
    return jnp.stack([rows] + [from_member(rows, turn) for turn in (1, 2, 3)])


def in_order(stacked, member):
    turns = [jnp.equal(member, i) for i in range(4)]
    pieces = []
    for k in range(4):
        piece = stacked[k ^ 3]
        for i in range(3):
            piece = jnp.where(turns[i], stacked[k ^ i], piece)
        pieces.append(piece)
    return jnp.stack(pieces)


def team_sum(parts):
    total = parts[0].astype(F32)
    for turn in (1, 2, 3):
        total = total + from_member(parts[turn].astype(BF16), turn).astype(F32)
    return total


def rms_factor(stream):
    return lax.rsqrt(jnp.mean(stream * stream, axis=-1, keepdims=True) + NORM_EPS)


def norm_back(stream, gain, factor, upstream):
    weighted = upstream * gain
    inner_mean = jnp.mean(weighted * stream, axis=-1, keepdims=True)
    grad_stream = factor * weighted - stream * factor * factor * factor * inner_mean
    grad_gain = jnp.sum(upstream * stream * factor, axis=0)
    return (grad_stream, grad_gain)


def attention_kernel(full_ref, some_ref, base_ref, rows_ref, limit_ref, out_ref, wide_ref, log_ref, keys):
    span = rows_ref.shape[2]
    step = pl.program_id(0)
    per_block = span // QUERY_TILE

    @pl.when(step == 0)
    def _():
        for s in range(rows_ref.shape[0]):
            keys[s] = rows_ref[s, HEAD : 2 * HEAD, :].T

    tile = base_ref[0] + step
    lanes = pl.ds(pl.multiple_of((tile % per_block) * QUERY_TILE, QUERY_TILE), QUERY_TILE)
    queries = rows_ref[tile // per_block, 0:HEAD, lanes] * BF16(HEAD**-0.5)
    limit = limit_ref[...]
    key_index = lax.broadcasted_iota(jnp.int32, (span, QUERY_TILE), 0)

    def sweep(s, state, masked):
        highest, total, running = state
        scores = jnp.dot(keys[s], queries, preferred_element_type=F32)
        if masked:
            scores = jnp.where(key_index < limit - s * span, scores, NEG_BIG)
        raised = jnp.maximum(highest, jnp.max(scores, axis=0, keepdims=True))
        terms = jnp.exp(scores - raised)
        shrink = jnp.exp(highest - raised)
        total = total * shrink + jnp.sum(terms, axis=0, keepdims=True)
        running = running * shrink + jnp.dot(
            rows_ref[s, 2 * HEAD :, :], terms.astype(BF16), preferred_element_type=F32
        )
        return (raised, total, running)

    state = (
        jnp.full((1, QUERY_TILE), NEG_BIG, F32),
        jnp.zeros((1, QUERY_TILE), F32),
        jnp.zeros((HEAD, QUERY_TILE), F32),
    )
    state = lax.fori_loop(0, full_ref[step], lambda s, c: sweep(s, c, False), state)
    state = lax.fori_loop(full_ref[step], some_ref[step], lambda s, c: sweep(s, c, True), state)
    highest, total, running = state
    result = running / total
    log_ref[...] = highest + jnp.log(total)
    wide_ref[...] = result
    stretch = out_ref.shape[2]
    for i in range(QUERY_TILE // stretch):
        out_ref[i] = result[:, i * stretch : (i + 1) * stretch].astype(BF16)


def attention_back_kernel(
    full_ref, some_ref, base_ref, rows_ref, limit_ref, grad_ref, wide_ref, log_ref, *refs
):
    out_ref, keys, values, key_sum, value_sum = refs[-5:]
    span = rows_ref.shape[2]
    blocks = rows_ref.shape[0]
    step = pl.program_id(0)
    per_block = span // QUERY_TILE

    @pl.when(step == 0)
    def _():
        for s in range(blocks):
            keys[s] = rows_ref[s, HEAD : 2 * HEAD, :].T
            values[s] = rows_ref[s, 2 * HEAD :, :].T
        key_sum[...] = jnp.zeros_like(key_sum)
        value_sum[...] = jnp.zeros_like(value_sum)
        out_ref[...] = jnp.zeros_like(out_ref)

    tile = base_ref[0] + step
    lanes = pl.ds(pl.multiple_of((tile % per_block) * QUERY_TILE, QUERY_TILE), QUERY_TILE)
    queries = rows_ref[tile // per_block, 0:HEAD, lanes] * BF16(HEAD**-0.5)
    limit = limit_ref[...]
    key_index = lax.broadcasted_iota(jnp.int32, (span, QUERY_TILE), 0)
    grads = jnp.concatenate([grad_ref[i] for i in range(grad_ref.shape[0])], axis=1)
    delta = jnp.sum(grads.astype(F32) * wide_ref[...], axis=0, keepdims=True)
    logs = log_ref[...]

    def sweep(s, query_grad, masked):
        scores = jnp.dot(keys[s], queries, preferred_element_type=F32)
        probs = jnp.exp(scores - logs)
        if masked:
            probs = jnp.where(key_index < limit - s * span, probs, 0.0)
        prob_grad = jnp.dot(values[s], grads, preferred_element_type=F32)
        score_grad = (probs * (prob_grad - delta)).astype(BF16)
        value_sum[s] += contract(grads, probs.astype(BF16), 1, 1)
        key_sum[s] += contract(queries, score_grad, 1, 1)
        return query_grad + jnp.dot(
            rows_ref[s, HEAD : 2 * HEAD, :], score_grad, preferred_element_type=F32
        )

    query_grad = jnp.zeros((HEAD, QUERY_TILE), F32)
    query_grad = lax.fori_loop(0, full_ref[step], lambda s, c: sweep(s, c, False), query_grad)
    query_grad = lax.fori_loop(
        full_ref[step], some_ref[step], lambda s, c: sweep(s, c, True), query_grad
    )
    out_ref[tile // per_block, 0:HEAD, lanes] = (query_grad * HEAD**-0.5).astype(BF16)

    @pl.when(step == pl.num_programs(0) - 1)
    def _():
        out_ref[:, HEAD : 2 * HEAD, :] = key_sum[...].astype(BF16)
        out_ref[:, 2 * HEAD :, :] = value_sum[...].astype(BF16)


def fixed_attention_kernel(rows_ref, limit_ref, out_ref, wide_ref, log_ref, keys, values):
    blocks, _, span = rows_ref.shape
    length = blocks * span
    stretch = out_ref.shape[2]
    for s in range(blocks):
        keys[s * span : (s + 1) * span, :] = rows_ref[s, HEAD : 2 * HEAD, :].T
        values[:, s * span : (s + 1) * span] = rows_ref[s, 2 * HEAD :, :]
    key_index = lax.broadcasted_iota(jnp.int32, (2 * QUERY_TILE, QUERY_TILE), 0)
    for tile in range(length // QUERY_TILE):
        start = tile * QUERY_TILE
        end = min(start + 2 * QUERY_TILE, length)
        lanes = slice(start % span, start % span + QUERY_TILE)
        queries = rows_ref[start // span, 0:HEAD, lanes] * BF16(HEAD**-0.5)
        scores = jnp.dot(keys[start:end, :], queries, preferred_element_type=F32)
        limit = limit_ref[:, start : start + QUERY_TILE] - start
        scores = jnp.where(key_index[: end - start] < limit, scores, NEG_BIG)
        highest = jnp.max(scores, axis=0, keepdims=True)
        if start > 0:
            before = jnp.dot(keys[:start, :], queries, preferred_element_type=F32)
            highest = jnp.maximum(highest, jnp.max(before, axis=0, keepdims=True))
        terms = jnp.exp(scores - highest)
        total = jnp.sum(terms, axis=0, keepdims=True)
        result = jnp.dot(values[:, start:end], terms.astype(BF16), preferred_element_type=F32)
        if start > 0:
            terms = jnp.exp(before - highest)
            total = total + jnp.sum(terms, axis=0, keepdims=True)
            result = result + jnp.dot(
                values[:, :start], terms.astype(BF16), preferred_element_type=F32
            )
        result = result / total
        log_ref[:, start : start + QUERY_TILE] = highest + jnp.log(total)
        wide_ref[:, start : start + QUERY_TILE] = result
        for i in range(QUERY_TILE // stretch):
            out_ref[start // stretch + i] = result[:, i * stretch : (i + 1) * stretch].astype(BF16)


def fixed_attention_back_kernel(rows_ref, limit_ref, grad_ref, wide_ref, log_ref, *refs):
    out_ref, keys, values, key_sum, value_sum = refs[-5:]
    blocks, _, span = rows_ref.shape
    length = blocks * span
    stretch = grad_ref.shape[2]
    for s in range(blocks):
        keys[s * span : (s + 1) * span, :] = rows_ref[s, HEAD : 2 * HEAD, :].T
        values[s * span : (s + 1) * span, :] = rows_ref[s, 2 * HEAD :, :].T
    key_sum[...] = jnp.zeros_like(key_sum)
    value_sum[...] = jnp.zeros_like(value_sum)
    key_index = lax.broadcasted_iota(jnp.int32, (2 * QUERY_TILE, QUERY_TILE), 0)
    for tile in range(length // QUERY_TILE):
        start = tile * QUERY_TILE
        end = min(start + 2 * QUERY_TILE, length)
        lanes = slice(start % span, start % span + QUERY_TILE)
        queries = rows_ref[start // span, 0:HEAD, lanes] * BF16(HEAD**-0.5)
        pieces = QUERY_TILE // stretch
        grads = jnp.concatenate([grad_ref[tile * pieces + i] for i in range(pieces)], axis=1)
        wide = wide_ref[:, start : start + QUERY_TILE]
        delta = jnp.sum(grads.astype(F32) * wide, axis=0, keepdims=True)
        logs = log_ref[:, start : start + QUERY_TILE]
        limit = limit_ref[:, start : start + QUERY_TILE] - start
        query_grad = jnp.zeros((HEAD, QUERY_TILE), F32)
        for low, high in ((0, start), (start, end)):
            if low == high:
                continue
            scores = jnp.dot(keys[low:high, :], queries, preferred_element_type=F32)
            probs = jnp.exp(scores - logs)
            if low == start:
                probs = jnp.where(key_index[: high - low] < limit, probs, 0.0)
            prob_grad = jnp.dot(values[low:high, :], grads, preferred_element_type=F32)
            score_grad = (probs * (prob_grad - delta)).astype(BF16)
            value_sum[:, low:high] += contract(grads, probs.astype(BF16), 1, 1)
            key_sum[:, low:high] += contract(queries, score_grad, 1, 1)
            query_grad = query_grad + contract(keys[low:high, :], score_grad, 0, 0)
        out_ref[start // span, 0:HEAD, lanes] = (query_grad * HEAD**-0.5).astype(BF16)
    for s in range(blocks):
        out_ref[s, HEAD : 2 * HEAD, :] = key_sum[:, s * span : (s + 1) * span].astype(BF16)
        out_ref[s, 2 * HEAD :, :] = value_sum[:, s * span : (s + 1) * span].astype(BF16)


IN_VMEM = pl.BlockSpec(memory_space=pltpu.VMEM)
ANYWHERE = pl.BlockSpec(memory_space=pl.ANY)


def fixed_attention(rows, limit, stretch):
    blocks, _, span = rows.shape
    length = blocks * span
    return pl.pallas_call(
        fixed_attention_kernel,
        in_specs=[IN_VMEM] * 2,
        out_specs=[IN_VMEM] * 3,
        out_shape=[
            jax.ShapeDtypeStruct((length // stretch, HEAD, stretch), BF16),
            jax.ShapeDtypeStruct((HEAD, length), F32),
            jax.ShapeDtypeStruct((1, length), F32),
        ],
        scratch_shapes=[pltpu.VMEM((length, HEAD), BF16), pltpu.VMEM((HEAD, length), BF16)],
        compiler_params=pltpu.CompilerParams(vmem_limit_bytes=VMEM_LIMIT),
        cost_estimate=cost(rows.size * length // 48, rows.size * 4, length * length),
        name="attend",
    )(rows, limit)


def fixed_attention_back(rows, limit, grads, wide, logs, later_than):
    blocks, _, span = rows.shape
    length = blocks * span
    return pl.pallas_call(
        fixed_attention_back_kernel,
        in_specs=[IN_VMEM] * 5 + [ANYWHERE] * len(later_than),
        out_specs=IN_VMEM,
        out_shape=jax.ShapeDtypeStruct(rows.shape, BF16),
        scratch_shapes=[
            pltpu.VMEM((length, HEAD), BF16),
            pltpu.VMEM((length, HEAD), BF16),
            pltpu.VMEM((HEAD, length), F32),
            pltpu.VMEM((HEAD, length), F32),
        ],
        compiler_params=pltpu.CompilerParams(vmem_limit_bytes=VMEM_LIMIT),
        cost_estimate=cost(rows.size * length // 16, rows.size * 4, length * length),
        name="attend_back",
    )(rows, limit, grads, wide, logs, *later_than)


def whole(shape):
    return pl.BlockSpec(shape, lambda step, *_: (0,) * len(shape))


def tile_at(step, full, some, base):
    return (0, base[0] + step)


def attention(rows, spans, stretch):
    full, some, base, limit, tiles, parts = spans
    if parts == 1:
        return fixed_attention(rows, limit, stretch)
    blocks, _, span = rows.shape
    length = tiles * QUERY_TILE
    return pl.pallas_call(
        attention_kernel,
        grid_spec=pltpu.PrefetchScalarGridSpec(
            num_scalar_prefetch=3,
            grid=(tiles,),
            in_specs=[whole(rows.shape), pl.BlockSpec((1, QUERY_TILE), tile_at)],
            out_specs=[
                pl.BlockSpec((QUERY_TILE // stretch, HEAD, stretch), lambda step, *_: (step, 0, 0)),
                pl.BlockSpec((HEAD, QUERY_TILE), lambda step, *_: (0, step)),
                pl.BlockSpec((1, QUERY_TILE), lambda step, *_: (0, step)),
            ],
            scratch_shapes=[pltpu.VMEM((blocks, span, HEAD), BF16)],
        ),
        out_shape=[
            jax.ShapeDtypeStruct((length // stretch, HEAD, stretch), BF16),
            jax.ShapeDtypeStruct((HEAD, length), F32),
            jax.ShapeDtypeStruct((1, length), F32),
        ],
        compiler_params=pltpu.CompilerParams(vmem_limit_bytes=VMEM_LIMIT),
        cost_estimate=cost(rows.size * length // 48, rows.size * 4, length * length),
        name="attend",
    )(full, some, base, rows, limit)


def attention_back(rows, spans, grads, wide, logs, later_than):
    full, some, base, limit, tiles, parts = spans
    if parts == 1:
        return fixed_attention_back(rows, limit, grads, wide, logs, later_than)
    blocks, _, span = rows.shape
    stretch = grads.shape[2]
    return pl.pallas_call(
        attention_back_kernel,
        grid_spec=pltpu.PrefetchScalarGridSpec(
            num_scalar_prefetch=3,
            grid=(tiles,),
            in_specs=[
                whole(rows.shape),
                pl.BlockSpec((1, QUERY_TILE), tile_at),
                pl.BlockSpec((QUERY_TILE // stretch, HEAD, stretch), lambda step, *_: (step, 0, 0)),
                pl.BlockSpec((HEAD, QUERY_TILE), lambda step, *_: (0, step)),
                pl.BlockSpec((1, QUERY_TILE), lambda step, *_: (0, step)),
                *[pl.BlockSpec(memory_space=pl.ANY)] * len(later_than),
            ],
            out_specs=whole(rows.shape),
            scratch_shapes=[
                pltpu.VMEM((blocks, span, HEAD), BF16),
                pltpu.VMEM((blocks, span, HEAD), BF16),
                pltpu.VMEM((blocks, HEAD, span), F32),
                pltpu.VMEM((blocks, HEAD, span), F32),
            ],
        ),
        out_shape=jax.ShapeDtypeStruct(rows.shape, BF16),
        compiler_params=pltpu.CompilerParams(vmem_limit_bytes=VMEM_LIMIT),
        cost_estimate=cost(rows.size * tiles * QUERY_TILE // 16, rows.size * 4, rows.size),
        name="attend_back",
    )(full, some, base, rows, limit, grads, wide, logs, *later_than)


def turn_heads(parts, cosine, sine, direction):
    first, second = parts[:, :2, 0], parts[:, :2, 1]
    turned = jnp.stack(
        [
            first * cosine - direction * (second * sine),
            second * cosine + direction * (first * sine),
        ],
        axis=2,
    )
    return jnp.concatenate([turned, parts[:, 2:]], axis=1)


def logistic(values):
    return 0.5 * jnp.tanh(0.5 * values) + 0.5


def swiglu_back(gate_pre, up_pre, hidden_grad):
    sigmoid_gate = logistic(gate_pre)
    silu_gate = gate_pre * sigmoid_gate
    gate_grad = hidden_grad * up_pre * (sigmoid_gate + silu_gate * (1.0 - sigmoid_gate))
    up_grad = hidden_grad * silu_gate
    return (gate_grad.astype(BF16), up_grad.astype(BF16))


def swiglu(gate_pre, up_pre):
    return (gate_pre * logistic(gate_pre) * up_pre).astype(BF16)


def expert_kernel(forward, backward, *refs):
    inputs = 1 + backward
    rows_ref, grads_ref = refs[0], refs[inputs - 1]
    gate_ref, up_ref, down_ref, out_ref, total = refs[inputs:]
    step = pl.program_id(0)
    rows = rows_ref[...]
    gate, up, down = gate_ref[0, 0], up_ref[0, 0], down_ref[0, 0]
    gate_pre = jnp.dot(rows, gate, preferred_element_type=F32)
    up_pre = jnp.dot(rows, up, preferred_element_type=F32)
    terms = []
    if forward:
        terms.append(jnp.dot(swiglu(gate_pre, up_pre), down, preferred_element_type=F32))
    if backward:
        hidden_grad = contract(grads_ref[...], down, 1, 1).astype(BF16).astype(F32)
        gate_grad, up_grad = swiglu_back(gate_pre, up_pre, hidden_grad)
        terms.append(contract(gate_grad, gate, 1, 1) + contract(up_grad, up, 1, 1))

    @pl.when(step == 0)
    def _():
        for i, term in enumerate(terms):
            total[:, i * D : (i + 1) * D] = term

    @pl.when(step > 0)
    def _():
        for i, term in enumerate(terms):
            total[:, i * D : (i + 1) * D] += term

    @pl.when(step == pl.num_programs(0) - 1)
    def _():
        out_ref[...] = total[...].astype(BF16)


def run_expert(layer, joint, down, rows, grads, forward):
    half = joint.shape[3] // 2
    chunk = min(512, half)
    chunks = half // chunk
    given = [rows] + ([grads] if grads is not None else [])
    count = rows[0].shape[0]
    width = D * (int(forward) + int(grads is not None))
    return pl.pallas_call(
        functools.partial(expert_kernel, forward, grads is not None),
        grid=(chunks,),
        in_specs=[
            *[pl.BlockSpec((count, D), lambda i, at=at: (0, at)) for _, at in given],
            pl.BlockSpec((1, 1, D, chunk), lambda i: (layer, 0, 0, i)),
            pl.BlockSpec((1, 1, D, chunk), lambda i: (layer, 0, 0, chunks + i)),
            pl.BlockSpec((1, 1, chunk, D), lambda i: (layer, 0, i, 0)),
        ],
        out_specs=pl.BlockSpec((count, width), lambda i: (0, 0)),
        out_shape=jax.ShapeDtypeStruct((count, width), BF16),
        scratch_shapes=[pltpu.VMEM((count, width), F32)],
        compiler_params=pltpu.CompilerParams(vmem_limit_bytes=VMEM_LIMIT),
        cost_estimate=cost(
            2 * count * D * half * (2 + int(forward) + 3 * int(grads is not None)),
            6 * D * half + 4 * count * width,
            count * half,
        ),
        name="expert_forward" if grads is None else "expert_both" if forward else "expert_back",
    )(*[array for array, _ in given], joint, joint, down)


def expert_grad_kernel(slot_ref, own_rows, own_grads, other_rows, other_grads, gate_ref, up_ref, down_ref, *refs):
    joint_out, down_out, rows_all, grads_all, turned, hold = refs[-6:]
    count = own_rows.shape[0]

    @pl.when((pl.program_id(0) == 0) & (pl.program_id(1) == 0))
    def _():
        own = pl.ds(pl.multiple_of(slot_ref[0] * count, count), count)
        other = pl.ds(pl.multiple_of((1 - slot_ref[0]) * count, count), count)
        rows_all[own, :] = own_rows[...]
        rows_all[other, :] = other_rows[...]
        grads_all[own, :] = own_grads[...]
        grads_all[other, :] = other_grads[...]
        turned[...] = rows_all[...].T

    @pl.when(pl.program_id(1) == 0)
    def _():
        rows = rows_all[...]
        grads = grads_all[...]
        gate_pre = jnp.dot(rows, gate_ref[0, 0], preferred_element_type=F32)
        up_pre = jnp.dot(rows, up_ref[0, 0], preferred_element_type=F32)
        hidden_grad = contract(grads, down_ref[0, 0], 1, 1).astype(BF16).astype(F32)
        gate_grad, up_grad = swiglu_back(gate_pre, up_pre, hidden_grad)
        hold[...] = up_grad
        down_out[0, 0] = contract(swiglu(gate_pre, up_pre), grads, 0, 0)
        joint_out[0, 0] = jnp.dot(turned[...], gate_grad, preferred_element_type=F32)

    @pl.when(pl.program_id(1) == 1)
    def _():
        joint_out[0, 0] = jnp.dot(turned[...], hold[...], preferred_element_type=F32)


def expert_grads(layer, own, other, joint, down, before, later_than):
    half = joint.shape[3] // 2
    given = [*own, *other]
    count = given[0][0].shape[0]
    chunk = min(512 if count <= 512 else 128, half)
    chunks = half // chunk
    slot = lax.axis_index("dp").astype(jnp.int32).reshape(1)
    in_specs = [
        pl.BlockSpec(memory_space=pltpu.SMEM),
        *[pl.BlockSpec((count, D), lambda i, h, at=at: (0, at)) for _, at in given],
        pl.BlockSpec((1, 1, D, chunk), lambda i, h: (layer, 0, 0, i)),
        pl.BlockSpec((1, 1, D, chunk), lambda i, h: (layer, 0, 0, chunks + i)),
        pl.BlockSpec((1, 1, chunk, D), lambda i, h: (layer, 0, i, 0)),
    ]
    operands = [slot] + [array for array, _ in given] + [joint, joint, down]
    aliases = {}
    if before is not None:
        aliases = {len(operands): 0, len(operands) + 1: 1}
        operands += list(before)
    operands.append(later_than)
    in_specs += [pl.BlockSpec(memory_space=pl.ANY)] * (len(operands) - len(in_specs))
    return pl.pallas_call(
        expert_grad_kernel,
        grid=(chunks, 2),
        in_specs=in_specs,
        out_specs=[
            pl.BlockSpec((1, 1, D, chunk), lambda i, h: (layer, 0, 0, h * chunks + i)),
            pl.BlockSpec((1, 1, chunk, D), lambda i, h: (layer, 0, i, 0)),
        ],
        out_shape=[
            jax.ShapeDtypeStruct(joint.shape, F32),
            jax.ShapeDtypeStruct(down.shape, F32),
        ],
        scratch_shapes=[
            pltpu.VMEM((2 * count, D), BF16),
            pltpu.VMEM((2 * count, D), BF16),
            pltpu.VMEM((D, 2 * count), BF16),
            pltpu.VMEM((2 * count, chunk), BF16),
        ],
        input_output_aliases=aliases,
        compiler_params=pltpu.CompilerParams(vmem_limit_bytes=VMEM_LIMIT),
        cost_estimate=cost((6 if layer == 0 else 24) * count * D * half, 6 * D * half),
        name="expert_grads",
    )(*operands)


def nothing(*refs):
    pass


def later(rows, *others):
    return pl.pallas_call(
        nothing,
        in_specs=[pl.BlockSpec(memory_space=pl.ANY)] * (1 + len(others)),
        out_specs=pl.BlockSpec(memory_space=pl.ANY),
        out_shape=jax.ShapeDtypeStruct(rows.shape, rows.dtype),
        input_output_aliases={0: 0},
        name="later",
    )(rows, *others)


def route_tables(route_ids):
    stretch_rows = route_ids.shape[0]
    experts_row = jnp.arange(EXPERTS, dtype=jnp.int32)
    route_hits = (route_ids[:, :, None] == experts_row[None, None, :]).astype(jnp.int32)
    running = (
        jnp.cumsum(route_hits.reshape(2 * stretch_rows, EXPERTS), axis=0).reshape(
            stretch_rows, 2, EXPERTS
        )
        - 1
    )
    slot_index = jnp.sum(route_hits * running, axis=2)
    route_rows = route_ids * SLOTS + slot_index
    all_rows = jnp.arange(EXPERTS * SLOTS, dtype=jnp.int32)
    tables = [
        (route_rows[:, c, None] == all_rows[None, :]).astype(BF16) for c in range(2)
    ]
    return (tables, route_hits.astype(F32))


def send_rows(outgoing, split_count):
    width = outgoing.shape[1]
    outgoing = outgoing.reshape(EXPERTS, SLOTS, width)
    if split_count > 1:
        outgoing = jnp.repeat(outgoing, split_count, axis=0)
    return exchange(outgoing, SEQ).reshape(-1, width)


def return_rows(rows, split_count):
    width = rows.shape[1]
    returned = exchange(rows.reshape(-1, SLOTS, width), SEQ)
    if split_count > 1:
        returned = (
            returned.reshape(EXPERTS, split_count, SLOTS, width).astype(F32).sum(axis=1)
        ).astype(BF16)
    return returned.reshape(EXPERTS * SLOTS, width)


def attention_start(stream, first_rows, gain_one, qkv_weight, context):
    stretch = stream.shape[0]
    group = TEAM_SIZE * stretch
    member = context["member"]
    factor_one = rms_factor(stream)
    if first_rows is not None:
        wide_rows = first_rows.astype(F32)
        normed_team = (wide_rows * rms_factor(wide_rows) * gain_one).astype(BF16)
    else:
        normed = (stream * factor_one * gain_one).astype(BF16)
        normed_team = in_order(team_gather(normed), member).reshape(group, D)
    projected = contract(qkv_weight, normed_team, 0, 1)
    turned = turn_heads(
        projected.reshape(TEAM_HEADS, 3, 2, HEAD // 2, group),
        context["cosine"],
        context["sine"],
        1.0,
    )
    heads = turned.astype(BF16).reshape(TEAM_HEADS, 3 * HEAD, group)
    heads = jnp.concatenate([heads, jnp.zeros((1,) + heads.shape[1:], BF16)], axis=0)
    parts = context["parts"]
    if parts > 1:
        heads = jnp.repeat(heads, parts, axis=0)
    head_rows = exchange(heads, "z")
    saved = dict(
        stream=stream, factor_one=factor_one, normed_team=normed_team, head_rows=head_rows
    )
    return (head_rows, saved)


def attend(head_rows, saved, context, stretch):
    attended, wide, logs = attention(head_rows, context["spans"], stretch)
    saved.update(attended=attended, wide=wide, logs=logs)


def attention_end(stream, saved, out_weight, context):
    stretch = stream.shape[0]
    parts = context["parts"]
    attended = saved["attended"]
    pieces = context["pieces"]
    if parts > 1:
        attended = lax.dynamic_update_slice_in_dim(
            jnp.zeros((pieces, HEAD, stretch), BF16),
            attended,
            context["part"] * (pieces // parts),
            0,
        )
    back = exchange(attended, SEQ)
    if parts > 1:
        back = (
            back.reshape(TEAM_SIZE, parts, TEAM_SIZE, HEAD, stretch).astype(F32).sum(axis=1)
        ).astype(BF16)
    back = back.reshape(TEAM_SIZE, TEAM_SIZE, HEAD, stretch)[:TEAM_HEADS]
    mixed = back.transpose(1, 0, 2, 3).reshape(D, stretch)
    middle = stream + contract(mixed, out_weight, 0, 0)
    saved.update(mixed=mixed)
    return middle


def feed_start(middle, weights, context):
    gain_two, router_weight = weights[3:5]
    factor_two = rms_factor(middle)
    normed_ffn = (middle * factor_two * gain_two).astype(BF16)
    logits = jnp.dot(normed_ffn, router_weight, preferred_element_type=F32)
    picked = jnp.sum(logits[:, None, :] * context["hits"], axis=2)
    gate_values = jax.nn.softmax(picked, axis=1)
    return dict(
        middle=middle, factor_two=factor_two, normed_ffn=normed_ffn, gate_values=gate_values
    )


def outgoing_rows(feed, context):
    table_one, table_two = context["tables"]
    return contract(table_one + table_two, feed["normed_ffn"], 0, 0).astype(BF16)


def outgoing_grads(feed, upstream, context):
    table_one, table_two = context["tables"]
    gates = feed["gate_values"]
    return (
        contract(table_one, (gates[:, 0:1] * upstream).astype(BF16), 0, 0)
        + contract(table_two, (gates[:, 1:2] * upstream).astype(BF16), 0, 0)
    ).astype(BF16)


def shared_forward(feed, weights, token):
    joint_weight, down_weight = weights[5:7]
    stretch = feed["normed_ffn"].shape[0]
    ffn_team = team_gather(feed["normed_ffn"]).reshape(TEAM_SIZE * stretch, D)
    ffn_team = later(ffn_team, token)
    shared_joint = jnp.dot(ffn_team, joint_weight, preferred_element_type=F32)
    half = shared_joint.shape[1] // 2
    shared_hidden = swiglu(shared_joint[:, :half], shared_joint[:, half:])
    shared_out = team_sum(
        jnp.dot(shared_hidden, down_weight, preferred_element_type=F32).reshape(
            TEAM_SIZE, stretch, D
        )
    )
    feed.update(ffn_team=ffn_team, shared_joint=shared_joint, shared_hidden=shared_hidden)
    return shared_out


def shared_backward(feed, grad_team, weights):
    joint_weight, down_weight = weights[5:7]
    shared_joint = feed["shared_joint"]
    half = shared_joint.shape[1] // 2
    hidden_grad = contract(grad_team, down_weight, 1, 1).astype(BF16).astype(F32)
    joint_grad = jnp.concatenate(
        swiglu_back(shared_joint[:, :half], shared_joint[:, half:], hidden_grad), axis=1
    )
    normed_grad = team_sum(
        contract(joint_grad, joint_weight, 1, 1).reshape(TEAM_SIZE, -1, D)
    )
    grad_down = contract(feed["shared_hidden"], grad_team, 0, 0).astype(BF16)
    grad_joint = contract(feed["ffn_team"], joint_grad, 0, 0).astype(BF16)
    return (normed_grad, grad_joint, grad_down)


def feed_output(feed, shared_out, returned, context):
    table_one, table_two = context["tables"]
    choices = [
        jnp.dot(table, returned, preferred_element_type=F32) for table in (table_one, table_two)
    ]
    gates = feed["gate_values"]
    feed["choices"] = choices
    return (
        feed["middle"] + shared_out + gates[:, 0:1] * choices[0] + gates[:, 1:2] * choices[1]
    )


def feed_backward(feed, upstream, shared_grad, returned_grad, weights, context):
    gain_two, router_weight = weights[3:5]
    table_one, table_two = context["tables"]
    gates = feed["gate_values"]
    choice_one, choice_two = feed["choices"]
    lead_grad = (
        gates[:, 0:1]
        * gates[:, 1:2]
        * jnp.sum((choice_one - choice_two) * upstream, axis=1, keepdims=True)
    )
    hits = context["hits"]
    logit_grad = lead_grad * (hits[:, 0, :] - hits[:, 1, :])
    grad_router = jnp.dot(feed["normed_ffn"].astype(F32).T, logit_grad, precision=PRECISE)
    normed_grad = (
        shared_grad
        + jnp.dot(logit_grad, router_weight.astype(F32).T, precision=PRECISE)
        + jnp.dot(table_one + table_two, returned_grad, preferred_element_type=F32)
    )
    norm_grad, grad_gain = norm_back(feed["middle"], gain_two, feed["factor_two"], normed_grad)
    return (upstream + norm_grad, grad_gain, grad_router)


def attention_backward(middle_grad, weights, context, saved, later_than, before_end, experts):
    gain_one, qkv_weight, out_weight = weights[:3]
    stretch = middle_grad.shape[0]
    group = TEAM_SIZE * stretch
    member = context["member"]
    attn_grad = middle_grad.astype(BF16)
    mixed_grad = contract(out_weight, attn_grad, 1, 1).astype(BF16)
    mixed_grad = mixed_grad.reshape(TEAM_SIZE, TEAM_HEADS, HEAD, stretch).transpose(1, 0, 2, 3)
    mixed_grad = jnp.concatenate(
        [mixed_grad, jnp.zeros((1,) + mixed_grad.shape[1:], BF16)], axis=0
    )
    parts = context["parts"]
    if parts > 1:
        mixed_grad = jnp.repeat(mixed_grad, parts, axis=0)
    pieces = context["pieces"]
    head_grad = exchange(mixed_grad.reshape(-1, HEAD, stretch), SEQ)
    if parts > 1:
        head_grad = lax.dynamic_slice_in_dim(
            head_grad, context["part"] * (pieces // parts), pieces // parts, 0
        )
    rows_grad = attention_back(
        saved["head_rows"], context["spans"], head_grad, saved["wide"], saved["logs"], later_than
    )
    terms = expert_grads(*experts, rows_grad)
    tokens = [before_end] if experts[0] == 0 else [before_end, terms[1]]
    team_grad = later(exchange(rows_grad, "z"), *tokens)
    if parts > 1:
        team_grad = team_grad.reshape(TEAM_SIZE, parts, 3 * HEAD, group).astype(F32).sum(axis=1)
        team_grad = team_grad.astype(BF16)
    projected_grad = turn_heads(
        team_grad[:TEAM_HEADS].astype(F32).reshape(TEAM_HEADS, 3, 2, HEAD // 2, group),
        context["cosine"],
        context["sine"],
        -1.0,
    )
    projected_grad = projected_grad.astype(BF16).reshape(TEAM_HEADS * 3 * HEAD, group)
    grad_qkv = contract(saved["normed_team"], projected_grad, 0, 1).astype(BF16)
    team_part = contract(projected_grad, qkv_weight, 0, 1).astype(BF16)
    team_part = in_order(team_part.reshape(TEAM_SIZE, stretch, D), member)
    norm_grad, grad_gain = norm_back(
        saved["stream"], gain_one, saved["factor_one"], team_sum(team_part)
    )
    return (middle_grad + norm_grad, grad_gain, grad_qkv, terms)


def team_turn(rows, member):
    pieces = rows.reshape(TEAM_SIZE, -1, rows.shape[1])
    parts = [lax.dynamic_index_in_dim(pieces, member ^ k, 0, keepdims=False) for k in range(4)]
    return in_order(
        jnp.stack([parts[0]] + [from_member(parts[k], k) for k in (1, 2, 3)]), member
    )


def padded_down(grad_down, rest, width):
    blocks = grad_down.reshape(rest, -1, D)
    blocks = jnp.pad(blocks, ((0, 0), (0, TEAM_SIZE * width - blocks.shape[1]), (0, 0)))
    return blocks.reshape(D, D)


def swap_halves(rows):
    halves = rows.reshape(2, -1, rows.shape[1])
    at = lax.axis_index("dp")
    mine = lax.dynamic_index_in_dim(halves, at, 0, keepdims=False)
    other = lax.dynamic_index_in_dim(halves, 1 - at, 0, keepdims=False)
    return (mine, other)


def dp_sum(mine, other, *tokens):
    arrived = lax.ppermute(other, "dp", SWAP)
    if tokens:
        arrived = later(arrived, *tokens)
    return (mine.astype(F32) + arrived.astype(F32)).astype(BF16)


def z_sum(rows):
    return lax.psum_scatter(rows, "z", scatter_dimension=0, tiled=True)


def merge_feed_grads(grad_joint, grad_out, grad_down):
    total = lax.axis_size(ALL)
    rest, width = total // TEAM_SIZE, D // total
    return jnp.concatenate([grad_joint, grad_out, padded_down(grad_down, rest, width)], axis=1)


def feed_sums(mine, member):
    edge = mine.shape[1] - D
    down_sum = mine[: FF // lax.axis_size(ALL), edge:].astype(F32)
    turned = team_turn(mine[:, :edge], member).astype(F32)
    return (turned[:, :, : edge - D], turned[:, :, edge - D :], down_sum)


def qkv_order(columns):
    width = columns.shape[1]
    return (
        columns.reshape(TEAM_SIZE, width, TEAM_HEADS, 3, HEAD)
        .transpose(1, 3, 0, 2, 4)
        .reshape(width, 3 * D)
    )


def joint_order(columns):
    width = columns.shape[1]
    total = lax.axis_size(ALL)
    return (
        columns.reshape(TEAM_SIZE, width, 2, total // TEAM_SIZE, FF // total)
        .transpose(1, 2, 3, 0, 4)
        .reshape(width, 2 * FF)
    )


def pack_small(grad_gain_one, grad_gain_two, grad_router):
    small = jnp.concatenate([grad_gain_one[:, None], grad_gain_two[:, None], grad_router], axis=1)
    return jnp.pad(small, ((0, 0), (0, 64 - small.shape[1]))).astype(BF16)


def qkv_sums(grad_qkv, small):
    total = lax.axis_size(ALL)
    packed = jnp.concatenate([grad_qkv, small], axis=1)
    packed = exchange(packed.reshape(total, D // total, -1), ALL).astype(F32)
    edge = grad_qkv.shape[1]
    small_sum = packed[:, :, edge:].sum(axis=0)
    columns = packed[:, :, :edge].reshape(-1, TEAM_SIZE, D // total, edge).sum(axis=0)
    return (columns, small_sum)


def spread(rows, axes):
    count = lax.axis_size(axes)
    copies = jnp.broadcast_to(rows[None], (count,) + rows.shape)
    return exchange(copies, axes).reshape((-1,) + rows.shape[1:])


def dp_rows(rows):
    other = lax.ppermute(rows, "dp", SWAP)
    first = lax.axis_index("dp") == 0
    return jnp.concatenate([jnp.where(first, rows, other), jnp.where(first, other, rows)], axis=0)


def small_weights(gain_attn, gain_ffn, w_router):
    width = gain_attn.shape[1]
    small = jnp.concatenate(
        [gain_attn.T, gain_ffn.T, w_router.transpose(1, 0, 2).reshape(width, -1)], axis=1
    )
    return jnp.broadcast_to(small[None], (TEAM_SIZE,) + small.shape)


def split_small(smalls):
    smalls = smalls.astype(F32)
    gains, routers = [], []
    for layer in range(LAYERS):
        gains.append((smalls[:, layer], smalls[:, LAYERS + layer]))
        at = 2 * LAYERS + layer * EXPERTS
        routers.append(smalls[:, at : at + EXPERTS].astype(BF16))
    return (gains, routers)


def qkv_columns(w_qkv):
    width = w_qkv.shape[0]
    blocks = w_qkv.reshape(width, 3, TEAM_SIZE, TEAM_HEADS, HEAD)
    return blocks.transpose(2, 0, 3, 1, 4).reshape(TEAM_SIZE, width, -1)


def joint_columns(shared_gate_up):
    total = lax.axis_size(ALL)
    width = shared_gate_up.shape[0]
    blocks = shared_gate_up.reshape(width, 2, total // TEAM_SIZE, TEAM_SIZE, FF // total)
    return blocks.transpose(3, 0, 1, 2, 4).reshape(TEAM_SIZE, width, -1)


def padded_rows(shared_down):
    total = lax.axis_size(ALL)
    return jnp.pad(shared_down, ((0, TEAM_SIZE * D // total - shared_down.shape[0]), (0, 0)))


def down_rows(padded):
    total = lax.axis_size(ALL)
    return padded.reshape(total // TEAM_SIZE, -1, D)[:, : FF // total].reshape(-1, D)


def side_by_side(*arrays):
    return jnp.concatenate(arrays, axis=2)


def copies(rows):
    return jnp.broadcast_to(rows[None], (TEAM_SIZE,) + rows.shape)


def z_gather(rows):
    return lax.all_gather(rows, "z", axis=0, tiled=True)


def rest_gather(rows):
    return lax.all_gather(rows, REST, axis=0, tiled=True)


def dp_gather(rows, edges, token):
    parts = []
    for low, high in zip(edges, edges[1:]):
        token = dp_rows(later(rows[:, low:high], token))
        parts.append(token)
    return parts


def layers(
    x_in,
    cotangent,
    gain_attn,
    w_qkv,
    w_out,
    gain_ffn,
    w_router,
    shared_gate_up,
    shared_down,
    joint,
    down,
    context,
):
    split_count = context["split_count"]
    member = context["member"]
    stretch = x_in.shape[0]
    group = TEAM_SIZE * stretch
    last = LAYERS - 1
    stream = x_in.astype(F32)
    upstream = cotangent.astype(F32)
    grad_team = team_gather(cotangent).reshape(group, D)
    kept, feeds, rows_held = [], [], [None] * LAYERS
    weights = []

    width = w_qkv.shape[1]
    qkv_width, joint_width = 3 * D // TEAM_SIZE, 2 * FF // TEAM_SIZE
    small = small_weights(gain_attn, gain_ffn, w_router)
    first_width = qkv_width + small.shape[2]
    rows = exchange(
        side_by_side(
            qkv_columns(w_qkv[0]), small, copies(w_out[0]), joint_columns(shared_gate_up[0])
        ),
        TEAM,
    ).reshape(TEAM_SIZE * width, -1)
    first_rows = spread(rows[:, :first_width], "z")
    main_rows = z_gather(later(rows[:, first_width:], first_rows))
    following = [padded_rows(shared_down[0])]
    sizes = []
    if LAYERS > 1:
        rows = side_by_side(
            *[qkv_columns(w_qkv[layer]) for layer in range(1, LAYERS)],
            *[copies(w_out[layer]) for layer in range(1, LAYERS)],
            *[joint_columns(shared_gate_up[layer]) for layer in range(1, LAYERS)],
        )
        rows = team_turn(rows.reshape(TEAM_SIZE * width, -1), member)
        rows = rows.reshape(TEAM_SIZE * width, -1)
        edge = (LAYERS - 1) * qkv_width
        following.append(rows[:, :edge])
        last_rows = jnp.concatenate(
            [rows[:, edge:], *[padded_rows(shared_down[layer]) for layer in range(1, LAYERS)]],
            axis=1,
        )
    following = jnp.concatenate(following, axis=1)
    following = jnp.pad(following, ((0, 0), (0, -following.shape[1] % 128)))
    first_rows = spread(first_rows, "dp")
    gains, routers = split_small(first_rows[:, qkv_width:])
    qkv_weights = [first_rows[:, :qkv_width]]

    for layer in range(LAYERS):
        first = None
        if layer == 0:
            first = in_order(team_gather(x_in), member).reshape(group, D)
        head_rows, saved = attention_start(
            stream, first, gains[layer][0], qkv_weights[layer], context
        )
        if layer == 0:
            out_weight, joint_weight = dp_gather(
                main_rows, [0, D, D + joint_width], head_rows
            )
            attend(head_rows, saved, context, stretch)
            following = rest_gather(later(following, head_rows))
            down_weight = following[:, :D]
            for i in range(1, LAYERS):
                qkv_weights.append(following[:, D + (i - 1) * qkv_width : D + i * qkv_width])
            if LAYERS > 1:
                last_rows = rest_gather(later(last_rows, saved["wide"]))
        else:
            count = LAYERS - 1
            at = layer - 1
            starts = [at * D, count * D + at * joint_width, count * (D + joint_width) + at * D]
            out_weight, joint_weight, down_weight = [
                last_rows[:, start : start + size]
                for start, size in zip(starts, [D, joint_width, D])
            ]
            attend(head_rows, saved, context, stretch)
        weights.append(
            (
                gains[layer][0],
                qkv_weights[layer],
                out_weight,
                gains[layer][1],
                routers[layer],
                joint_weight,
                down_rows(down_weight),
            )
        )
        middle = attention_end(stream, saved, out_weight, context)
        kept.append(saved)
        feed = feed_start(middle, weights[layer], context)
        feeds.append(feed)
        outgoing = outgoing_rows(feed, context)
        if layer == last:
            outgoing = jnp.concatenate(
                [outgoing, outgoing_grads(feed, upstream, context)], axis=1
            )
        arrived = send_rows(outgoing, split_count)
        other = lax.ppermute(arrived, "dp", SWAP)
        rows_held[layer] = (arrived, other)
        returned = run_expert(
            layer,
            joint,
            down,
            (arrived, 0),
            (arrived, 1) if layer == last else None,
            True,
        )
        shared_out = shared_forward(feed, weights[layer], returned)
        returned = return_rows(returned, split_count)
        stream = feed_output(feed, shared_out, returned[:, :D], context)
    output = stream
    returned_grad = returned[:, D:]

    sums, feed_parts, head_parts = [None] * LAYERS, [None] * LAYERS, [None] * LAYERS
    terms = None
    for layer in reversed(range(LAYERS)):
        feed = feeds[layer]
        arrived, other = rows_held[layer]
        if layer == last:
            own = ((arrived, 0), (arrived, 1))
            others = ((other, 0), (other, 1))
        else:
            grad_team = team_gather(upstream.astype(BF16)).reshape(group, D)
            arrived_grad = send_rows(outgoing_grads(feed, upstream, context), split_count)
            packed = z_sum(dp_sum(*waiting, arrived_grad))
            packed = team_turn(packed, member).astype(F32)
            edge = 3 * D // TEAM_SIZE
            head_parts[layer + 1] = (packed[:, :, :edge], packed[:, :, edge:].sum(axis=0))
            own = ((arrived, 0), (arrived_grad, 0))
            others = ((other, 0), (lax.ppermute(arrived_grad, "dp", SWAP), 0))
            returned_grad = run_expert(
                layer, joint, down, (arrived, 0), (arrived_grad, 0), False
            )
            returned_grad = return_rows(returned_grad, split_count)
        shared_grad, grad_joint, grad_down = shared_backward(feed, grad_team, weights[layer])
        middle_grad, grad_gain_two, grad_router = feed_backward(
            feed, upstream, shared_grad, returned_grad, weights[layer], context
        )
        attn_grad = middle_grad.astype(BF16)
        grad_out = jnp.dot(kept[layer]["mixed"], attn_grad, preferred_element_type=F32).astype(BF16)
        feed_mine, feed_other = swap_halves(merge_feed_grads(grad_joint, grad_out, grad_down))
        feed_both = dp_sum(feed_mine, feed_other)
        upstream, grad_gain_one, grad_qkv, terms = attention_backward(
            middle_grad,
            weights[layer],
            context,
            kept[layer],
            [feed_other],
            feed_both,
            (layer, own, others, joint, down, terms),
        )
        columns, out_sum, down_sum = feed_sums(z_sum(feed_both), member)
        small = pack_small(grad_gain_one, grad_gain_two, grad_router)
        if layer > 0:
            waiting = swap_halves(jnp.concatenate([grad_qkv, small], axis=1))
        else:
            qkv_sum, small_sum = qkv_sums(grad_qkv, small)
        feed_parts[layer] = (columns, out_sum.sum(axis=0), down_sum)
        if layer == 0:
            head_parts[0] = (qkv_sum, small_sum)
    for layer in range(LAYERS):
        columns, out_sum, down_sum = feed_parts[layer]
        qkv_sum, small_sum = head_parts[layer]
        sums[layer] = (
            small_sum[:, 0],
            qkv_order(qkv_sum),
            out_sum,
            small_sum[:, 1],
            small_sum[:, 2 : 2 + EXPERTS],
            joint_order(columns),
            down_sum,
        )
    return (output, upstream, sums, terms)


def query_spans(block_row, group, part, parts):
    length = block_row.shape[0]
    limit = jnp.sum((block_row[None, :] <= block_row[:, None]).astype(jnp.int32), axis=1)
    tiles = length // QUERY_TILE // parts
    base = part * tiles
    ends = lax.dynamic_slice_in_dim(limit.reshape(-1, QUERY_TILE), base, tiles, 0)
    full = ends[:, 0] // group
    some = (ends[:, -1] + group - 1) // group
    base = jnp.full((1,), base, jnp.int32)
    return (full, some, base, limit[None, :], tiles, parts)


def local(
    x_in,
    block_ids,
    expert_ids,
    cotangent,
    gain_attn,
    w_qkv,
    w_out,
    gain_ffn,
    w_router,
    shared_gate_up,
    shared_down,
    expert_gate_up,
    expert_down,
):
    stretch = x_in.shape[1]
    group = TEAM_SIZE * stretch
    deep = lax.axis_size("z")
    parts = max(1, deep // TEAM_SIZE)
    at = lax.axis_index("z")
    member = lax.axis_index("core") * lax.axis_size("ulysses") + lax.axis_index("ulysses")
    half_size = HEAD // 2
    spacing = 10000.0 ** (-jnp.arange(half_size).astype(F32) * 2.0 / HEAD)
    positions = (at * group + jnp.arange(group, dtype=jnp.int32)).astype(F32)
    angles = spacing[:, None] * positions[None, :]
    tables, hits = route_tables(expert_ids[0])
    part = at % parts
    context = dict(
        member=member,
        cosine=jnp.cos(angles),
        sine=jnp.sin(angles),
        tables=tables,
        hits=hits,
        parts=parts,
        part=part,
        pieces=deep * TEAM_SIZE,
        split_count=deep * TEAM_SIZE // EXPERTS,
        spans=query_spans(block_ids[0], group, part, parts),
    )
    stream, upstream, sums, terms = layers(
        x_in[0],
        cotangent[0],
        gain_attn,
        w_qkv,
        w_out,
        gain_ffn,
        w_router,
        shared_gate_up,
        shared_down,
        expert_gate_up,
        expert_down,
        context,
    )
    stacked = [jnp.stack([sums[layer][i] for layer in range(LAYERS)]) for i in range(7)]
    return (
        stream.astype(BF16)[None],
        upstream.astype(BF16)[None],
        *stacked,
        *terms,
    )


def solution(mesh):
    dp, blk, ulysses = mesh.devices.shape
    grid = Mesh(mesh.devices.reshape(dp, blk // 2, 2, ulysses), ALL)
    rows = P("dp", SEQ, None)
    in_specs = (
        rows,
        P("dp", None),
        rows,
        rows,
        P(None, ALL),
        P(None, ALL, None),
        P(None, ALL, None),
        P(None, ALL),
        P(None, ALL, None),
        P(None, ALL, None),
        P(None, ALL, None),
        P(None, SEQ, None, None),
        P(None, SEQ, None, None),
    )
    out_specs = (
        rows,
        rows,
        P(None, ALL),
        P(None, ALL, None),
        P(None, ALL, None),
        P(None, ALL),
        P(None, ALL, None),
        P(None, ALL, None),
        P(None, ALL, None),
        P(None, SEQ, None, None),
        P(None, SEQ, None, None),
    )
    return jax.shard_map(local, mesh=grid, in_specs=in_specs, out_specs=out_specs, check_vma=False)
```

```python
import functools
import math

import jax
import jax.numpy as jnp
from jax import lax
from jax.experimental import pallas as pl
from jax.experimental.pallas import tpu as pltpu
from jax.sharding import Mesh
from jax.sharding import PartitionSpec as P

D = 768
HEADS = 12
HEAD = 64
FF = 2048
EXPERTS = 16
LAYERS = 2
MOST = 21
SLOTS = -(-MOST // 8) * 8
TEAM_SIZE = 4
TEAM_HEADS = HEADS // TEAM_SIZE

ALL = ("dp", "z", "core", "ulysses")
SEQ = ("z", "core", "ulysses")
TEAM = ("core", "ulysses")
REST = ("dp", "z")

NORM_EPS = 1e-06
NEG_BIG = -1e30
PRECISE = lax.Precision.HIGHEST
F32 = jnp.float32
BF16 = jnp.bfloat16
QUERY_TILE = 256
MIB = 1024 * 1024


def vmem(size):
    return pltpu.CompilerParams(vmem_limit_bytes=61 * MIB)


def cost(flops, moved, steps=0):
    return pl.CostEstimate(flops=flops, bytes_accessed=moved, transcendentals=steps)


def contract(left, right, left_dim, right_dim):
    return lax.dot_general(
        left, right, (((left_dim,), (right_dim,)), ((), ())), preferred_element_type=F32
    )


def exchange(rows, axes):
    return lax.all_to_all(rows, axes, split_axis=0, concat_axis=0, tiled=True)


SWAP = [(0, 1), (1, 0)]


def from_member(rows, turn):
    if turn == 1:
        return lax.ppermute(rows, "ulysses", SWAP)
    if turn == 2:
        return lax.ppermute(rows, "core", SWAP)
    return lax.ppermute(rows, TEAM, [(i, 3 - i) for i in range(4)])


def team_gather(rows):
    return jnp.stack([rows] + [from_member(rows, turn) for turn in (1, 2, 3)])


def in_order(stacked, member):
    turns = [jnp.equal(member, i) for i in range(4)]
    pieces = []
    for k in range(4):
        piece = stacked[k ^ 3]
        for i in range(3):
            piece = jnp.where(turns[i], stacked[k ^ i], piece)
        pieces.append(piece)
    return jnp.stack(pieces)


def team_sum(parts):
    total = parts[0].astype(F32)
    for turn in (1, 2, 3):
        total = total + from_member(parts[turn].astype(BF16), turn).astype(F32)
    return total


def rms_factor(stream):
    return lax.rsqrt(jnp.mean(stream * stream, axis=-1, keepdims=True) + NORM_EPS)


def norm_back(stream, gain, factor, upstream):
    weighted = upstream * gain
    inner_mean = jnp.mean(weighted * stream, axis=-1, keepdims=True)
    grad_stream = factor * weighted - stream * factor * factor * factor * inner_mean
    grad_gain = jnp.sum(upstream * stream * factor, axis=0)
    return (grad_stream, grad_gain)


def attention_kernel(full_ref, some_ref, base_ref, rows_ref, limit_ref, out_ref, wide_ref, log_ref, keys):
    span = rows_ref.shape[2]
    step = pl.program_id(0)
    per_block = span // QUERY_TILE

    @pl.when(step == 0)
    def _():
        for s in range(rows_ref.shape[0]):
            keys[s] = rows_ref[s, HEAD : 2 * HEAD, :].T

    tile = base_ref[0] + step
    lanes = pl.ds(pl.multiple_of((tile % per_block) * QUERY_TILE, QUERY_TILE), QUERY_TILE)
    queries = rows_ref[tile // per_block, 0:HEAD, lanes] * BF16(HEAD**-0.5)
    limit = limit_ref[...]
    key_index = lax.broadcasted_iota(jnp.int32, (span, QUERY_TILE), 0)

    def sweep(s, state, masked):
        highest, total, running = state
        scores = jnp.dot(keys[s], queries, preferred_element_type=F32)
        if masked:
            scores = jnp.where(key_index < limit - s * span, scores, NEG_BIG)
        raised = jnp.maximum(highest, jnp.max(scores, axis=0, keepdims=True))
        terms = jnp.exp(scores - raised)
        shrink = jnp.exp(highest - raised)
        total = total * shrink + jnp.sum(terms, axis=0, keepdims=True)
        running = running * shrink + jnp.dot(
            rows_ref[s, 2 * HEAD :, :], terms.astype(BF16), preferred_element_type=F32
        )
        return (raised, total, running)

    state = (
        jnp.full((1, QUERY_TILE), NEG_BIG, F32),
        jnp.zeros((1, QUERY_TILE), F32),
        jnp.zeros((HEAD, QUERY_TILE), F32),
    )
    state = lax.fori_loop(0, full_ref[step], lambda s, c: sweep(s, c, False), state)
    state = lax.fori_loop(full_ref[step], some_ref[step], lambda s, c: sweep(s, c, True), state)
    highest, total, running = state
    result = running / total
    log_ref[...] = highest + jnp.log(total)
    wide_ref[...] = result
    stretch = out_ref.shape[2]
    for i in range(QUERY_TILE // stretch):
        out_ref[i] = result[:, i * stretch : (i + 1) * stretch].astype(BF16)


def attention_back_kernel(
    full_ref, some_ref, base_ref, rows_ref, limit_ref, grad_ref, wide_ref, log_ref, *refs
):
    out_ref, keys, values, key_sum, value_sum = refs[-5:]
    span = rows_ref.shape[2]
    blocks = rows_ref.shape[0]
    step = pl.program_id(0)
    per_block = span // QUERY_TILE

    @pl.when(step == 0)
    def _():
        for s in range(blocks):
            keys[s] = rows_ref[s, HEAD : 2 * HEAD, :].T
            values[s] = rows_ref[s, 2 * HEAD :, :].T
        key_sum[...] = jnp.zeros_like(key_sum)
        value_sum[...] = jnp.zeros_like(value_sum)
        out_ref[...] = jnp.zeros_like(out_ref)

    tile = base_ref[0] + step
    lanes = pl.ds(pl.multiple_of((tile % per_block) * QUERY_TILE, QUERY_TILE), QUERY_TILE)
    queries = rows_ref[tile // per_block, 0:HEAD, lanes] * BF16(HEAD**-0.5)
    limit = limit_ref[...]
    key_index = lax.broadcasted_iota(jnp.int32, (span, QUERY_TILE), 0)
    grads = jnp.concatenate([grad_ref[i] for i in range(grad_ref.shape[0])], axis=1)
    delta = jnp.sum(grads.astype(F32) * wide_ref[...], axis=0, keepdims=True)
    logs = log_ref[...]

    def sweep(s, query_grad, masked):
        scores = jnp.dot(keys[s], queries, preferred_element_type=F32)
        probs = jnp.exp(scores - logs)
        if masked:
            probs = jnp.where(key_index < limit - s * span, probs, 0.0)
        prob_grad = jnp.dot(values[s], grads, preferred_element_type=F32)
        score_grad = (probs * (prob_grad - delta)).astype(BF16)
        value_sum[s] += contract(grads, probs.astype(BF16), 1, 1)
        key_sum[s] += contract(queries, score_grad, 1, 1)
        return query_grad + jnp.dot(
            rows_ref[s, HEAD : 2 * HEAD, :], score_grad, preferred_element_type=F32
        )

    query_grad = jnp.zeros((HEAD, QUERY_TILE), F32)
    query_grad = lax.fori_loop(0, full_ref[step], lambda s, c: sweep(s, c, False), query_grad)
    query_grad = lax.fori_loop(
        full_ref[step], some_ref[step], lambda s, c: sweep(s, c, True), query_grad
    )
    out_ref[tile // per_block, 0:HEAD, lanes] = (query_grad * HEAD**-0.5).astype(BF16)

    @pl.when(step == pl.num_programs(0) - 1)
    def _():
        out_ref[:, HEAD : 2 * HEAD, :] = key_sum[...].astype(BF16)
        out_ref[:, 2 * HEAD :, :] = value_sum[...].astype(BF16)


def fixed_attention_kernel(place_ref, *refs):
    rows_ref, out_ref, wide_ref, log_ref, keys, values = refs[-6:]
    blocks, _, span = rows_ref.shape
    pieces, limit_ref = refs[:blocks], refs[blocks]
    for turn in range(blocks):
        rows_ref[lax.rem(place_ref[1] + blocks - turn, blocks)] = pieces[turn][...]
    length = blocks * span
    stretch = out_ref.shape[2]
    for s in range(blocks):
        keys[s * span : (s + 1) * span, :] = rows_ref[s, HEAD : 2 * HEAD, :].T
        values[:, s * span : (s + 1) * span] = rows_ref[s, 2 * HEAD :, :]
    key_index = lax.broadcasted_iota(jnp.int32, (2 * QUERY_TILE, QUERY_TILE), 0)
    for tile in range(length // QUERY_TILE):
        start = tile * QUERY_TILE
        end = min(start + 2 * QUERY_TILE, length)
        lanes = slice(start % span, start % span + QUERY_TILE)
        queries = rows_ref[start // span, 0:HEAD, lanes] * BF16(HEAD**-0.5)
        scores = jnp.dot(keys[start:end, :], queries, preferred_element_type=F32)
        limit = limit_ref[:, start : start + QUERY_TILE] - start
        scores = jnp.where(key_index[: end - start] < limit, scores, NEG_BIG)
        highest = jnp.max(scores, axis=0, keepdims=True)
        if start > 0:
            before = jnp.dot(keys[:start, :], queries, preferred_element_type=F32)
            highest = jnp.maximum(highest, jnp.max(before, axis=0, keepdims=True))
        terms = jnp.exp(scores - highest)
        total = jnp.sum(terms, axis=0, keepdims=True)
        result = jnp.dot(values[:, start:end], terms.astype(BF16), preferred_element_type=F32)
        if start > 0:
            terms = jnp.exp(before - highest)
            total = total + jnp.sum(terms, axis=0, keepdims=True)
            result = result + jnp.dot(
                values[:, :start], terms.astype(BF16), preferred_element_type=F32
            )
        result = result / total
        log_ref[:, start : start + QUERY_TILE] = highest + jnp.log(total)
        wide_ref[:, start : start + QUERY_TILE] = result
        for i in range(QUERY_TILE // stretch):
            out_ref[start // stretch + i] = result[:, i * stretch : (i + 1) * stretch].astype(BF16)


def fixed_attention_back_kernel(place_ref, rows_ref, limit_ref, grad_ref, wide_ref, log_ref, *refs):
    blocks, _, span = rows_ref.shape
    out_ref, keys, values, key_sum, value_sum = refs[-5:]
    outs = refs[-5 - blocks : -5]
    length = blocks * span
    stretch = grad_ref.shape[2]
    for s in range(blocks):
        keys[s * span : (s + 1) * span, :] = rows_ref[s, HEAD : 2 * HEAD, :].T
        values[s * span : (s + 1) * span, :] = rows_ref[s, 2 * HEAD :, :].T
    key_sum[...] = jnp.zeros_like(key_sum)
    value_sum[...] = jnp.zeros_like(value_sum)
    key_index = lax.broadcasted_iota(jnp.int32, (2 * QUERY_TILE, QUERY_TILE), 0)
    for tile in range(length // QUERY_TILE):
        start = tile * QUERY_TILE
        end = min(start + 2 * QUERY_TILE, length)
        lanes = slice(start % span, start % span + QUERY_TILE)
        queries = rows_ref[start // span, 0:HEAD, lanes] * BF16(HEAD**-0.5)
        pieces = QUERY_TILE // stretch
        grads = jnp.concatenate([grad_ref[tile * pieces + i] for i in range(pieces)], axis=1)
        wide = wide_ref[:, start : start + QUERY_TILE]
        delta = jnp.sum(grads.astype(F32) * wide, axis=0, keepdims=True)
        logs = log_ref[:, start : start + QUERY_TILE]
        limit = limit_ref[:, start : start + QUERY_TILE] - start
        query_grad = jnp.zeros((HEAD, QUERY_TILE), F32)
        for low, high in ((0, start), (start, end)):
            if low == high:
                continue
            scores = jnp.dot(keys[low:high, :], queries, preferred_element_type=F32)
            probs = jnp.exp(scores - logs)
            if low == start:
                probs = jnp.where(key_index[: high - low] < limit, probs, 0.0)
            prob_grad = jnp.dot(values[low:high, :], grads, preferred_element_type=F32)
            score_grad = (probs * (prob_grad - delta)).astype(BF16)
            value_sum[:, low:high] += contract(grads, probs.astype(BF16), 1, 1)
            key_sum[:, low:high] += contract(queries, score_grad, 1, 1)
            query_grad = query_grad + contract(keys[low:high, :], score_grad, 0, 0)
        out_ref[start // span, 0:HEAD, lanes] = (query_grad * HEAD**-0.5).astype(BF16)
    for s in range(blocks):
        out_ref[s, HEAD : 2 * HEAD, :] = key_sum[:, s * span : (s + 1) * span].astype(BF16)
        out_ref[s, 2 * HEAD :, :] = value_sum[:, s * span : (s + 1) * span].astype(BF16)
    for turn in range(blocks):
        outs[turn][...] = out_ref[lax.rem(place_ref[1] + turn, blocks)]


def at_once(shape):
    return pl.BlockSpec(shape, lambda step: (0,) * len(shape))


ANYWHERE = pl.BlockSpec(memory_space=pl.ANY)
IN_SMEM = pl.BlockSpec(memory_space=pltpu.SMEM)


def fixed_attention(pieces, limit, place, stretch, after):
    blocks = len(pieces)
    features, span = pieces[0].shape
    length = blocks * span
    return pl.pallas_call(
        fixed_attention_kernel,
        grid=(1,),
        in_specs=[IN_SMEM, *[at_once(array.shape) for array in (*pieces, limit)]]
        + [ANYWHERE] * len(after),
        out_specs=[
            at_once((blocks, features, span)),
            at_once((length // stretch, HEAD, stretch)),
            at_once((HEAD, length)),
            at_once((1, length)),
        ],
        out_shape=[
            jax.ShapeDtypeStruct((blocks, features, span), BF16),
            jax.ShapeDtypeStruct((length // stretch, HEAD, stretch), BF16),
            jax.ShapeDtypeStruct((HEAD, length), F32),
            jax.ShapeDtypeStruct((1, length), F32),
        ],
        scratch_shapes=[pltpu.VMEM((length, HEAD), BF16), pltpu.VMEM((HEAD, length), BF16)],
        compiler_params=vmem(16 * MIB),
        cost_estimate=cost(features * length * length // 48, features * length * 4, length * length),
        name="attend",
    )(place, *pieces, limit, *after)


def fixed_attention_back(rows, limit, grads, wide, logs, place, later_than):
    blocks, features, span = rows.shape
    length = blocks * span
    return pl.pallas_call(
        fixed_attention_back_kernel,
        grid=(1,),
        in_specs=[
            IN_SMEM,
            *[at_once(array.shape) for array in (rows, limit, grads, wide, logs)],
        ]
        + [ANYWHERE] * len(later_than),
        out_specs=[at_once((features, span))] * blocks,
        out_shape=[jax.ShapeDtypeStruct((features, span), BF16)] * blocks,
        scratch_shapes=[
            pltpu.VMEM(rows.shape, BF16),
            pltpu.VMEM((length, HEAD), BF16),
            pltpu.VMEM((length, HEAD), BF16),
            pltpu.VMEM((HEAD, length), F32),
            pltpu.VMEM((HEAD, length), F32),
        ],
        compiler_params=vmem(20 * MIB),
        cost_estimate=cost(rows.size * length // 16, rows.size * 4, length * length),
        name="attend_back",
    )(place, rows, limit, grads, wide, logs, *later_than)


def whole(shape):
    return pl.BlockSpec(shape, lambda step, *_: (0,) * len(shape))


def tile_at(step, full, some, base):
    return (0, base[0] + step)


def attention(rows, spans, stretch):
    full, some, base, limit, tiles, parts = spans
    blocks, _, span = rows.shape
    length = tiles * QUERY_TILE
    return pl.pallas_call(
        attention_kernel,
        grid_spec=pltpu.PrefetchScalarGridSpec(
            num_scalar_prefetch=3,
            grid=(tiles,),
            in_specs=[whole(rows.shape), pl.BlockSpec((1, QUERY_TILE), tile_at)],
            out_specs=[
                pl.BlockSpec((QUERY_TILE // stretch, HEAD, stretch), lambda step, *_: (step, 0, 0)),
                pl.BlockSpec((HEAD, QUERY_TILE), lambda step, *_: (0, step)),
                pl.BlockSpec((1, QUERY_TILE), lambda step, *_: (0, step)),
            ],
            scratch_shapes=[pltpu.VMEM((blocks, span, HEAD), BF16)],
        ),
        out_shape=[
            jax.ShapeDtypeStruct((length // stretch, HEAD, stretch), BF16),
            jax.ShapeDtypeStruct((HEAD, length), F32),
            jax.ShapeDtypeStruct((1, length), F32),
        ],
        compiler_params=vmem(52 * MIB),
        cost_estimate=cost(rows.size * length // 48, rows.size * 4, length * length),
        name="attend",
    )(full, some, base, rows, limit)


def attention_back(rows, spans, grads, wide, logs, later_than):
    full, some, base, limit, tiles, parts = spans
    blocks, _, span = rows.shape
    stretch = grads.shape[2]
    return pl.pallas_call(
        attention_back_kernel,
        grid_spec=pltpu.PrefetchScalarGridSpec(
            num_scalar_prefetch=3,
            grid=(tiles,),
            in_specs=[
                whole(rows.shape),
                pl.BlockSpec((1, QUERY_TILE), tile_at),
                pl.BlockSpec((QUERY_TILE // stretch, HEAD, stretch), lambda step, *_: (step, 0, 0)),
                pl.BlockSpec((HEAD, QUERY_TILE), lambda step, *_: (0, step)),
                pl.BlockSpec((1, QUERY_TILE), lambda step, *_: (0, step)),
                *[pl.BlockSpec(memory_space=pl.ANY)] * len(later_than),
            ],
            out_specs=whole(rows.shape),
            scratch_shapes=[
                pltpu.VMEM((blocks, span, HEAD), BF16),
                pltpu.VMEM((blocks, span, HEAD), BF16),
                pltpu.VMEM((blocks, HEAD, span), F32),
                pltpu.VMEM((blocks, HEAD, span), F32),
            ],
        ),
        out_shape=jax.ShapeDtypeStruct(rows.shape, BF16),
        compiler_params=vmem(52 * MIB),
        cost_estimate=cost(rows.size * tiles * QUERY_TILE // 16, rows.size * 4, rows.size),
        name="attend_back",
    )(full, some, base, rows, limit, grads, wide, logs, *later_than)


def run_kernel(kernel, operands, outputs, scratch=(), after=(), flops=0, name=None, room=6):
    moved = sum(array.size * array.dtype.itemsize for array in operands)
    size = 2 * moved
    for times, arrays in ((2, outputs), (1, scratch)):
        for shape, dtype in arrays:
            size += times * math.prod(shape) * jnp.dtype(dtype).itemsize
    given, kept = len(operands), len(operands) + len(after)
    return pl.pallas_call(
        lambda *refs: kernel(*refs[:given], *refs[kept:]),
        grid=(1,),
        in_specs=[IN_SMEM, *[at_once(array.shape) for array in operands[1:]]]
        + [ANYWHERE] * len(after),
        out_specs=[at_once(shape) for shape, _ in outputs],
        out_shape=[jax.ShapeDtypeStruct(shape, dtype) for shape, dtype in outputs],
        scratch_shapes=[pltpu.VMEM(shape, dtype) for shape, dtype in scratch],
        compiler_params=vmem(room * MIB + size),
        cost_estimate=cost(flops, moved),
        name=name,
    )(*operands, *after)


def rows_at(index, size):
    return pl.ds(pl.multiple_of(index * size, size), size)


def qkv_kernel(fixed, normed, place_ref, *refs):
    rows_refs, (gain_ref, weight_ref, cosine_ref, sine_ref) = refs[:4], refs[4:8]
    pieces, team, heads = refs[8:-2], refs[-2], refs[-1]
    member = place_ref[0]
    stretch = rows_refs[0].shape[0]
    half = HEAD // 2
    for turn in range(4):
        rows = rows_refs[turn][...]
        if not normed:
            wide = rows.astype(F32)
            rows = (wide * rms_factor(wide) * gain_ref[...]).astype(BF16)
        team[rows_at(member ^ turn, stretch), :] = rows
    projected = contract(weight_ref[...], team[...], 0, 1)
    cosine, sine = cosine_ref[...], sine_ref[...]
    for head in range(TEAM_HEADS):
        for part in range(3):
            at = (head * 3 + part) * HEAD
            first, second = projected[at : at + half], projected[at + half : at + HEAD]
            if part < 2:
                first, second = (
                    first * cosine - second * sine,
                    second * cosine + first * sine,
                )
            heads[head, part * HEAD : part * HEAD + half] = first.astype(BF16)
            heads[head, part * HEAD + half : (part + 1) * HEAD] = second.astype(BF16)
    for turn, piece in enumerate(pieces):
        head = turn
        if fixed:
            head = lax.rem(place_ref[1] + turn, len(pieces)) - place_ref[2]
            head = jnp.clip(head, 0, TEAM_HEADS - 1)
        piece[...] = heads[head]


def qkv_step(rows, normed, gain, weight, after, context):
    group = TEAM_SIZE * rows[0].shape[0]
    fixed = context["parts"] == 1
    return run_kernel(
        functools.partial(qkv_kernel, fixed, normed),
        [context["place"], *rows, gain, weight, context["cosine"], context["sine"]],
        [((3 * HEAD, group), BF16)] * (context["deep"] if fixed else TEAM_HEADS)
        + [((group, D), BF16)],
        [((TEAM_HEADS, 3 * HEAD, group), BF16)],
        after,
        flops=2 * group * D * weight.shape[1],
        name="qkv",
    )


def qkv_back_kernel(fixed, halves, place_ref, *refs):
    count = len(refs) - (16 if halves else 15)
    grads, refs = refs[:count], refs[count:]
    weight_ref, cosine_ref, sine_ref, team_ref, gain_ref, small_ref = refs[:6]
    outs, (stacked, turned, parts, packed) = refs[6:-4], refs[-4:]
    half = HEAD // 2
    stretch = outs[0].shape[0]
    for turn in range(count):
        stacked[turn] = grads[turn][...]
    cosine, sine = cosine_ref[...], sine_ref[...]
    for head in range(TEAM_HEADS):
        at = head
        if fixed:
            at = lax.rem(place_ref[1] - head - place_ref[2] + 2 * count, count)
        rows = stacked[at].astype(F32)
        for part in range(3):
            low = part * HEAD
            first, second = rows[low : low + half], rows[low + half : low + HEAD]
            if part < 2:
                first, second = (
                    first * cosine + second * sine,
                    second * cosine - first * sine,
                )
            low += head * 3 * HEAD
            turned[low : low + half] = first.astype(BF16)
            turned[low + half : low + HEAD] = second.astype(BF16)
    projected_grad = turned[...].T
    normed_grad = contract(projected_grad, weight_ref[...], 1, 1)
    parts[...] = normed_grad.astype(BF16)
    for turn in range(4):
        outs[turn][...] = parts[rows_at(place_ref[0] ^ turn, stretch), :]
    team = team_ref[...]
    edge = projected_grad.shape[1]
    packed[:, :edge] = contract(team, projected_grad, 0, 0).astype(BF16)
    gain_grad = jnp.sum(normed_grad * team.astype(F32), axis=0, keepdims=True) / gain_ref[...]
    small = small_ref[...]
    lane = lax.broadcasted_iota(jnp.int32, small.shape, 1)
    small = jnp.where(lane == 0, jnp.broadcast_to(gain_grad, (128, D)).T, small)
    packed[:, edge:] = small[:, : packed.shape[1] - edge].astype(BF16)
    if halves:
        outs[4][...] = packed[rows_at(place_ref[3], D // 2), :]
        outs[5][...] = packed[rows_at(1 - place_ref[3], D // 2), :]
    else:
        outs[4][...] = packed[...]


def qkv_back_step(grads, weight, team, gain, small, halves, after, context):
    group = team.shape[0]
    width = weight.shape[1] + 64
    packed = [((D // 2, width), BF16)] * 2 if halves else [((D, width), BF16)]
    return run_kernel(
        functools.partial(qkv_back_kernel, context["parts"] == 1, halves),
        [
            context["place"],
            *grads,
            weight,
            context["cosine"],
            context["sine"],
            team,
            gain,
            small,
        ],
        [((group // TEAM_SIZE, D), BF16)] * TEAM_SIZE + packed,
        [
            ((len(grads), 3 * HEAD, group), BF16),
            ((weight.shape[1], group), BF16),
            ((group, D), BF16),
            ((D, width), BF16),
        ],
        after,
        flops=4 * group * D * weight.shape[1],
        name="qkv_back",
    )


def head_slot(head, fixed):
    member = head // TEAM_HEADS
    return (head % TEAM_HEADS + (member // 2 if fixed else 0)) * TEAM_SIZE + member


def chosen(ids_ref, choice):
    ids = ids_ref[:, choice : choice + 1]
    return lax.broadcasted_iota(jnp.int32, (ids.shape[0], 128), 1) == ids + 2


def row_table(slots_ref, choice):
    slots = slots_ref[:, choice : choice + 1]
    index = lax.broadcasted_iota(jnp.int32, (slots.shape[0], EXPERTS * SLOTS), 1)
    return jnp.where(index == slots, 1.0, 0.0).astype(BF16)


def slot_table(turned_ref, choice):
    slots = turned_ref[choice : choice + 1, :]
    index = lax.broadcasted_iota(jnp.int32, (EXPERTS * SLOTS, slots.shape[1]), 0)
    return jnp.where(index == slots, 1.0, 0.0).astype(BF16)


def slots_of_grads(turned_ref, gates, upstream):
    terms = [
        jnp.dot(
            slot_table(turned_ref, c),
            (gates[:, c : c + 1] * upstream).astype(BF16),
            preferred_element_type=F32,
        )
        for c in range(2)
    ]
    return (terms[0] + terms[1]).astype(BF16)


def feed_kernel(fixed, last, place_ref, *refs):
    back_ref, stream_ref, weight_ref, gain_ref, router_ref, ids_ref, turned_ref = refs[:7]
    middle_ref, normed_ref, gates_ref, out_ref, mixed_ref = refs[-5:]
    for head in range(HEADS):
        mixed_ref[head * HEAD : (head + 1) * HEAD, :] = back_ref[head_slot(head, fixed)]
    middle = stream_ref[...].astype(F32) + contract(mixed_ref[...], weight_ref[...], 0, 0)
    normed = (middle * rms_factor(middle) * gain_ref[...]).astype(BF16)
    middle_ref[...] = middle
    normed_ref[...] = normed
    table = slot_table(turned_ref, 0) + slot_table(turned_ref, 1)
    out_ref[:, :D] = jnp.dot(table, normed, preferred_element_type=F32).astype(BF16)
    logits = jnp.dot(normed, router_ref[...], preferred_element_type=F32)
    picked = [
        jnp.sum(jnp.where(chosen(ids_ref, c), logits, 0.0), axis=1, keepdims=True)
        for c in range(2)
    ]
    highest = jnp.maximum(picked[0], picked[1])
    powers = [jnp.exp(pick - highest) for pick in picked]
    total = powers[0] + powers[1]
    gates = jnp.concatenate([powers[0] / total, powers[1] / total], axis=1)
    gates_ref[...] = gates
    if last:
        out_ref[:, D:] = slots_of_grads(turned_ref, gates, refs[7][...].astype(F32))


def feed_step(back, stream, out_weight, gain, router, upstream, after, context):
    stretch = stream.shape[0]
    last = upstream is not None
    operands = [
        context["place"],
        back,
        stream,
        out_weight,
        gain,
        router,
        context["ids"],
        context["turned_slots"],
    ]
    return run_kernel(
        functools.partial(feed_kernel, context["parts"] == 1, last),
        operands + ([upstream] if last else []),
        [
            ((stretch, D), F32),
            ((stretch, D), BF16),
            ((stretch, 2), F32),
            ((EXPERTS * SLOTS, 2 * D if last else D), BF16),
            ((D, stretch), BF16),
        ],
        (),
        after,
        flops=4 * stretch * D * D,
        name="feed",
    )


def add_up(parts):
    total = parts[0][...].astype(F32)
    for part in parts[1:]:
        total = total + part[...].astype(F32)
    return total


def layer_end_kernel(place_ref, *refs):
    returned_ref, middle_ref, gates_ref, slots_ref, gain_ref = refs[:5]
    parts = refs[5:9]
    stream_ref, gap_ref, normed_ref = refs[-3:]
    choices = [
        jnp.dot(row_table(slots_ref, c), returned_ref[...], preferred_element_type=F32)
        for c in range(2)
    ]
    gates = gates_ref[...]
    stream = middle_ref[...] + add_up(parts) + gates[:, 0:1] * choices[0]
    stream = stream + gates[:, 1:2] * choices[1]
    stream_ref[...] = stream
    gap_ref[...] = choices[0] - choices[1]
    normed_ref[...] = (stream * rms_factor(stream) * gain_ref[...]).astype(BF16)


def layer_end_step(returned, feed, parts, next_gain, after, context):
    shape = feed["middle"].shape
    return run_kernel(
        layer_end_kernel,
        [
            context["place"],
            returned,
            feed["middle"],
            feed["gates"],
            context["slots"],
            next_gain,
            *parts,
        ],
        [(shape, F32), (shape, F32), (shape, BF16)],
        (),
        after,
        flops=4 * shape[0] * D * returned.shape[0],
        name="layer_end",
    )


def feed_back_kernel(fixed, last, place_ref, *refs):
    (
        returned_ref,
        middle_ref,
        normed_ref,
        gates_ref,
        slots_ref,
        ids_ref,
        upstream_ref,
        gain_ref,
        router_ref,
        weight_ref,
    ) = refs[:10]
    parts = refs[10:14]
    outs = refs[-4:]
    tables = [row_table(slots_ref, c) for c in range(2)]
    gates = gates_ref[...]
    middle = middle_ref[...]
    upstream = upstream_ref[...].astype(F32)
    if last:
        choices = [
            jnp.dot(table, returned_ref[:, :D], preferred_element_type=F32) for table in tables
        ]
        gap = choices[0] - choices[1]
        output = middle + add_up(refs[14:18]) + gates[:, 0:1] * choices[0]
        refs[-5][...] = (output + gates[:, 1:2] * choices[1]).astype(BF16)
        grad_rows = returned_ref[:, D:]
    else:
        gap = refs[14][...]
        grad_rows = returned_ref[...]
    lead = gates[:, 0:1] * gates[:, 1:2] * jnp.sum(gap * upstream, axis=1, keepdims=True)
    logit_grad = jnp.where(chosen(ids_ref, 0), lead, 0.0) - jnp.where(
        chosen(ids_ref, 1), lead, 0.0
    )
    high = logit_grad.astype(BF16)
    low = (logit_grad - high.astype(F32)).astype(BF16)
    router = router_ref[...]
    normed_grad = (
        add_up(parts)
        + contract(high, router, 1, 1)
        + contract(low, router, 1, 1)
        + jnp.dot(tables[0] + tables[1], grad_rows, preferred_element_type=F32)
    )
    factor = rms_factor(middle)
    norm_grad, _ = norm_back(middle, gain_ref[...], factor, normed_grad)
    middle_grad = upstream + norm_grad
    attn_grad = middle_grad.astype(BF16)
    middle_grad_ref, attn_ref, heads_ref, small_ref = outs
    middle_grad_ref[...] = middle_grad
    attn_ref[...] = attn_grad
    mixed_grad = contract(weight_ref[...], attn_grad, 1, 1).astype(BF16)
    used = set()
    for head in range(HEADS):
        slot = head_slot(head, fixed)
        used.add(slot)
        heads_ref[slot] = mixed_grad[head * HEAD : (head + 1) * HEAD]
    for slot in range(heads_ref.shape[0]):
        if slot not in used:
            heads_ref[slot] = jnp.zeros_like(heads_ref[slot])
    gain_grad = jnp.sum(normed_grad * middle * factor, axis=0, keepdims=True)
    normed = normed_ref[...]
    small = contract(normed, high, 0, 0) + contract(normed, low, 0, 0)
    lane = lax.broadcasted_iota(jnp.int32, small.shape, 1)
    small_ref[...] = jnp.where(lane == 1, jnp.broadcast_to(gain_grad, (128, D)).T, small)


def feed_back_step(returned, feed, upstream, parts, others, weights, last, after, context):
    stretch = feed["middle"].shape[0]
    shape = (stretch, D)
    return run_kernel(
        functools.partial(feed_back_kernel, context["parts"] == 1, last),
        [
            context["place"],
            returned,
            feed["middle"],
            feed["normed_ffn"],
            feed["gates"],
            context["slots"],
            context["ids"],
            upstream,
            weights["gain_two"],
            weights["router"],
            weights["out"],
            *parts,
            *others,
        ],
        ([(shape, BF16)] if last else [])
        + [
            (shape, F32),
            (shape, BF16),
            ((TEAM_SIZE * TEAM_SIZE, HEAD, stretch), BF16),
            ((D, 128), F32),
        ],
        (),
        after,
        flops=4 * stretch * D * D,
        name="feed_back",
    )


def layer_start_kernel(more, place_ref, *refs):
    stream_ref, middle_grad_ref, gain_ref = refs[:3]
    parts = refs[3:7]
    stream = stream_ref[...].astype(F32)
    norm_grad, _ = norm_back(stream, gain_ref[...], rms_factor(stream), add_up(parts))
    upstream = middle_grad_ref[...] + norm_grad
    if more:
        gates_ref, turned_ref, wide_ref, out_ref = refs[7:9] + refs[-3:-2] + refs[-1:]
        wide_ref[...] = upstream
        refs[-2][...] = upstream.astype(BF16)
        out_ref[...] = slots_of_grads(turned_ref, gates_ref[...], upstream)
    else:
        refs[-1][...] = upstream.astype(BF16)


def layer_start_step(stream, middle_grad, gain, parts, feed, context):
    shape = stream.shape
    more = feed is not None
    return run_kernel(
        functools.partial(layer_start_kernel, more),
        [
            context["place"],
            stream,
            middle_grad,
            gain,
            *parts,
            *([feed["gates"], context["turned_slots"]] if more else []),
        ],
        [(shape, F32), (shape, BF16), ((EXPERTS * SLOTS, D), BF16)] if more else [(shape, BF16)],
        flops=4 * shape[0] * D * EXPERTS * SLOTS if more else 0,
        name="layer_start",
    )


def shared_grads_kernel(unit, place_ref, *refs):
    team_ref, joint_ref, hidden_ref, grads_ref = refs[:4]
    joint_outs, down_outs = refs[4:6], refs[6:8]
    half = D // 2
    units = hidden_ref.shape[1] // 2
    for place, dp in enumerate((place_ref[3], 1 - place_ref[3])):
        joint_outs[place][...] = contract(
            team_ref[:, rows_at(dp, half)], joint_ref[...], 0, 0
        ).astype(BF16)
        down = contract(hidden_ref[:, rows_at(dp, units)], grads_ref[...], 0, 0).astype(BF16)
        out = down_outs[place]
        for block in range(units // unit):
            low, high = block * unit, (block + 1) * unit
            at, end = block * half * unit // units, (block + 1) * half * unit // units
            out[at : at + unit] = down[low:high]
            out[at + unit : end] = jnp.zeros((end - at - unit, D), BF16)


def shared_grads_step(team, joint_grad, hidden, grad_team, context):
    return run_kernel(
        functools.partial(shared_grads_kernel, FF // lax.axis_size(ALL)),
        [context["place"], team, joint_grad, hidden, grad_team],
        [((D // 2, joint_grad.shape[1]), BF16)] * 2 + [((D // 2, D), BF16)] * 2,
        flops=2 * team.shape[0] * D * (joint_grad.shape[1] + D),
        name="shared_grads",
    )


def shared_grads(shared, context):
    team, grads, hidden, joint_grad = shared[-4:]
    return shared_grads_step(team, joint_grad, hidden, grads, context)


def out_grads_kernel(place_ref, mixed_ref, attn_ref, own_ref, other_ref):
    for out, dp in zip((own_ref, other_ref), (place_ref[3], 1 - place_ref[3])):
        out[...] = jnp.dot(
            mixed_ref[rows_at(dp, D // 2), :], attn_ref[...], preferred_element_type=F32
        ).astype(BF16)


def out_grads_step(mixed, attn_grad, context):
    return run_kernel(
        out_grads_kernel,
        [context["place"], mixed, attn_grad],
        [((D // 2, D), BF16)] * 2,
        flops=2 * mixed.shape[1] * D * D,
        name="out_grads",
    )


def feed_end_kernel(place_ref, *refs):
    layers_count = (len(refs) - 4) // 9
    pieces = refs[: 4 * layers_count]
    out_pieces = refs[4 * layers_count : 8 * layers_count]
    downs = refs[8 * layers_count : 9 * layers_count]
    joint_out, out_out, down_out, columns = refs[-4:]
    width = joint_out.shape[1]
    joint_width = pieces[0].shape[1]
    unit = down_out.shape[1]
    rest = joint_width // (2 * unit)
    for layer in range(layers_count):
        total = None
        for turn in range(4):
            columns[place_ref[0] ^ turn] = pieces[4 * layer + turn][...].astype(F32)
            part = out_pieces[4 * layer + turn][...].astype(F32)
            total = part if total is None else total + part
        out_out[layer] = total
        for member in range(4):
            rows = columns[member]
            for part in range(2):
                for block in range(rest):
                    low = (part * rest + block) * unit
                    at = part * (joint_out.shape[2] // 2) + (block * 4 + member) * unit
                    joint_out[layer, :, at : at + unit] = rows[:, low : low + unit]
        down_out[layer] = downs[layer][...].astype(F32)


def qkv_end_kernel(place_ref, *refs):
    first_ref, pieces = refs[0], refs[1:-3]
    qkv_out, small_out, columns = refs[-3:]
    edge = TEAM_HEADS * 3 * HEAD
    layers_count = qkv_out.shape[0]
    for layer in range(layers_count):
        small = None
        for turn in range(4):
            if layer == 0:
                total = None
                for block in range(first_ref.shape[0] // 4):
                    part = first_ref[block * 4 + turn].astype(F32)
                    total = part if total is None else total + part
                columns[turn] = total
            else:
                total = pieces[4 * (layer - 1) + turn][...].astype(F32)
                columns[place_ref[0] ^ turn] = total
            part = total[:, edge:]
            small = part if small is None else small + part
        small_out[layer] = small
        for member in range(4):
            rows = columns[member]
            for head in range(TEAM_HEADS):
                for part in range(3):
                    low = (head * 3 + part) * HEAD
                    at = part * D + (member * TEAM_HEADS + head) * HEAD
                    qkv_out[layer, :, at : at + HEAD] = rows[:, low : low + HEAD]


def logistic(values):
    return 0.5 * jnp.tanh(0.5 * values) + 0.5


def swiglu_back(gate_pre, up_pre, hidden_grad):
    sigmoid_gate = logistic(gate_pre)
    silu_gate = gate_pre * sigmoid_gate
    gate_grad = hidden_grad * up_pre * (sigmoid_gate + silu_gate * (1.0 - sigmoid_gate))
    up_grad = hidden_grad * silu_gate
    return (gate_grad.astype(BF16), up_grad.astype(BF16))


def swiglu(gate_pre, up_pre):
    return (gate_pre * logistic(gate_pre) * up_pre).astype(BF16)


def expert_kernel(forward, backward, *refs):
    inputs = 1 + backward
    rows_ref, grads_ref = refs[0], refs[inputs - 1]
    gate_ref, up_ref, down_ref, out_ref, total = refs[inputs:]
    step = pl.program_id(0)
    rows = rows_ref[...]
    gate, up, down = gate_ref[0, 0], up_ref[0, 0], down_ref[0, 0]
    gate_pre = jnp.dot(rows, gate, preferred_element_type=F32)
    up_pre = jnp.dot(rows, up, preferred_element_type=F32)
    terms = []
    if forward:
        terms.append(jnp.dot(swiglu(gate_pre, up_pre), down, preferred_element_type=F32))
    if backward:
        hidden_grad = contract(grads_ref[...], down, 1, 1).astype(BF16).astype(F32)
        gate_grad, up_grad = swiglu_back(gate_pre, up_pre, hidden_grad)
        terms.append(contract(gate_grad, gate, 1, 1) + contract(up_grad, up, 1, 1))

    @pl.when(step == 0)
    def _():
        for i, term in enumerate(terms):
            total[:, i * D : (i + 1) * D] = term

    @pl.when(step > 0)
    def _():
        for i, term in enumerate(terms):
            total[:, i * D : (i + 1) * D] += term

    @pl.when(step == pl.num_programs(0) - 1)
    def _():
        out_ref[...] = total[...].astype(BF16)


def run_expert(layer, joint, down, rows, grads, forward, after=()):
    half = joint.shape[3] // 2
    chunk = min(512, half)
    chunks = half // chunk
    given = [rows] + ([grads] if grads is not None else [])
    count = rows[0].shape[0]
    width = D * (int(forward) + int(grads is not None))
    drop = len(given) + 3
    body = functools.partial(expert_kernel, forward, grads is not None)
    return pl.pallas_call(
        lambda *refs: body(*refs[:drop], *refs[drop + len(after) :]),
        grid=(chunks,),
        in_specs=[
            *[pl.BlockSpec((count, D), lambda i, at=at: (0, at)) for _, at in given],
            pl.BlockSpec((1, 1, D, chunk), lambda i: (layer, 0, 0, i)),
            pl.BlockSpec((1, 1, D, chunk), lambda i: (layer, 0, 0, chunks + i)),
            pl.BlockSpec((1, 1, chunk, D), lambda i: (layer, 0, i, 0)),
            *[ANYWHERE] * len(after),
        ],
        out_specs=pl.BlockSpec((count, width), lambda i: (0, 0)),
        out_shape=jax.ShapeDtypeStruct((count, width), BF16),
        scratch_shapes=[pltpu.VMEM((count, width), F32)],
        compiler_params=vmem(
            4 * len(given) * count * D + 12 * D * chunk + 8 * count * width + 32 * count * chunk
        ),
        cost_estimate=cost(
            2 * count * D * half * (2 + int(forward) + 3 * int(grads is not None)),
            6 * D * half + 4 * count * width,
            count * half,
        ),
        name="expert_forward" if grads is None else "expert_both" if forward else "expert_back",
    )(*[array for array, _ in given], joint, joint, down, *after)


def expert_grad_kernel(place_ref, own_rows, own_grads, other_rows, other_grads, gate_ref, up_ref, down_ref, *refs):
    joint_out, down_out, rows_all, grads_all, turned, hold = refs[-6:]
    count = own_rows.shape[0]

    @pl.when((pl.program_id(0) == 0) & (pl.program_id(1) == 0))
    def _():
        own = rows_at(place_ref[3], count)
        other = rows_at(1 - place_ref[3], count)
        rows_all[own, :] = own_rows[...]
        rows_all[other, :] = other_rows[...]
        grads_all[own, :] = own_grads[...]
        grads_all[other, :] = other_grads[...]
        turned[...] = rows_all[...].T

    @pl.when(pl.program_id(1) == 0)
    def _():
        rows = rows_all[...]
        grads = grads_all[...]
        gate_pre = jnp.dot(rows, gate_ref[0, 0], preferred_element_type=F32)
        up_pre = jnp.dot(rows, up_ref[0, 0], preferred_element_type=F32)
        hidden_grad = contract(grads, down_ref[0, 0], 1, 1).astype(BF16).astype(F32)
        gate_grad, up_grad = swiglu_back(gate_pre, up_pre, hidden_grad)
        hold[...] = up_grad
        down_out[0, 0] = contract(swiglu(gate_pre, up_pre), grads, 0, 0)
        joint_out[0, 0] = jnp.dot(turned[...], gate_grad, preferred_element_type=F32)

    @pl.when(pl.program_id(1) == 1)
    def _():
        joint_out[0, 0] = jnp.dot(turned[...], hold[...], preferred_element_type=F32)


def expert_grads(layer, part, own, other, joint, down, before, later_than, context):
    half = joint.shape[3] // 2
    given = [*own, *other]
    count = given[0][0].shape[0]
    chunk = min(512 if count <= 512 else 128, half // 2)
    chunks = half // chunk
    steps = chunks // 2
    first = part * steps
    in_specs = [
        IN_SMEM,
        *[pl.BlockSpec((count, D), lambda i, h, at=at: (0, at)) for _, at in given],
        pl.BlockSpec((1, 1, D, chunk), lambda i, h: (layer, 0, 0, first + i)),
        pl.BlockSpec((1, 1, D, chunk), lambda i, h: (layer, 0, 0, chunks + first + i)),
        pl.BlockSpec((1, 1, chunk, D), lambda i, h: (layer, 0, first + i, 0)),
    ]
    operands = [context["place"]] + [array for array, _ in given] + [joint, joint, down]
    aliases = {}
    if before is not None:
        aliases = {len(operands): 0, len(operands) + 1: 1}
        operands += list(before)
    operands.append(later_than)
    in_specs += [ANYWHERE] * (len(operands) - len(in_specs))
    return pl.pallas_call(
        expert_grad_kernel,
        grid=(steps, 2),
        in_specs=in_specs,
        out_specs=[
            pl.BlockSpec((1, 1, D, chunk), lambda i, h: (layer, 0, 0, h * chunks + first + i)),
            pl.BlockSpec((1, 1, chunk, D), lambda i, h: (layer, 0, first + i, 0)),
        ],
        out_shape=[
            jax.ShapeDtypeStruct(joint.shape, F32),
            jax.ShapeDtypeStruct(down.shape, F32),
        ],
        scratch_shapes=[
            pltpu.VMEM((2 * count, D), BF16),
            pltpu.VMEM((2 * count, D), BF16),
            pltpu.VMEM((D, 2 * count), BF16),
            pltpu.VMEM((2 * count, chunk), BF16),
        ],
        input_output_aliases=aliases,
        compiler_params=vmem(30 * count * D + 28 * D * chunk + 56 * count * chunk),
        cost_estimate=cost(12 * count * D * half, 9 * D * half, count * half),
        name="expert_grads",
    )(*operands)


def nothing(*refs):
    pass


def later(rows, *others):
    return pl.pallas_call(
        nothing,
        in_specs=[pl.BlockSpec(memory_space=pl.ANY)] * (1 + len(others)),
        out_specs=pl.BlockSpec(memory_space=pl.ANY),
        out_shape=jax.ShapeDtypeStruct(rows.shape, rows.dtype),
        input_output_aliases={0: 0},
        name="later",
    )(rows, *others)


def route_slots(route_ids):
    stretch_rows = route_ids.shape[0]
    experts_row = jnp.arange(EXPERTS, dtype=jnp.int32)
    route_hits = (route_ids[:, :, None] == experts_row[None, None, :]).astype(jnp.int32)
    running = jnp.cumsum(route_hits.reshape(2 * stretch_rows, EXPERTS), axis=0) - 1
    running = running.reshape(stretch_rows, 2, EXPERTS)
    return route_ids * SLOTS + jnp.sum(route_hits * running, axis=2)


def send_rows(outgoing, split_count):
    width = outgoing.shape[1]
    outgoing = outgoing.reshape(EXPERTS, SLOTS, width)
    if split_count > 1:
        outgoing = jnp.repeat(outgoing, split_count, axis=0)
    return exchange(outgoing, SEQ).reshape(-1, width)


def return_rows(rows, split_count):
    width = rows.shape[1]
    returned = exchange(rows.reshape(-1, SLOTS, width), SEQ)
    if split_count > 1:
        returned = (
            returned.reshape(EXPERTS, split_count, SLOTS, width).astype(F32).sum(axis=1)
        ).astype(BF16)
    return returned.reshape(EXPERTS * SLOTS, width)


def shared_kernel(forward, backward, place_ref, *refs):
    rows_refs, refs = refs[:4], refs[4:]
    if backward:
        grads_refs, refs = refs[:4], refs[4:]
    joint_ref, down_ref = refs[:2]
    outs = refs[2:]
    stretch = rows_refs[0].shape[0]
    team = jnp.concatenate([ref[...] for ref in rows_refs], axis=0)
    joint, down = joint_ref[...], down_ref[...]
    half = joint.shape[1] // 2
    pre = jnp.dot(team, joint, preferred_element_type=F32)
    gate_pre, up_pre = pre[:, :half], pre[:, half:]
    hidden = swiglu(gate_pre, up_pre)
    if forward:
        result = jnp.dot(hidden, down, preferred_element_type=F32)
        for turn in range(4):
            outs[turn][...] = result[turn * stretch : (turn + 1) * stretch].astype(BF16)
        outs = outs[4:]
    if backward:
        grads = jnp.concatenate([ref[...] for ref in grads_refs], axis=0)
        hidden_grad = contract(grads, down, 1, 1).astype(BF16).astype(F32)
        gate_grad, up_grad = swiglu_back(gate_pre, up_pre, hidden_grad)
        joint_grad = jnp.concatenate([gate_grad, up_grad], axis=1)
        result = contract(joint_grad, joint, 1, 1)
        for turn in range(4):
            outs[turn][...] = result[turn * stretch : (turn + 1) * stretch].astype(BF16)
        team_out, grads_out, hidden_out, joint_out = outs[4:]
        team_out[...] = team
        grads_out[...] = grads
        hidden_out[...] = hidden
        joint_out[...] = joint_grad


def shared_step(rows, grads, joint, down, forward, after, context):
    stretch = rows[0].shape[0]
    group = TEAM_SIZE * stretch
    backward = grads is not None
    parts = [((stretch, D), BF16)] * 4
    outputs = list(parts) if forward else []
    if backward:
        outputs += parts + [
            ((group, D), BF16),
            ((group, D), BF16),
            ((group, down.shape[0]), BF16),
            ((group, joint.shape[1]), BF16),
        ]
    return run_kernel(
        functools.partial(shared_kernel, forward, backward),
        [context["place"], *rows, *(grads if backward else []), joint, down],
        outputs,
        (),
        after,
        flops=2 * group * joint.size * (3 if backward else 1),
        name="shared",
        room=16,
    )


def z_turn(pieces, out):
    count = len(pieces)
    arrived = [pieces[0]]
    for turn in range(1, count):
        pairs = []
        for z in range(count):
            for core in range(2):
                to = (z + turn) % count
                if 0 <= (to if out else z) - core < TEAM_HEADS:
                    pairs.append((z * 2 + core, to * 2 + core))
        arrived.append(lax.ppermute(pieces[turn], ("z", "core"), pairs))
    return arrived


def to_heads(pieces, context):
    parts = context["parts"]
    if parts == 1:
        return z_turn(pieces, True)
    heads = jnp.stack([*pieces, jnp.zeros_like(pieces[0])])
    return [exchange(jnp.repeat(heads, parts, axis=0), "z")]


def attention_forward(arrived, after, context, stretch):
    parts = context["parts"]
    if parts == 1:
        rows, attended, wide, logs = fixed_attention(
            arrived, context["spans"][3], context["place"], stretch, after
        )
        return (exchange(attended, SEQ), (rows, wide, logs))
    (rows,) = arrived
    attended, wide, logs = attention(rows, context["spans"], stretch)
    count = context["deep"] * TEAM_SIZE
    attended = lax.dynamic_update_slice_in_dim(
        jnp.zeros((count, HEAD, stretch), BF16), attended, context["part"] * (count // parts), 0
    )
    back = exchange(attended, SEQ).reshape(TEAM_SIZE, parts, TEAM_SIZE, HEAD, stretch)
    back = back.astype(F32).sum(axis=1).astype(BF16)
    return (back.reshape(-1, HEAD, stretch), (rows, wide, logs))


def attention_backward(head_grads, saved, after, context):
    parts = context["parts"]
    rows, wide, logs = saved
    if parts == 1:
        grads = exchange(head_grads, SEQ)
        pieces = fixed_attention_back(
            rows, context["spans"][3], grads, wide, logs, context["place"], after
        )
        return (z_turn(pieces, False), pieces[0])
    stretch = head_grads.shape[2]
    head_grads = head_grads.reshape(TEAM_SIZE, TEAM_SIZE, HEAD, stretch)
    grads = exchange(jnp.repeat(head_grads, parts, axis=0).reshape(-1, HEAD, stretch), SEQ)
    count = grads.shape[0] // parts
    grads = lax.dynamic_slice_in_dim(grads, context["part"] * count, count, 0)
    rows_grad = attention_back(rows, context["spans"], grads, wide, logs, after)
    back = exchange(rows_grad, "z")
    back = back.reshape((TEAM_SIZE, parts) + back.shape[1:]).astype(F32).sum(axis=1).astype(BF16)
    return ([back[i] for i in range(TEAM_HEADS)], rows_grad)


def team_pieces(rows, member):
    pieces = rows.reshape(TEAM_SIZE, -1, rows.shape[1])
    parts = [lax.dynamic_index_in_dim(pieces, member ^ k, 0, keepdims=False) for k in range(4)]
    return [parts[0]] + [from_member(parts[k], k) for k in (1, 2, 3)]


def team_turn(rows, member):
    return in_order(jnp.stack(team_pieces(rows, member)), member)


def swap(rows):
    return lax.ppermute(rows, "dp", SWAP)


def beside(pairs):
    return jnp.concatenate(
        [(own.astype(F32) + other.astype(F32)).astype(BF16) for own, other in pairs], axis=1
    )


def z_sum(rows):
    return lax.psum_scatter(rows, "z", scatter_dimension=0, tiled=True)


def z_sum_direct(rows):
    count = lax.axis_size("z")
    if count > 4:
        return z_sum(rows)
    at = lax.axis_index("z")
    blocks = rows.reshape(count, -1, rows.shape[1])
    total = lax.dynamic_index_in_dim(blocks, at, 0, keepdims=False).astype(F32)
    for turn in range(1, count):
        block = lax.dynamic_index_in_dim(blocks, (at + turn) % count, 0, keepdims=False)
        block = lax.ppermute(block, "z", [(i, (i + turn) % count) for i in range(count)])
        total = total + block.astype(F32)
    return total.astype(BF16)


def to_team(parts):
    return [parts[0]] + [from_member(parts[k], k) for k in (1, 2, 3)]


def from_team(rows):
    return [rows] + [from_member(rows, k) for k in (1, 2, 3)]


def spread(rows, axes):
    count = lax.axis_size(axes)
    copies = jnp.broadcast_to(rows[None], (count,) + rows.shape)
    return exchange(copies, axes).reshape((-1,) + rows.shape[1:])


def dp_rows(rows):
    other = lax.ppermute(rows, "dp", SWAP)
    first = lax.axis_index("dp") == 0
    return jnp.concatenate([jnp.where(first, rows, other), jnp.where(first, other, rows)], axis=0)


def small_weights(gain_attn, gain_ffn, w_router):
    small = jnp.concatenate([gain_attn[:, :, None], gain_ffn[:, :, None], w_router], axis=2)
    small = small.transpose(1, 0, 2).reshape(gain_attn.shape[1], -1)
    return jnp.broadcast_to(small[None], (TEAM_SIZE,) + small.shape)


def split_small(smalls):
    weights = []
    for layer in range(LAYERS):
        part = smalls[:, layer * (2 + EXPERTS) : (layer + 1) * (2 + EXPERTS)]
        gains = part[:, :2].astype(F32).T
        weights.append(
            dict(
                gain_one=gains[0:1],
                gain_two=gains[1:2],
                router=jnp.pad(part, ((0, 0), (0, 128 - part.shape[1]))),
            )
        )
    return weights


def qkv_columns(w_qkv):
    width = w_qkv.shape[0]
    blocks = w_qkv.reshape(width, 3, TEAM_SIZE, TEAM_HEADS, HEAD)
    return blocks.transpose(2, 0, 3, 1, 4).reshape(TEAM_SIZE, width, -1)


def joint_columns(shared_gate_up):
    total = lax.axis_size(ALL)
    width = shared_gate_up.shape[0]
    blocks = shared_gate_up.reshape(width, 2, total // TEAM_SIZE, TEAM_SIZE, FF // total)
    return blocks.transpose(3, 0, 1, 2, 4).reshape(TEAM_SIZE, width, -1)


def padded_rows(shared_down):
    total = lax.axis_size(ALL)
    return jnp.pad(shared_down, ((0, TEAM_SIZE * D // total - shared_down.shape[0]), (0, 0)))


def down_rows(padded):
    total = lax.axis_size(ALL)
    return padded.reshape(total // TEAM_SIZE, -1, D)[:, : FF // total].reshape(-1, D)


def side_by_side(*arrays):
    return jnp.concatenate(arrays, axis=2)


def copies(rows):
    return jnp.broadcast_to(rows[None], (TEAM_SIZE,) + rows.shape)


def z_gather(rows):
    return lax.all_gather(rows, "z", axis=0, tiled=True)


def rest_gather(rows):
    return lax.all_gather(rows, REST, axis=0, tiled=True)


def dp_gather(rows, edges, token):
    parts = []
    for low, high in zip(edges, edges[1:]):
        token = dp_rows(later(rows[:, low:high], token))
        parts.append(token)
    return parts


def layers(
    x_in,
    cotangent,
    gain_attn,
    w_qkv,
    w_out,
    gain_ffn,
    w_router,
    shared_gate_up,
    shared_down,
    joint,
    down,
    context,
):
    split_count = context["split_count"]
    member = context["member"]
    stretch = x_in.shape[0]
    last = LAYERS - 1

    width = w_qkv.shape[1]
    qkv_width, joint_width = 3 * D // TEAM_SIZE, 2 * FF // TEAM_SIZE
    small = small_weights(gain_attn, gain_ffn, w_router)
    rows = side_by_side(qkv_columns(w_qkv[0]), small).reshape(TEAM_SIZE * width, -1)
    rows = team_turn(rows, member).reshape(TEAM_SIZE * width, -1)
    first_rows = spread(rows, "z")
    rows = side_by_side(copies(w_out[0]), joint_columns(shared_gate_up[0]))
    rows = exchange(rows, TEAM).reshape(TEAM_SIZE * width, -1)
    main_rows = jnp.concatenate([rows, padded_rows(shared_down[0])], axis=1)
    main_rows = z_gather(later(main_rows, first_rows))
    if LAYERS > 1:
        rows = side_by_side(
            *[qkv_columns(w_qkv[layer]) for layer in range(1, LAYERS)],
            *[copies(w_out[layer]) for layer in range(1, LAYERS)],
            *[joint_columns(shared_gate_up[layer]) for layer in range(1, LAYERS)],
        )
        rows = team_turn(rows.reshape(TEAM_SIZE * width, -1), member)
        rows = rows.reshape(TEAM_SIZE * width, -1)
        more_edges = [(LAYERS - 1) * qkv_width]
        for size in (D, joint_width):
            more_edges.append(more_edges[-1] + (LAYERS - 1) * size)
        more_rows = jnp.concatenate(
            [rows, *[padded_rows(shared_down[layer]) for layer in range(1, LAYERS)]], axis=1
        )
    first_rows = dp_rows(first_rows)
    weights = split_small(first_rows[:, qkv_width:])
    weights[0]["qkv"] = first_rows[:, :qkv_width]

    stream = x_in
    rows = from_team(x_in)
    grad_rows = from_team(cotangent)
    feeds = []
    for layer in range(LAYERS):
        mine = weights[layer]
        *pieces, team = qkv_step(
            rows,
            layer > 0,
            mine["gain_one"],
            mine["qkv"],
            [mine["out"]] if layer > 0 else [],
            context,
        )
        if layer == 0:
            at, held_rows, edges = 0, main_rows, [0, D, D + joint_width]
        else:
            at, held_rows, edges = layer - 1, more_rows, more_edges
        columns = [
            held_rows[:, low + at * size : low + (at + 1) * size]
            for low, size in zip(edges, (D, joint_width, D))
        ]
        after = grad_rows[1:] if layer == last else []
        back, attended = attention_forward(to_heads(pieces, context), after, context, stretch)
        if layer == 0:
            mine["out"] = dp_rows(later(columns[0], attended[1]))
        if layer == 0 and LAYERS > 1:
            more_rows = z_gather(later(more_rows, attended[1]))
        middle, normed_ffn, gates, outgoing, mixed = feed_step(
            back,
            stream,
            mine["out"],
            mine["gain_two"],
            mine["router"],
            cotangent if layer == last else None,
            [feeds[0]["other"]] if layer > 0 else [],
            context,
        )
        mine["joint"] = dp_rows(later(columns[1], attended[1] if layer > 0 else normed_ffn))
        down_padded = dp_rows(later(columns[2], attended[1] if layer > 0 else normed_ffn))
        mine["down"] = down_rows(down_padded)
        arrived = send_rows(outgoing, split_count)
        other = swap(arrived)
        ffn_rows = from_team(normed_ffn)
        returned = run_expert(
            layer,
            joint,
            down,
            (arrived, 0),
            (arrived, 1) if layer == last else None,
            True,
            [*ffn_rows[1:], mine["joint"], *([down_padded] if layer > 0 else [])],
        )
        shared = shared_step(
            ffn_rows,
            grad_rows if layer == last else None,
            mine["joint"],
            mine["down"],
            True,
            [returned],
            context,
        )
        if layer == 0:
            for i in range(1, LAYERS):
                columns = more_rows[:, (i - 1) * qkv_width : i * qkv_width]
                weights[i]["qkv"] = dp_rows(later(columns, returned))
        returned = return_rows(returned, split_count)
        feed = dict(
            stream=stream,
            team=team,
            attended=attended,
            middle=middle,
            normed_ffn=normed_ffn,
            gates=gates,
            mixed=mixed,
            arrived=arrived,
            other=other,
            ffn_rows=ffn_rows,
        )
        feeds.append(feed)
        parts = to_team(shared[:4])
        if layer < last:
            stream, feed["gap"], normed = layer_end_step(
                returned, feed, parts, weights[layer + 1]["gain_one"], [weights[layer + 1]["qkv"]], context
            )
            rows = from_team(normed)
            low = more_edges[0] + layer * D
            weights[layer + 1]["out"] = dp_rows(later(more_rows[:, low : low + D], normed))

    upstream = cotangent
    terms = None
    unit = FF // lax.axis_size(ALL)
    feed_parts, head_parts = [None] * LAYERS, [None] * LAYERS
    for layer in reversed(range(LAYERS)):
        feed, mine = feeds[layer], weights[layer]
        arrived, other = feed["arrived"], feed["other"]
        if layer == last:
            grads, other_grads = (arrived, 1), (other, 1)
            shared_parts = shared_grads(shared, context)
            output, middle_grad, attn_grad, head_grads, small = feed_back_step(
                returned,
                feed,
                upstream,
                to_team(shared[4:8]),
                parts,
                mine,
                True,
                [shared_parts[1], shared_parts[3]],
                context,
            )
        else:
            arrived_grad = send_rows(outgoing_grads, split_count)
            grads, other_grads = (arrived_grad, 0), (swap(arrived_grad), 0)
            grad_rows = from_team(upstream_rows)
            waiting = [(own, swap(rows)) for own, rows in waiting[:2]]
            returned = run_expert(
                layer,
                joint,
                down,
                (arrived, 0),
                (arrived_grad, 0),
                False,
                [*grad_rows[1:], *[rows for _, rows in waiting], terms[1]],
            )
            shared = shared_step(
                feed["ffn_rows"],
                grad_rows,
                mine["joint"],
                mine["down"],
                False,
                [returned],
                context,
            )
            waiting = [(own, later(rows, shared[0])) for own, rows in waiting]
            waiting_sum = z_sum(beside([*waiting, waited]))
            returned = return_rows(returned, split_count)
            shared_parts = shared_grads(shared, context)
            middle_grad, attn_grad, head_grads, small = feed_back_step(
                returned,
                feed,
                upstream,
                to_team(shared[:4]),
                [feed["gap"]],
                mine,
                False,
                [shared_parts[1], shared_parts[3]],
                context,
            )
        out_own, out_other = out_grads_step(feed["mixed"], attn_grad, context)
        joint_arrived, down_arrived = swap(shared_parts[1]), swap(shared_parts[3])
        out_arrived = swap(out_other)
        joint_sum = z_sum(beside([(shared_parts[0], later(joint_arrived, head_grads))]))
        pieces, token = attention_backward(
            head_grads,
            feed["attended"],
            [out_other, other_grads[0]] + ([waiting_sum] if layer < last else []),
            context,
        )
        held = ((arrived, 0), grads), ((other, 0), other_grads)
        terms = expert_grads(layer, 0, *held, joint, down, terms, token, context)
        results = qkv_back_step(
            pieces,
            mine["qkv"],
            feed["team"],
            mine["gain_one"],
            small,
            layer > 0,
            [down_arrived, terms[1], joint_sum] + ([] if layer > 0 else [out_arrived]),
            context,
        )
        normed_parts, packed = to_team(results[:4]), results[4:]
        if layer > 0:
            waiting = [packed, (out_own, out_other)]
            waited = (shared_parts[2], down_arrived)
            upstream, upstream_rows, outgoing_grads = layer_start_step(
                feed["stream"], middle_grad, mine["gain_one"], normed_parts, feeds[layer - 1], context
            )
            terms = expert_grads(layer, 1, *held, joint, down, terms, outgoing_grads, context)
        else:
            (upstream_rows,) = layer_start_step(
                feed["stream"], middle_grad, mine["gain_one"], normed_parts, None, context
            )
            total = lax.axis_size(ALL)
            first_sum = exchange(packed[0].reshape(total, D // total, -1), ALL)
            tail_sum = z_sum(
                beside(
                    [
                        (out_own, later(out_arrived, packed[0])),
                        (shared_parts[2], down_arrived),
                    ]
                )
            )
            terms = expert_grads(layer, 1, *held, joint, down, terms, packed[0], context)
        feed_parts[layer] = [
            team_pieces(joint_sum, member),
            team_pieces(tail_sum[:, :D], member) if layer == 0 else None,
            tail_sum[:unit, D:] if layer == 0 else None,
        ]
        if layer < last:
            edge = waiting_sum.shape[1] - 2 * D
            head_parts[layer + 1] = team_pieces(waiting_sum[:, :edge], member)
            feed_parts[layer + 1][1] = team_pieces(waiting_sum[:, edge : edge + D], member)
            feed_parts[layer + 1][2] = waiting_sum[:unit, edge + D :]
    joint_sum, out_sum, down_sum = run_kernel(
        feed_end_kernel,
        [
            context["place"],
            *[piece for pieces, _, _ in feed_parts for piece in pieces],
            *[piece for _, pieces, _ in feed_parts for piece in pieces],
            *[rows for _, _, rows in feed_parts],
        ],
        [
            ((LAYERS, width, 2 * FF), F32),
            ((LAYERS, width, D), F32),
            ((LAYERS, unit, D), F32),
        ],
        [((TEAM_SIZE, width, joint_width), F32)],
        name="feed_end",
    )
    qkv_sum, small_sum = run_kernel(
        qkv_end_kernel,
        [context["place"], first_sum, *[piece for pieces in head_parts[1:] for piece in pieces]],
        [((LAYERS, width, 3 * D), F32), ((LAYERS, width, 64), F32)],
        [((TEAM_SIZE, width, first_sum.shape[2]), F32)],
        name="qkv_end",
    )
    dense = (
        small_sum[:, :, 0],
        qkv_sum,
        out_sum,
        small_sum[:, :, 1],
        small_sum[:, :, 2 : 2 + EXPERTS],
        joint_sum,
        down_sum,
    )
    return (output, upstream_rows, dense, terms)


def query_spans(block_row, group, part, parts):
    length = block_row.shape[0]
    limit = jnp.sum((block_row[None, :] <= block_row[:, None]).astype(jnp.int32), axis=1)
    tiles = length // QUERY_TILE // parts
    base = part * tiles
    ends = lax.dynamic_slice_in_dim(limit.reshape(-1, QUERY_TILE), base, tiles, 0)
    full = ends[:, 0] // group
    some = (ends[:, -1] + group - 1) // group
    base = jnp.full((1,), base, jnp.int32)
    return (full, some, base, limit[None, :], tiles, parts)


def local(
    x_in,
    block_ids,
    expert_ids,
    cotangent,
    gain_attn,
    w_qkv,
    w_out,
    gain_ffn,
    w_router,
    shared_gate_up,
    shared_down,
    expert_gate_up,
    expert_down,
):
    stretch = x_in.shape[1]
    group = TEAM_SIZE * stretch
    deep = lax.axis_size("z")
    parts = max(1, deep // TEAM_SIZE)
    at = lax.axis_index("z")
    member = lax.axis_index("core") * lax.axis_size("ulysses") + lax.axis_index("ulysses")
    half_size = HEAD // 2
    spacing = 10000.0 ** (-jnp.arange(half_size).astype(F32) * 2.0 / HEAD)
    positions = (at * group + jnp.arange(group, dtype=jnp.int32)).astype(F32)
    angles = spacing[:, None] * positions[None, :]
    part = at % parts
    slots = route_slots(expert_ids[0])
    place = [member, at, lax.axis_index("core"), lax.axis_index("dp")]
    context = dict(
        member=member,
        place=jnp.stack(place).astype(jnp.int32),
        cosine=jnp.cos(angles),
        sine=jnp.sin(angles),
        ids=expert_ids[0],
        slots=slots,
        turned_slots=slots.T,
        parts=parts,
        part=part,
        deep=deep,
        split_count=deep * TEAM_SIZE // EXPERTS,
        spans=query_spans(block_ids[0], group, part, parts),
    )
    output, grad_x, dense, terms = layers(
        x_in[0],
        cotangent[0],
        gain_attn,
        w_qkv,
        w_out,
        gain_ffn,
        w_router,
        shared_gate_up,
        shared_down,
        expert_gate_up,
        expert_down,
        context,
    )
    return (output[None], grad_x[None], *dense, *terms)


def solution(mesh):
    dp, blk, ulysses = mesh.devices.shape
    grid = Mesh(mesh.devices.reshape(dp, blk // 2, 2, ulysses), ALL)
    rows = P("dp", SEQ, None)
    in_specs = (
        rows,
        P("dp", None),
        rows,
        rows,
        P(None, ALL),
        P(None, ALL, None),
        P(None, ALL, None),
        P(None, ALL),
        P(None, ALL, None),
        P(None, ALL, None),
        P(None, ALL, None),
        P(None, SEQ, None, None),
        P(None, SEQ, None, None),
    )
    out_specs = (
        rows,
        rows,
        P(None, ALL),
        P(None, ALL, None),
        P(None, ALL, None),
        P(None, ALL),
        P(None, ALL, None),
        P(None, ALL, None),
        P(None, ALL, None),
        P(None, SEQ, None, None),
        P(None, SEQ, None, None),
    )
    return jax.shard_map(local, mesh=grid, in_specs=in_specs, out_specs=out_specs, check_vma=False)
```

```python
import functools
import math

import jax
import jax.numpy as jnp
from jax import lax
from jax.experimental import pallas as pl
from jax.experimental.pallas import tpu as pltpu
from jax.sharding import Mesh
from jax.sharding import PartitionSpec as P

D = 768
HEADS = 12
HEAD = 64
FF = 2048
EXPERTS = 16
LAYERS = 2
MOST = 21
SLOTS = -(-MOST // 8) * 8
TEAM_SIZE = 4
TEAM_HEADS = HEADS // TEAM_SIZE

ALL = ("dp", "z", "core", "ulysses")
SEQ = ("z", "core", "ulysses")
TEAM = ("core", "ulysses")
REST = ("dp", "z")

NORM_EPS = 1e-06
NEG_BIG = -1e30
PRECISE = lax.Precision.HIGHEST
F32 = jnp.float32
BF16 = jnp.bfloat16
QUERY_TILE = 256
MIB = 1024 * 1024


def vmem(size):
    return pltpu.CompilerParams(vmem_limit_bytes=61 * MIB)


def cost(flops, moved, steps=0):
    return pl.CostEstimate(flops=flops, bytes_accessed=moved, transcendentals=steps)


def contract(left, right, left_dim, right_dim):
    return lax.dot_general(
        left, right, (((left_dim,), (right_dim,)), ((), ())), preferred_element_type=F32
    )


def exchange(rows, axes):
    return lax.all_to_all(rows, axes, split_axis=0, concat_axis=0, tiled=True)


SWAP = [(0, 1), (1, 0)]


def from_member(rows, turn):
    if turn == 1:
        return lax.ppermute(rows, "ulysses", SWAP)
    if turn == 2:
        return lax.ppermute(rows, "core", SWAP)
    return lax.ppermute(rows, TEAM, [(i, 3 - i) for i in range(4)])


def team_gather(rows):
    return jnp.stack([rows] + [from_member(rows, turn) for turn in (1, 2, 3)])


def in_order(stacked, member):
    turns = [jnp.equal(member, i) for i in range(4)]
    pieces = []
    for k in range(4):
        piece = stacked[k ^ 3]
        for i in range(3):
            piece = jnp.where(turns[i], stacked[k ^ i], piece)
        pieces.append(piece)
    return jnp.stack(pieces)


def team_sum(parts):
    total = parts[0].astype(F32)
    for turn in (1, 2, 3):
        total = total + from_member(parts[turn].astype(BF16), turn).astype(F32)
    return total


def rms_factor(stream):
    return lax.rsqrt(jnp.mean(stream * stream, axis=-1, keepdims=True) + NORM_EPS)


def norm_back(stream, gain, factor, upstream):
    weighted = upstream * gain
    inner_mean = jnp.mean(weighted * stream, axis=-1, keepdims=True)
    grad_stream = factor * weighted - stream * factor * factor * factor * inner_mean
    grad_gain = jnp.sum(upstream * stream * factor, axis=0)
    return (grad_stream, grad_gain)


def attention_kernel(full_ref, some_ref, base_ref, rows_ref, limit_ref, out_ref, wide_ref, log_ref, keys):
    span = rows_ref.shape[2]
    step = pl.program_id(0)
    per_block = span // QUERY_TILE

    @pl.when(step == 0)
    def _():
        for s in range(rows_ref.shape[0]):
            keys[s] = rows_ref[s, HEAD : 2 * HEAD, :].T

    tile = base_ref[0] + step
    lanes = pl.ds(pl.multiple_of((tile % per_block) * QUERY_TILE, QUERY_TILE), QUERY_TILE)
    queries = rows_ref[tile // per_block, 0:HEAD, lanes] * BF16(HEAD**-0.5)
    limit = limit_ref[...]
    key_index = lax.broadcasted_iota(jnp.int32, (span, QUERY_TILE), 0)

    def sweep(s, state, masked):
        highest, total, running = state
        scores = jnp.dot(keys[s], queries, preferred_element_type=F32)
        if masked:
            scores = jnp.where(key_index < limit - s * span, scores, NEG_BIG)
        raised = jnp.maximum(highest, jnp.max(scores, axis=0, keepdims=True))
        terms = jnp.exp(scores - raised)
        shrink = jnp.exp(highest - raised)
        total = total * shrink + jnp.sum(terms, axis=0, keepdims=True)
        running = running * shrink + jnp.dot(
            rows_ref[s, 2 * HEAD :, :], terms.astype(BF16), preferred_element_type=F32
        )
        return (raised, total, running)

    state = (
        jnp.full((1, QUERY_TILE), NEG_BIG, F32),
        jnp.zeros((1, QUERY_TILE), F32),
        jnp.zeros((HEAD, QUERY_TILE), F32),
    )
    state = lax.fori_loop(0, full_ref[step], lambda s, c: sweep(s, c, False), state)
    state = lax.fori_loop(full_ref[step], some_ref[step], lambda s, c: sweep(s, c, True), state)
    highest, total, running = state
    result = running / total
    log_ref[...] = highest + jnp.log(total)
    wide_ref[...] = result
    stretch = out_ref.shape[2]
    for i in range(QUERY_TILE // stretch):
        out_ref[i] = result[:, i * stretch : (i + 1) * stretch].astype(BF16)


def attention_back_kernel(
    full_ref, some_ref, base_ref, rows_ref, limit_ref, grad_ref, wide_ref, log_ref, *refs
):
    out_ref, keys, values, key_sum, value_sum = refs[-5:]
    span = rows_ref.shape[2]
    blocks = rows_ref.shape[0]
    step = pl.program_id(0)
    per_block = span // QUERY_TILE

    @pl.when(step == 0)
    def _():
        for s in range(blocks):
            keys[s] = rows_ref[s, HEAD : 2 * HEAD, :].T
            values[s] = rows_ref[s, 2 * HEAD :, :].T
        key_sum[...] = jnp.zeros_like(key_sum)
        value_sum[...] = jnp.zeros_like(value_sum)
        out_ref[...] = jnp.zeros_like(out_ref)

    tile = base_ref[0] + step
    lanes = pl.ds(pl.multiple_of((tile % per_block) * QUERY_TILE, QUERY_TILE), QUERY_TILE)
    queries = rows_ref[tile // per_block, 0:HEAD, lanes] * BF16(HEAD**-0.5)
    limit = limit_ref[...]
    key_index = lax.broadcasted_iota(jnp.int32, (span, QUERY_TILE), 0)
    grads = jnp.concatenate([grad_ref[i] for i in range(grad_ref.shape[0])], axis=1)
    delta = jnp.sum(grads.astype(F32) * wide_ref[...], axis=0, keepdims=True)
    logs = log_ref[...]

    def sweep(s, query_grad, masked):
        scores = jnp.dot(keys[s], queries, preferred_element_type=F32)
        probs = jnp.exp(scores - logs)
        if masked:
            probs = jnp.where(key_index < limit - s * span, probs, 0.0)
        prob_grad = jnp.dot(values[s], grads, preferred_element_type=F32)
        score_grad = (probs * (prob_grad - delta)).astype(BF16)
        value_sum[s] += contract(grads, probs.astype(BF16), 1, 1)
        key_sum[s] += contract(queries, score_grad, 1, 1)
        return query_grad + jnp.dot(
            rows_ref[s, HEAD : 2 * HEAD, :], score_grad, preferred_element_type=F32
        )

    query_grad = jnp.zeros((HEAD, QUERY_TILE), F32)
    query_grad = lax.fori_loop(0, full_ref[step], lambda s, c: sweep(s, c, False), query_grad)
    query_grad = lax.fori_loop(
        full_ref[step], some_ref[step], lambda s, c: sweep(s, c, True), query_grad
    )
    out_ref[tile // per_block, 0:HEAD, lanes] = (query_grad * HEAD**-0.5).astype(BF16)

    @pl.when(step == pl.num_programs(0) - 1)
    def _():
        out_ref[:, HEAD : 2 * HEAD, :] = key_sum[...].astype(BF16)
        out_ref[:, 2 * HEAD :, :] = value_sum[...].astype(BF16)


def fixed_attention_kernel(place_ref, *refs):
    rows_ref, out_ref, wide_ref, log_ref, keys, values = refs[-6:]
    blocks, _, span = rows_ref.shape
    pieces, limit_ref = refs[:blocks], refs[blocks]
    for turn in range(blocks):
        rows_ref[lax.rem(place_ref[1] + blocks - turn, blocks)] = pieces[turn][...]
    length = blocks * span
    stretch = out_ref.shape[2]
    for s in range(blocks):
        keys[s * span : (s + 1) * span, :] = rows_ref[s, HEAD : 2 * HEAD, :].T
        values[:, s * span : (s + 1) * span] = rows_ref[s, 2 * HEAD :, :]
    key_index = lax.broadcasted_iota(jnp.int32, (2 * QUERY_TILE, QUERY_TILE), 0)
    for tile in range(length // QUERY_TILE):
        start = tile * QUERY_TILE
        end = min(start + 2 * QUERY_TILE, length)
        lanes = slice(start % span, start % span + QUERY_TILE)
        queries = rows_ref[start // span, 0:HEAD, lanes] * BF16(HEAD**-0.5)
        scores = jnp.dot(keys[start:end, :], queries, preferred_element_type=F32)
        limit = limit_ref[:, start : start + QUERY_TILE] - start
        scores = jnp.where(key_index[: end - start] < limit, scores, NEG_BIG)
        highest = jnp.max(scores, axis=0, keepdims=True)
        if start > 0:
            before = jnp.dot(keys[:start, :], queries, preferred_element_type=F32)
            highest = jnp.maximum(highest, jnp.max(before, axis=0, keepdims=True))
        terms = jnp.exp(scores - highest)
        total = jnp.sum(terms, axis=0, keepdims=True)
        result = jnp.dot(values[:, start:end], terms.astype(BF16), preferred_element_type=F32)
        if start > 0:
            terms = jnp.exp(before - highest)
            total = total + jnp.sum(terms, axis=0, keepdims=True)
            result = result + jnp.dot(
                values[:, :start], terms.astype(BF16), preferred_element_type=F32
            )
        result = result / total
        log_ref[:, start : start + QUERY_TILE] = highest + jnp.log(total)
        wide_ref[:, start : start + QUERY_TILE] = result
        for i in range(QUERY_TILE // stretch):
            out_ref[start // stretch + i] = result[:, i * stretch : (i + 1) * stretch].astype(BF16)


def fixed_attention_back_kernel(place_ref, rows_ref, limit_ref, grad_ref, wide_ref, log_ref, *refs):
    blocks, _, span = rows_ref.shape
    out_ref, keys, values, key_sum, value_sum = refs[-5:]
    outs = refs[-5 - blocks : -5]
    length = blocks * span
    stretch = grad_ref.shape[2]
    for s in range(blocks):
        keys[s * span : (s + 1) * span, :] = rows_ref[s, HEAD : 2 * HEAD, :].T
        values[s * span : (s + 1) * span, :] = rows_ref[s, 2 * HEAD :, :].T
    key_sum[...] = jnp.zeros_like(key_sum)
    value_sum[...] = jnp.zeros_like(value_sum)
    key_index = lax.broadcasted_iota(jnp.int32, (2 * QUERY_TILE, QUERY_TILE), 0)
    for tile in range(length // QUERY_TILE):
        start = tile * QUERY_TILE
        end = min(start + 2 * QUERY_TILE, length)
        lanes = slice(start % span, start % span + QUERY_TILE)
        queries = rows_ref[start // span, 0:HEAD, lanes] * BF16(HEAD**-0.5)
        pieces = QUERY_TILE // stretch
        grads = jnp.concatenate([grad_ref[tile * pieces + i] for i in range(pieces)], axis=1)
        wide = wide_ref[:, start : start + QUERY_TILE]
        delta = jnp.sum(grads.astype(F32) * wide, axis=0, keepdims=True)
        logs = log_ref[:, start : start + QUERY_TILE]
        limit = limit_ref[:, start : start + QUERY_TILE] - start
        query_grad = jnp.zeros((HEAD, QUERY_TILE), F32)
        for low, high in ((0, start), (start, end)):
            if low == high:
                continue
            scores = jnp.dot(keys[low:high, :], queries, preferred_element_type=F32)
            probs = jnp.exp(scores - logs)
            if low == start:
                probs = jnp.where(key_index[: high - low] < limit, probs, 0.0)
            prob_grad = jnp.dot(values[low:high, :], grads, preferred_element_type=F32)
            score_grad = (probs * (prob_grad - delta)).astype(BF16)
            value_sum[:, low:high] += contract(grads, probs.astype(BF16), 1, 1)
            key_sum[:, low:high] += contract(queries, score_grad, 1, 1)
            query_grad = query_grad + contract(keys[low:high, :], score_grad, 0, 0)
        out_ref[start // span, 0:HEAD, lanes] = (query_grad * HEAD**-0.5).astype(BF16)
    for s in range(blocks):
        out_ref[s, HEAD : 2 * HEAD, :] = key_sum[:, s * span : (s + 1) * span].astype(BF16)
        out_ref[s, 2 * HEAD :, :] = value_sum[:, s * span : (s + 1) * span].astype(BF16)
    for turn in range(blocks):
        outs[turn][...] = out_ref[lax.rem(place_ref[1] + turn, blocks)]


def at_once(shape):
    return pl.BlockSpec(shape, lambda step: (0,) * len(shape))


ANYWHERE = pl.BlockSpec(memory_space=pl.ANY)
IN_SMEM = pl.BlockSpec(memory_space=pltpu.SMEM)


def fixed_attention(pieces, limit, place, stretch, after):
    blocks = len(pieces)
    features, span = pieces[0].shape
    length = blocks * span
    return pl.pallas_call(
        fixed_attention_kernel,
        grid=(1,),
        in_specs=[IN_SMEM, *[at_once(array.shape) for array in (*pieces, limit)]]
        + [ANYWHERE] * len(after),
        out_specs=[
            at_once((blocks, features, span)),
            at_once((length // stretch, HEAD, stretch)),
            at_once((HEAD, length)),
            at_once((1, length)),
        ],
        out_shape=[
            jax.ShapeDtypeStruct((blocks, features, span), BF16),
            jax.ShapeDtypeStruct((length // stretch, HEAD, stretch), BF16),
            jax.ShapeDtypeStruct((HEAD, length), F32),
            jax.ShapeDtypeStruct((1, length), F32),
        ],
        scratch_shapes=[pltpu.VMEM((length, HEAD), BF16), pltpu.VMEM((HEAD, length), BF16)],
        compiler_params=vmem(16 * MIB),
        cost_estimate=cost(features * length * length // 48, features * length * 4, length * length),
        name="attend",
    )(place, *pieces, limit, *after)


def fixed_attention_back(rows, limit, grads, wide, logs, place, later_than):
    blocks, features, span = rows.shape
    length = blocks * span
    return pl.pallas_call(
        fixed_attention_back_kernel,
        grid=(1,),
        in_specs=[
            IN_SMEM,
            *[at_once(array.shape) for array in (rows, limit, grads, wide, logs)],
        ]
        + [ANYWHERE] * len(later_than),
        out_specs=[at_once((features, span))] * blocks,
        out_shape=[jax.ShapeDtypeStruct((features, span), BF16)] * blocks,
        scratch_shapes=[
            pltpu.VMEM(rows.shape, BF16),
            pltpu.VMEM((length, HEAD), BF16),
            pltpu.VMEM((length, HEAD), BF16),
            pltpu.VMEM((HEAD, length), F32),
            pltpu.VMEM((HEAD, length), F32),
        ],
        compiler_params=vmem(20 * MIB),
        cost_estimate=cost(rows.size * length // 16, rows.size * 4, length * length),
        name="attend_back",
    )(place, rows, limit, grads, wide, logs, *later_than)


def whole(shape):
    return pl.BlockSpec(shape, lambda step, *_: (0,) * len(shape))


def tile_at(step, full, some, base):
    return (0, base[0] + step)


def attention(rows, spans, stretch):
    full, some, base, limit, tiles, parts = spans
    blocks, _, span = rows.shape
    length = tiles * QUERY_TILE
    return pl.pallas_call(
        attention_kernel,
        grid_spec=pltpu.PrefetchScalarGridSpec(
            num_scalar_prefetch=3,
            grid=(tiles,),
            in_specs=[whole(rows.shape), pl.BlockSpec((1, QUERY_TILE), tile_at)],
            out_specs=[
                pl.BlockSpec((QUERY_TILE // stretch, HEAD, stretch), lambda step, *_: (step, 0, 0)),
                pl.BlockSpec((HEAD, QUERY_TILE), lambda step, *_: (0, step)),
                pl.BlockSpec((1, QUERY_TILE), lambda step, *_: (0, step)),
            ],
            scratch_shapes=[pltpu.VMEM((blocks, span, HEAD), BF16)],
        ),
        out_shape=[
            jax.ShapeDtypeStruct((length // stretch, HEAD, stretch), BF16),
            jax.ShapeDtypeStruct((HEAD, length), F32),
            jax.ShapeDtypeStruct((1, length), F32),
        ],
        compiler_params=vmem(52 * MIB),
        cost_estimate=cost(rows.size * length // 48, rows.size * 4, length * length),
        name="attend",
    )(full, some, base, rows, limit)


def attention_back(rows, spans, grads, wide, logs, later_than):
    full, some, base, limit, tiles, parts = spans
    blocks, _, span = rows.shape
    stretch = grads.shape[2]
    return pl.pallas_call(
        attention_back_kernel,
        grid_spec=pltpu.PrefetchScalarGridSpec(
            num_scalar_prefetch=3,
            grid=(tiles,),
            in_specs=[
                whole(rows.shape),
                pl.BlockSpec((1, QUERY_TILE), tile_at),
                pl.BlockSpec((QUERY_TILE // stretch, HEAD, stretch), lambda step, *_: (step, 0, 0)),
                pl.BlockSpec((HEAD, QUERY_TILE), lambda step, *_: (0, step)),
                pl.BlockSpec((1, QUERY_TILE), lambda step, *_: (0, step)),
                *[pl.BlockSpec(memory_space=pl.ANY)] * len(later_than),
            ],
            out_specs=whole(rows.shape),
            scratch_shapes=[
                pltpu.VMEM((blocks, span, HEAD), BF16),
                pltpu.VMEM((blocks, span, HEAD), BF16),
                pltpu.VMEM((blocks, HEAD, span), F32),
                pltpu.VMEM((blocks, HEAD, span), F32),
            ],
        ),
        out_shape=jax.ShapeDtypeStruct(rows.shape, BF16),
        compiler_params=vmem(52 * MIB),
        cost_estimate=cost(rows.size * tiles * QUERY_TILE // 16, rows.size * 4, rows.size),
        name="attend_back",
    )(full, some, base, rows, limit, grads, wide, logs, *later_than)


def run_kernel(kernel, operands, outputs, scratch=(), after=(), flops=0, name=None, room=6):
    moved = sum(array.size * array.dtype.itemsize for array in operands)
    size = 2 * moved
    for times, arrays in ((2, outputs), (1, scratch)):
        for shape, dtype in arrays:
            size += times * math.prod(shape) * jnp.dtype(dtype).itemsize
    given, kept = len(operands), len(operands) + len(after)
    return pl.pallas_call(
        lambda *refs: kernel(*refs[:given], *refs[kept:]),
        grid=(1,),
        in_specs=[IN_SMEM, *[at_once(array.shape) for array in operands[1:]]]
        + [ANYWHERE] * len(after),
        out_specs=[at_once(shape) for shape, _ in outputs],
        out_shape=[jax.ShapeDtypeStruct(shape, dtype) for shape, dtype in outputs],
        scratch_shapes=[pltpu.VMEM(shape, dtype) for shape, dtype in scratch],
        compiler_params=vmem(room * MIB + size),
        cost_estimate=cost(flops, moved),
        name=name,
    )(*operands, *after)


def rows_at(index, size):
    return pl.ds(pl.multiple_of(index * size, size), size)


def qkv_kernel(fixed, normed, place_ref, *refs):
    rows_refs, (gain_ref, weight_ref, cosine_ref, sine_ref) = refs[:4], refs[4:8]
    pieces, team, heads = refs[8:-2], refs[-2], refs[-1]
    member = place_ref[0]
    stretch = rows_refs[0].shape[0]
    half = HEAD // 2
    for turn in range(4):
        rows = rows_refs[turn][...]
        if not normed:
            wide = rows.astype(F32)
            rows = (wide * rms_factor(wide) * gain_ref[...]).astype(BF16)
        team[rows_at(member ^ turn, stretch), :] = rows
    projected = contract(weight_ref[...], team[...], 0, 1)
    cosine, sine = cosine_ref[...], sine_ref[...]
    for head in range(TEAM_HEADS):
        for part in range(3):
            at = (head * 3 + part) * HEAD
            first, second = projected[at : at + half], projected[at + half : at + HEAD]
            if part < 2:
                first, second = (
                    first * cosine - second * sine,
                    second * cosine + first * sine,
                )
            heads[head, part * HEAD : part * HEAD + half] = first.astype(BF16)
            heads[head, part * HEAD + half : (part + 1) * HEAD] = second.astype(BF16)
    for turn, piece in enumerate(pieces):
        head = turn
        if fixed:
            head = lax.rem(place_ref[1] + turn, len(pieces)) - place_ref[2]
            head = jnp.clip(head, 0, TEAM_HEADS - 1)
        piece[...] = heads[head]


def qkv_step(rows, normed, gain, weight, after, context):
    group = TEAM_SIZE * rows[0].shape[0]
    fixed = context["parts"] == 1
    return run_kernel(
        functools.partial(qkv_kernel, fixed, normed),
        [context["place"], *rows, gain, weight, context["cosine"], context["sine"]],
        [((3 * HEAD, group), BF16)] * (context["deep"] if fixed else TEAM_HEADS)
        + [((group, D), BF16)],
        [((TEAM_HEADS, 3 * HEAD, group), BF16)],
        after,
        flops=2 * group * D * weight.shape[1],
        name="qkv",
    )


def qkv_back_kernel(fixed, halves, place_ref, *refs):
    count = len(refs) - (16 if halves else 15)
    grads, refs = refs[:count], refs[count:]
    weight_ref, cosine_ref, sine_ref, team_ref, gain_ref, small_ref = refs[:6]
    outs, (stacked, turned, parts, packed) = refs[6:-4], refs[-4:]
    half = HEAD // 2
    stretch = outs[0].shape[0]
    for turn in range(count):
        stacked[turn] = grads[turn][...]
    cosine, sine = cosine_ref[...], sine_ref[...]
    for head in range(TEAM_HEADS):
        at = head
        if fixed:
            at = lax.rem(place_ref[1] - head - place_ref[2] + 2 * count, count)
        rows = stacked[at].astype(F32)
        for part in range(3):
            low = part * HEAD
            first, second = rows[low : low + half], rows[low + half : low + HEAD]
            if part < 2:
                first, second = (
                    first * cosine + second * sine,
                    second * cosine - first * sine,
                )
            low += head * 3 * HEAD
            turned[low : low + half] = first.astype(BF16)
            turned[low + half : low + HEAD] = second.astype(BF16)
    projected_grad = turned[...].T
    normed_grad = contract(projected_grad, weight_ref[...], 1, 1)
    parts[...] = normed_grad.astype(BF16)
    for turn in range(4):
        outs[turn][...] = parts[rows_at(place_ref[0] ^ turn, stretch), :]
    team = team_ref[...]
    edge = projected_grad.shape[1]
    packed[:, :edge] = contract(team, projected_grad, 0, 0).astype(BF16)
    gain_grad = jnp.sum(normed_grad * team.astype(F32), axis=0, keepdims=True) / gain_ref[...]
    small = small_ref[...]
    lane = lax.broadcasted_iota(jnp.int32, small.shape, 1)
    small = jnp.where(lane == 0, jnp.broadcast_to(gain_grad, (128, D)).T, small)
    packed[:, edge:] = small[:, : packed.shape[1] - edge].astype(BF16)
    if halves:
        outs[4][...] = packed[rows_at(place_ref[3], D // 2), :]
        outs[5][...] = packed[rows_at(1 - place_ref[3], D // 2), :]
    else:
        outs[4][...] = packed[...]


def qkv_back_step(grads, weight, team, gain, small, halves, after, context):
    group = team.shape[0]
    width = weight.shape[1] + 64
    packed = [((D // 2, width), BF16)] * 2 if halves else [((D, width), BF16)]
    return run_kernel(
        functools.partial(qkv_back_kernel, context["parts"] == 1, halves),
        [
            context["place"],
            *grads,
            weight,
            context["cosine"],
            context["sine"],
            team,
            gain,
            small,
        ],
        [((group // TEAM_SIZE, D), BF16)] * TEAM_SIZE + packed,
        [
            ((len(grads), 3 * HEAD, group), BF16),
            ((weight.shape[1], group), BF16),
            ((group, D), BF16),
            ((D, width), BF16),
        ],
        after,
        flops=4 * group * D * weight.shape[1],
        name="qkv_back",
    )


def head_slot(head, fixed):
    member = head // TEAM_HEADS
    return (head % TEAM_HEADS + (member // 2 if fixed else 0)) * TEAM_SIZE + member


def chosen(ids_ref, choice):
    ids = ids_ref[:, choice : choice + 1]
    return lax.broadcasted_iota(jnp.int32, (ids.shape[0], 128), 1) == ids + 2


def row_table(slots_ref, choice):
    slots = slots_ref[:, choice : choice + 1]
    index = lax.broadcasted_iota(jnp.int32, (slots.shape[0], EXPERTS * SLOTS), 1)
    return jnp.where(index == slots, 1.0, 0.0).astype(BF16)


def slot_table(turned_ref, choice):
    slots = turned_ref[choice : choice + 1, :]
    index = lax.broadcasted_iota(jnp.int32, (EXPERTS * SLOTS, slots.shape[1]), 0)
    return jnp.where(index == slots, 1.0, 0.0).astype(BF16)


def slots_of_grads(turned_ref, gates, upstream):
    terms = [
        jnp.dot(
            slot_table(turned_ref, c),
            (gates[:, c : c + 1] * upstream).astype(BF16),
            preferred_element_type=F32,
        )
        for c in range(2)
    ]
    return (terms[0] + terms[1]).astype(BF16)


def feed_kernel(fixed, last, place_ref, *refs):
    back_ref, stream_ref, weight_ref, gain_ref, router_ref, ids_ref, turned_ref = refs[:7]
    middle_ref, normed_ref, gates_ref, out_ref, mixed_ref = refs[-5:]
    for head in range(HEADS):
        mixed_ref[head * HEAD : (head + 1) * HEAD, :] = back_ref[head_slot(head, fixed)]
    middle = stream_ref[...].astype(F32) + contract(mixed_ref[...], weight_ref[...], 0, 0)
    normed = (middle * rms_factor(middle) * gain_ref[...]).astype(BF16)
    middle_ref[...] = middle
    normed_ref[...] = normed
    table = slot_table(turned_ref, 0) + slot_table(turned_ref, 1)
    out_ref[:, :D] = jnp.dot(table, normed, preferred_element_type=F32).astype(BF16)
    logits = jnp.dot(normed, router_ref[...], preferred_element_type=F32)
    picked = [
        jnp.sum(jnp.where(chosen(ids_ref, c), logits, 0.0), axis=1, keepdims=True)
        for c in range(2)
    ]
    highest = jnp.maximum(picked[0], picked[1])
    powers = [jnp.exp(pick - highest) for pick in picked]
    total = powers[0] + powers[1]
    gates = jnp.concatenate([powers[0] / total, powers[1] / total], axis=1)
    gates_ref[...] = gates
    if last:
        out_ref[:, D:] = slots_of_grads(turned_ref, gates, refs[7][...].astype(F32))


def feed_step(back, stream, out_weight, gain, router, upstream, after, context):
    stretch = stream.shape[0]
    last = upstream is not None
    operands = [
        context["place"],
        back,
        stream,
        out_weight,
        gain,
        router,
        context["ids"],
        context["turned_slots"],
    ]
    return run_kernel(
        functools.partial(feed_kernel, context["parts"] == 1, last),
        operands + ([upstream] if last else []),
        [
            ((stretch, D), F32),
            ((stretch, D), BF16),
            ((stretch, 2), F32),
            ((EXPERTS * SLOTS, 2 * D if last else D), BF16),
            ((D, stretch), BF16),
        ],
        (),
        after,
        flops=4 * stretch * D * D,
        name="feed",
    )


def add_up(parts):
    total = parts[0][...].astype(F32)
    for part in parts[1:]:
        total = total + part[...].astype(F32)
    return total


def layer_end_kernel(place_ref, *refs):
    returned_ref, middle_ref, gates_ref, slots_ref, gain_ref = refs[:5]
    parts = refs[5:9]
    stream_ref, gap_ref, normed_ref = refs[-3:]
    choices = [
        jnp.dot(row_table(slots_ref, c), returned_ref[...], preferred_element_type=F32)
        for c in range(2)
    ]
    gates = gates_ref[...]
    stream = middle_ref[...] + add_up(parts) + gates[:, 0:1] * choices[0]
    stream = stream + gates[:, 1:2] * choices[1]
    stream_ref[...] = stream
    gap_ref[...] = choices[0] - choices[1]
    normed_ref[...] = (stream * rms_factor(stream) * gain_ref[...]).astype(BF16)


def layer_end_step(returned, feed, parts, next_gain, after, context):
    shape = feed["middle"].shape
    return run_kernel(
        layer_end_kernel,
        [
            context["place"],
            returned,
            feed["middle"],
            feed["gates"],
            context["slots"],
            next_gain,
            *parts,
        ],
        [(shape, F32), (shape, F32), (shape, BF16)],
        (),
        after,
        flops=4 * shape[0] * D * returned.shape[0],
        name="layer_end",
    )


def feed_back_kernel(fixed, last, place_ref, *refs):
    (
        returned_ref,
        middle_ref,
        normed_ref,
        gates_ref,
        slots_ref,
        ids_ref,
        upstream_ref,
        gain_ref,
        router_ref,
        weight_ref,
    ) = refs[:10]
    parts = refs[10:14]
    outs = refs[-4:]
    tables = [row_table(slots_ref, c) for c in range(2)]
    gates = gates_ref[...]
    middle = middle_ref[...]
    upstream = upstream_ref[...].astype(F32)
    if last:
        choices = [
            jnp.dot(table, returned_ref[:, :D], preferred_element_type=F32) for table in tables
        ]
        gap = choices[0] - choices[1]
        sums = add_up(parts)
        output = middle + sums[:, :D] + gates[:, 0:1] * choices[0]
        refs[-5][...] = (output + gates[:, 1:2] * choices[1]).astype(BF16)
        grad_rows, shared_grad = returned_ref[:, D:], sums[:, D:]
    else:
        gap = refs[14][...]
        grad_rows, shared_grad = returned_ref[...], add_up(parts)
    lead = gates[:, 0:1] * gates[:, 1:2] * jnp.sum(gap * upstream, axis=1, keepdims=True)
    logit_grad = jnp.where(chosen(ids_ref, 0), lead, 0.0) - jnp.where(
        chosen(ids_ref, 1), lead, 0.0
    )
    high = logit_grad.astype(BF16)
    low = (logit_grad - high.astype(F32)).astype(BF16)
    router = router_ref[...]
    normed_grad = (
        shared_grad
        + contract(high, router, 1, 1)
        + contract(low, router, 1, 1)
        + jnp.dot(tables[0] + tables[1], grad_rows, preferred_element_type=F32)
    )
    factor = rms_factor(middle)
    norm_grad, _ = norm_back(middle, gain_ref[...], factor, normed_grad)
    middle_grad = upstream + norm_grad
    attn_grad = middle_grad.astype(BF16)
    middle_grad_ref, attn_ref, heads_ref, small_ref = outs
    middle_grad_ref[...] = middle_grad
    attn_ref[...] = attn_grad
    mixed_grad = contract(weight_ref[...], attn_grad, 1, 1).astype(BF16)
    used = set()
    for head in range(HEADS):
        slot = head_slot(head, fixed)
        used.add(slot)
        heads_ref[slot] = mixed_grad[head * HEAD : (head + 1) * HEAD]
    for slot in range(heads_ref.shape[0]):
        if slot not in used:
            heads_ref[slot] = jnp.zeros_like(heads_ref[slot])
    gain_grad = jnp.sum(normed_grad * middle * factor, axis=0, keepdims=True)
    normed = normed_ref[...]
    small = contract(normed, high, 0, 0) + contract(normed, low, 0, 0)
    lane = lax.broadcasted_iota(jnp.int32, small.shape, 1)
    small_ref[...] = jnp.where(lane == 1, jnp.broadcast_to(gain_grad, (128, D)).T, small)


def feed_back_step(returned, feed, upstream, parts, others, weights, last, after, context):
    stretch = feed["middle"].shape[0]
    shape = (stretch, D)
    return run_kernel(
        functools.partial(feed_back_kernel, context["parts"] == 1, last),
        [
            context["place"],
            returned,
            feed["middle"],
            feed["normed_ffn"],
            feed["gates"],
            context["slots"],
            context["ids"],
            upstream,
            weights["gain_two"],
            weights["router"],
            weights["out"],
            *parts,
            *others,
        ],
        ([(shape, BF16)] if last else [])
        + [
            (shape, F32),
            (shape, BF16),
            ((TEAM_SIZE * TEAM_SIZE, HEAD, stretch), BF16),
            ((D, 128), F32),
        ],
        (),
        after,
        flops=4 * stretch * D * D,
        name="feed_back",
    )


def layer_start_kernel(more, place_ref, *refs):
    stream_ref, middle_grad_ref, gain_ref = refs[:3]
    parts = refs[3:7]
    stream = stream_ref[...].astype(F32)
    norm_grad, _ = norm_back(stream, gain_ref[...], rms_factor(stream), add_up(parts))
    upstream = middle_grad_ref[...] + norm_grad
    if more:
        gates_ref, turned_ref, wide_ref, out_ref = refs[7:9] + refs[-3:-2] + refs[-1:]
        wide_ref[...] = upstream
        refs[-2][...] = upstream.astype(BF16)
        out_ref[...] = slots_of_grads(turned_ref, gates_ref[...], upstream)
    else:
        refs[-1][...] = upstream.astype(BF16)


def layer_start_step(stream, middle_grad, gain, parts, feed, context):
    shape = stream.shape
    more = feed is not None
    return run_kernel(
        functools.partial(layer_start_kernel, more),
        [
            context["place"],
            stream,
            middle_grad,
            gain,
            *parts,
            *([feed["gates"], context["turned_slots"]] if more else []),
        ],
        [(shape, F32), (shape, BF16), ((EXPERTS * SLOTS, D), BF16)] if more else [(shape, BF16)],
        flops=4 * shape[0] * D * EXPERTS * SLOTS if more else 0,
        name="layer_start",
    )


def shared_grads_kernel(unit, place_ref, *refs):
    team_ref, joint_ref, hidden_ref, grads_ref = refs[:4]
    joint_outs, down_outs = refs[4:6], refs[6:8]
    half = D // 2
    units = hidden_ref.shape[1] // 2
    for place, dp in enumerate((place_ref[3], 1 - place_ref[3])):
        joint_outs[place][...] = contract(
            team_ref[:, rows_at(dp, half)], joint_ref[...], 0, 0
        ).astype(BF16)
        down = contract(hidden_ref[:, rows_at(dp, units)], grads_ref[...], 0, 0).astype(BF16)
        out = down_outs[place]
        for block in range(units // unit):
            low, high = block * unit, (block + 1) * unit
            at, end = block * half * unit // units, (block + 1) * half * unit // units
            out[at : at + unit] = down[low:high]
            out[at + unit : end] = jnp.zeros((end - at - unit, D), BF16)


def shared_grads_step(team, joint_grad, hidden, grad_team, after, context):
    return run_kernel(
        functools.partial(shared_grads_kernel, FF // lax.axis_size(ALL)),
        [context["place"], team, joint_grad, hidden, grad_team],
        [((D // 2, joint_grad.shape[1]), BF16)] * 2 + [((D // 2, D), BF16)] * 2,
        (),
        after,
        flops=2 * team.shape[0] * D * (joint_grad.shape[1] + D),
        name="shared_grads",
    )


def shared_grads(shared, after, context):
    team, grads, hidden, joint_grad = shared[-4:]
    return shared_grads_step(team, joint_grad, hidden, grads, after, context)


def out_grads_kernel(place_ref, mixed_ref, attn_ref, own_ref, other_ref):
    for out, dp in zip((own_ref, other_ref), (place_ref[3], 1 - place_ref[3])):
        out[...] = jnp.dot(
            mixed_ref[rows_at(dp, D // 2), :], attn_ref[...], preferred_element_type=F32
        ).astype(BF16)


def out_grads_step(mixed, attn_grad, context):
    return run_kernel(
        out_grads_kernel,
        [context["place"], mixed, attn_grad],
        [((D // 2, D), BF16)] * 2,
        flops=2 * mixed.shape[1] * D * D,
        name="out_grads",
    )


def feed_end_kernel(place_ref, *refs):
    layers_count = (len(refs) - 4) // 9
    pieces = refs[: 4 * layers_count]
    out_pieces = refs[4 * layers_count : 8 * layers_count]
    downs = refs[8 * layers_count : 9 * layers_count]
    joint_out, out_out, down_out, columns = refs[-4:]
    width = joint_out.shape[1]
    joint_width = pieces[0].shape[1]
    unit = down_out.shape[1]
    rest = joint_width // (2 * unit)
    for layer in range(layers_count):
        total = None
        for turn in range(4):
            columns[place_ref[0] ^ turn] = pieces[4 * layer + turn][...].astype(F32)
            part = out_pieces[4 * layer + turn][...].astype(F32)
            total = part if total is None else total + part
        out_out[layer] = total
        for member in range(4):
            rows = columns[member]
            for part in range(2):
                for block in range(rest):
                    low = (part * rest + block) * unit
                    at = part * (joint_out.shape[2] // 2) + (block * 4 + member) * unit
                    joint_out[layer, :, at : at + unit] = rows[:, low : low + unit]
        down_out[layer] = downs[layer][...].astype(F32)


def qkv_end_kernel(place_ref, *refs):
    first_ref, pieces = refs[0], refs[1:-3]
    qkv_out, small_out, columns = refs[-3:]
    edge = TEAM_HEADS * 3 * HEAD
    layers_count = qkv_out.shape[0]
    for layer in range(layers_count):
        small = None
        for turn in range(4):
            if layer == 0:
                total = None
                for block in range(first_ref.shape[0] // 4):
                    part = first_ref[block * 4 + turn].astype(F32)
                    total = part if total is None else total + part
                columns[turn] = total
            else:
                total = pieces[4 * (layer - 1) + turn][...].astype(F32)
                columns[place_ref[0] ^ turn] = total
            part = total[:, edge:]
            small = part if small is None else small + part
        small_out[layer] = small
        for member in range(4):
            rows = columns[member]
            for head in range(TEAM_HEADS):
                for part in range(3):
                    low = (head * 3 + part) * HEAD
                    at = part * D + (member * TEAM_HEADS + head) * HEAD
                    qkv_out[layer, :, at : at + HEAD] = rows[:, low : low + HEAD]


def logistic(values):
    return 0.5 * jnp.tanh(0.5 * values) + 0.5


def swiglu_back(gate_pre, up_pre, hidden_grad):
    sigmoid_gate = logistic(gate_pre)
    silu_gate = gate_pre * sigmoid_gate
    gate_grad = hidden_grad * up_pre * (sigmoid_gate + silu_gate * (1.0 - sigmoid_gate))
    up_grad = hidden_grad * silu_gate
    return (gate_grad.astype(BF16), up_grad.astype(BF16))


def swiglu(gate_pre, up_pre):
    return (gate_pre * logistic(gate_pre) * up_pre).astype(BF16)


def expert_kernel(forward, backward, *refs):
    inputs = 1 + backward
    rows_ref, grads_ref = refs[0], refs[inputs - 1]
    gate_ref, up_ref, down_ref, out_ref, total = refs[inputs:]
    step = pl.program_id(0)
    rows = rows_ref[...]
    gate, up, down = gate_ref[0, 0], up_ref[0, 0], down_ref[0, 0]
    gate_pre = jnp.dot(rows, gate, preferred_element_type=F32)
    up_pre = jnp.dot(rows, up, preferred_element_type=F32)
    terms = []
    if forward:
        terms.append(jnp.dot(swiglu(gate_pre, up_pre), down, preferred_element_type=F32))
    if backward:
        hidden_grad = contract(grads_ref[...], down, 1, 1).astype(BF16).astype(F32)
        gate_grad, up_grad = swiglu_back(gate_pre, up_pre, hidden_grad)
        terms.append(contract(gate_grad, gate, 1, 1) + contract(up_grad, up, 1, 1))

    @pl.when(step == 0)
    def _():
        for i, term in enumerate(terms):
            total[:, i * D : (i + 1) * D] = term

    @pl.when(step > 0)
    def _():
        for i, term in enumerate(terms):
            total[:, i * D : (i + 1) * D] += term

    @pl.when(step == pl.num_programs(0) - 1)
    def _():
        out_ref[...] = total[...].astype(BF16)


def run_expert(layer, joint, down, rows, grads, forward, after=()):
    half = joint.shape[3] // 2
    chunk = min(512, half)
    chunks = half // chunk
    given = [rows] + ([grads] if grads is not None else [])
    count = rows[0].shape[0]
    width = D * (int(forward) + int(grads is not None))
    drop = len(given) + 3
    body = functools.partial(expert_kernel, forward, grads is not None)
    return pl.pallas_call(
        lambda *refs: body(*refs[:drop], *refs[drop + len(after) :]),
        grid=(chunks,),
        in_specs=[
            *[pl.BlockSpec((count, D), lambda i, at=at: (0, at)) for _, at in given],
            pl.BlockSpec((1, 1, D, chunk), lambda i: (layer, 0, 0, i)),
            pl.BlockSpec((1, 1, D, chunk), lambda i: (layer, 0, 0, chunks + i)),
            pl.BlockSpec((1, 1, chunk, D), lambda i: (layer, 0, i, 0)),
            *[ANYWHERE] * len(after),
        ],
        out_specs=pl.BlockSpec((count, width), lambda i: (0, 0)),
        out_shape=jax.ShapeDtypeStruct((count, width), BF16),
        scratch_shapes=[pltpu.VMEM((count, width), F32)],
        compiler_params=vmem(
            4 * len(given) * count * D + 12 * D * chunk + 8 * count * width + 32 * count * chunk
        ),
        cost_estimate=cost(
            2 * count * D * half * (2 + int(forward) + 3 * int(grads is not None)),
            6 * D * half + 4 * count * width,
            count * half,
        ),
        name="expert_forward" if grads is None else "expert_both" if forward else "expert_back",
    )(*[array for array, _ in given], joint, joint, down, *after)


def expert_grad_kernel(place_ref, own_rows, own_grads, other_rows, other_grads, gate_ref, up_ref, down_ref, *refs):
    joint_out, down_out, rows_all, grads_all, turned, hold = refs[-6:]
    count = own_rows.shape[0]

    @pl.when((pl.program_id(0) == 0) & (pl.program_id(1) == 0))
    def _():
        own = rows_at(place_ref[3], count)
        other = rows_at(1 - place_ref[3], count)
        rows_all[own, :] = own_rows[...]
        rows_all[other, :] = other_rows[...]
        grads_all[own, :] = own_grads[...]
        grads_all[other, :] = other_grads[...]
        turned[...] = rows_all[...].T

    @pl.when(pl.program_id(1) == 0)
    def _():
        rows = rows_all[...]
        grads = grads_all[...]
        gate_pre = jnp.dot(rows, gate_ref[0, 0], preferred_element_type=F32)
        up_pre = jnp.dot(rows, up_ref[0, 0], preferred_element_type=F32)
        hidden_grad = contract(grads, down_ref[0, 0], 1, 1).astype(BF16).astype(F32)
        gate_grad, up_grad = swiglu_back(gate_pre, up_pre, hidden_grad)
        hold[...] = up_grad
        down_out[0, 0] = contract(swiglu(gate_pre, up_pre), grads, 0, 0)
        joint_out[0, 0] = jnp.dot(turned[...], gate_grad, preferred_element_type=F32)

    @pl.when(pl.program_id(1) == 1)
    def _():
        joint_out[0, 0] = jnp.dot(turned[...], hold[...], preferred_element_type=F32)


def expert_grads(layer, part, own, other, joint, down, before, later_than, context):
    half = joint.shape[3] // 2
    given = [*own, *other]
    count = given[0][0].shape[0]
    chunk = min(512 if count <= 512 else 128, half // 2)
    chunks = half // chunk
    steps = chunks // 2
    first = part * steps
    in_specs = [
        IN_SMEM,
        *[pl.BlockSpec((count, D), lambda i, h, at=at: (0, at)) for _, at in given],
        pl.BlockSpec((1, 1, D, chunk), lambda i, h: (layer, 0, 0, first + i)),
        pl.BlockSpec((1, 1, D, chunk), lambda i, h: (layer, 0, 0, chunks + first + i)),
        pl.BlockSpec((1, 1, chunk, D), lambda i, h: (layer, 0, first + i, 0)),
    ]
    operands = [context["place"]] + [array for array, _ in given] + [joint, joint, down]
    aliases = {}
    if before is not None:
        aliases = {len(operands): 0, len(operands) + 1: 1}
        operands += list(before)
    operands += later_than
    in_specs += [ANYWHERE] * (len(operands) - len(in_specs))
    return pl.pallas_call(
        expert_grad_kernel,
        grid=(steps, 2),
        in_specs=in_specs,
        out_specs=[
            pl.BlockSpec((1, 1, D, chunk), lambda i, h: (layer, 0, 0, h * chunks + first + i)),
            pl.BlockSpec((1, 1, chunk, D), lambda i, h: (layer, 0, first + i, 0)),
        ],
        out_shape=[
            jax.ShapeDtypeStruct(joint.shape, F32),
            jax.ShapeDtypeStruct(down.shape, F32),
        ],
        scratch_shapes=[
            pltpu.VMEM((2 * count, D), BF16),
            pltpu.VMEM((2 * count, D), BF16),
            pltpu.VMEM((D, 2 * count), BF16),
            pltpu.VMEM((2 * count, chunk), BF16),
        ],
        input_output_aliases=aliases,
        compiler_params=vmem(30 * count * D + 28 * D * chunk + 56 * count * chunk),
        cost_estimate=cost(12 * count * D * half, 9 * D * half, count * half),
        name="expert_grads",
    )(*operands)


def nothing(*refs):
    pass


def later(rows, *others):
    return pl.pallas_call(
        nothing,
        in_specs=[pl.BlockSpec(memory_space=pl.ANY)] * (1 + len(others)),
        out_specs=pl.BlockSpec(memory_space=pl.ANY),
        out_shape=jax.ShapeDtypeStruct(rows.shape, rows.dtype),
        input_output_aliases={0: 0},
        name="later",
    )(rows, *others)


def route_slots(route_ids):
    stretch_rows = route_ids.shape[0]
    experts_row = jnp.arange(EXPERTS, dtype=jnp.int32)
    route_hits = (route_ids[:, :, None] == experts_row[None, None, :]).astype(jnp.int32)
    running = jnp.cumsum(route_hits.reshape(2 * stretch_rows, EXPERTS), axis=0) - 1
    running = running.reshape(stretch_rows, 2, EXPERTS)
    return route_ids * SLOTS + jnp.sum(route_hits * running, axis=2)


def send_rows(outgoing, split_count):
    width = outgoing.shape[1]
    outgoing = outgoing.reshape(EXPERTS, SLOTS, width)
    if split_count > 1:
        outgoing = jnp.repeat(outgoing, split_count, axis=0)
    return exchange(outgoing, SEQ).reshape(-1, width)


def return_rows(rows, split_count):
    width = rows.shape[1]
    returned = exchange(rows.reshape(-1, SLOTS, width), SEQ)
    if split_count > 1:
        returned = (
            returned.reshape(EXPERTS, split_count, SLOTS, width).astype(F32).sum(axis=1)
        ).astype(BF16)
    return returned.reshape(EXPERTS * SLOTS, width)


def shared_kernel(forward, backward, place_ref, *refs):
    rows_refs, refs = refs[:4], refs[4:]
    if backward:
        grads_refs, refs = refs[:4], refs[4:]
    joint_ref, down_ref = refs[:2]
    parts, outs = refs[2:6], refs[6:]
    stretch = rows_refs[0].shape[0]
    team = jnp.concatenate([ref[...] for ref in rows_refs], axis=0)
    joint, down = joint_ref[...], down_ref[...]
    half = joint.shape[1] // 2
    pre = jnp.dot(team, joint, preferred_element_type=F32)
    gate_pre, up_pre = pre[:, :half], pre[:, half:]
    hidden = swiglu(gate_pre, up_pre)
    results = []
    if forward:
        results.append(jnp.dot(hidden, down, preferred_element_type=F32))
    if backward:
        grads = jnp.concatenate([ref[...] for ref in grads_refs], axis=0)
        hidden_grad = contract(grads, down, 1, 1).astype(BF16).astype(F32)
        gate_grad, up_grad = swiglu_back(gate_pre, up_pre, hidden_grad)
        joint_grad = jnp.concatenate([gate_grad, up_grad], axis=1)
        results.append(contract(joint_grad, joint, 1, 1))
        team_out, grads_out, hidden_out, joint_out = outs
        team_out[...] = team
        grads_out[...] = grads
        hidden_out[...] = hidden
        joint_out[...] = joint_grad
    for place, result in enumerate(results):
        for turn in range(4):
            parts[turn][:, place * D : (place + 1) * D] = result[
                turn * stretch : (turn + 1) * stretch
            ].astype(BF16)


def shared_step(rows, grads, joint, down, forward, after, context):
    stretch = rows[0].shape[0]
    group = TEAM_SIZE * stretch
    backward = grads is not None
    outputs = [((stretch, D * (int(forward) + int(backward))), BF16)] * 4
    if backward:
        outputs += [
            ((group, D), BF16),
            ((group, D), BF16),
            ((group, down.shape[0]), BF16),
            ((group, joint.shape[1]), BF16),
        ]
    return run_kernel(
        functools.partial(shared_kernel, forward, backward),
        [context["place"], *rows, *(grads if backward else []), joint, down],
        outputs,
        (),
        after,
        flops=2 * group * joint.size * (3 if backward else 1),
        name="shared",
        room=16,
    )


def z_turn(pieces, out):
    count = len(pieces)
    arrived = [pieces[0]]
    for turn in range(1, count):
        pairs = []
        for z in range(count):
            for core in range(2):
                to = (z + turn) % count
                if 0 <= (to if out else z) - core < TEAM_HEADS:
                    pairs.append((z * 2 + core, to * 2 + core))
        arrived.append(lax.ppermute(pieces[turn], ("z", "core"), pairs))
    return arrived


def to_heads(pieces, context):
    parts = context["parts"]
    if parts == 1:
        return z_turn(pieces, True)
    heads = jnp.stack([*pieces, jnp.zeros_like(pieces[0])])
    return [exchange(jnp.repeat(heads, parts, axis=0), "z")]


def attention_forward(arrived, after, context, stretch):
    parts = context["parts"]
    if parts == 1:
        rows, attended, wide, logs = fixed_attention(
            arrived, context["spans"][3], context["place"], stretch, after
        )
        return (exchange(attended, SEQ), (rows, wide, logs))
    (rows,) = arrived
    attended, wide, logs = attention(rows, context["spans"], stretch)
    count = context["deep"] * TEAM_SIZE
    attended = lax.dynamic_update_slice_in_dim(
        jnp.zeros((count, HEAD, stretch), BF16), attended, context["part"] * (count // parts), 0
    )
    back = exchange(attended, SEQ).reshape(TEAM_SIZE, parts, TEAM_SIZE, HEAD, stretch)
    back = back.astype(F32).sum(axis=1).astype(BF16)
    return (back.reshape(-1, HEAD, stretch), (rows, wide, logs))


def grads_to_heads(head_grads, context):
    parts = context["parts"]
    if parts > 1:
        stretch = head_grads.shape[2]
        head_grads = head_grads.reshape(TEAM_SIZE, TEAM_SIZE, HEAD, stretch)
        head_grads = jnp.repeat(head_grads, parts, axis=0).reshape(-1, HEAD, stretch)
    return exchange(head_grads, SEQ)


def attention_backward(grads, saved, after, context):
    parts = context["parts"]
    rows, wide, logs = saved
    if parts == 1:
        pieces = fixed_attention_back(
            rows, context["spans"][3], grads, wide, logs, context["place"], after
        )
        return (z_turn(pieces, False), pieces[0])
    count = grads.shape[0] // parts
    grads = lax.dynamic_slice_in_dim(grads, context["part"] * count, count, 0)
    rows_grad = attention_back(rows, context["spans"], grads, wide, logs, after)
    back = exchange(rows_grad, "z")
    back = back.reshape((TEAM_SIZE, parts) + back.shape[1:]).astype(F32).sum(axis=1).astype(BF16)
    return ([back[i] for i in range(TEAM_HEADS)], rows_grad)


def team_pieces(rows, member):
    pieces = rows.reshape(TEAM_SIZE, -1, rows.shape[1])
    parts = [lax.dynamic_index_in_dim(pieces, member ^ k, 0, keepdims=False) for k in range(4)]
    return [parts[0]] + [from_member(parts[k], k) for k in (1, 2, 3)]


def team_turn(rows, member):
    return in_order(jnp.stack(team_pieces(rows, member)), member)


def swap(rows):
    return lax.ppermute(rows, "dp", SWAP)


def beside(pairs):
    return jnp.concatenate(
        [(own.astype(F32) + other.astype(F32)).astype(BF16) for own, other in pairs], axis=1
    )


def z_sum(rows):
    return lax.psum_scatter(rows, "z", scatter_dimension=0, tiled=True)


def z_sum_direct(rows):
    count = lax.axis_size("z")
    if count > 4:
        return z_sum(rows)
    at = lax.axis_index("z")
    blocks = rows.reshape(count, -1, rows.shape[1])
    total = lax.dynamic_index_in_dim(blocks, at, 0, keepdims=False).astype(F32)
    for turn in range(1, count):
        block = lax.dynamic_index_in_dim(blocks, (at + turn) % count, 0, keepdims=False)
        block = lax.ppermute(block, "z", [(i, (i + turn) % count) for i in range(count)])
        total = total + block.astype(F32)
    return total.astype(BF16)


def to_team(parts):
    return [parts[0]] + [from_member(parts[k], k) for k in (1, 2, 3)]


def from_team(rows):
    return [rows] + [from_member(rows, k) for k in (1, 2, 3)]


def spread(rows, axes):
    count = lax.axis_size(axes)
    copies = jnp.broadcast_to(rows[None], (count,) + rows.shape)
    return exchange(copies, axes).reshape((-1,) + rows.shape[1:])


def dp_rows(rows):
    other = lax.ppermute(rows, "dp", SWAP)
    first = lax.axis_index("dp") == 0
    return jnp.concatenate([jnp.where(first, rows, other), jnp.where(first, other, rows)], axis=0)


def small_weights(gain_attn, gain_ffn, w_router):
    small = jnp.concatenate([gain_attn[:, :, None], gain_ffn[:, :, None], w_router], axis=2)
    small = small.transpose(1, 0, 2).reshape(gain_attn.shape[1], -1)
    return jnp.broadcast_to(small[None], (TEAM_SIZE,) + small.shape)


def split_small(smalls):
    weights = []
    for layer in range(LAYERS):
        part = smalls[:, layer * (2 + EXPERTS) : (layer + 1) * (2 + EXPERTS)]
        gains = part[:, :2].astype(F32).T
        weights.append(
            dict(
                gain_one=gains[0:1],
                gain_two=gains[1:2],
                router=jnp.pad(part, ((0, 0), (0, 128 - part.shape[1]))),
            )
        )
    return weights


def qkv_columns(w_qkv):
    width = w_qkv.shape[0]
    blocks = w_qkv.reshape(width, 3, TEAM_SIZE, TEAM_HEADS, HEAD)
    return blocks.transpose(2, 0, 3, 1, 4).reshape(TEAM_SIZE, width, -1)


def joint_columns(shared_gate_up):
    total = lax.axis_size(ALL)
    width = shared_gate_up.shape[0]
    blocks = shared_gate_up.reshape(width, 2, total // TEAM_SIZE, TEAM_SIZE, FF // total)
    return blocks.transpose(3, 0, 1, 2, 4).reshape(TEAM_SIZE, width, -1)


def padded_rows(shared_down):
    total = lax.axis_size(ALL)
    return jnp.pad(shared_down, ((0, TEAM_SIZE * D // total - shared_down.shape[0]), (0, 0)))


def down_rows(padded):
    total = lax.axis_size(ALL)
    return padded.reshape(total // TEAM_SIZE, -1, D)[:, : FF // total].reshape(-1, D)


def side_by_side(*arrays):
    return jnp.concatenate(arrays, axis=2)


def copies(rows):
    return jnp.broadcast_to(rows[None], (TEAM_SIZE,) + rows.shape)


def z_gather(rows):
    return lax.all_gather(rows, "z", axis=0, tiled=True)


def rest_gather(rows):
    return lax.all_gather(rows, REST, axis=0, tiled=True)


def dp_gather(rows, edges, token):
    parts = []
    for low, high in zip(edges, edges[1:]):
        token = dp_rows(later(rows[:, low:high], token))
        parts.append(token)
    return parts


def layers(
    x_in,
    cotangent,
    gain_attn,
    w_qkv,
    w_out,
    gain_ffn,
    w_router,
    shared_gate_up,
    shared_down,
    joint,
    down,
    context,
):
    split_count = context["split_count"]
    member = context["member"]
    stretch = x_in.shape[0]
    last = LAYERS - 1

    width = w_qkv.shape[1]
    qkv_width, joint_width = 3 * D // TEAM_SIZE, 2 * FF // TEAM_SIZE
    small = small_weights(gain_attn, gain_ffn, w_router)
    rows = side_by_side(qkv_columns(w_qkv[0]), small).reshape(TEAM_SIZE * width, -1)
    rows = team_turn(rows, member).reshape(TEAM_SIZE * width, -1)
    first_rows = spread(rows, "z")
    rows = side_by_side(copies(w_out[0]), joint_columns(shared_gate_up[0]))
    rows = exchange(rows, TEAM).reshape(TEAM_SIZE * width, -1)
    main_rows = jnp.concatenate([rows, padded_rows(shared_down[0])], axis=1)
    main_rows = z_gather(later(main_rows, first_rows))
    if LAYERS > 1:
        rows = side_by_side(
            *[qkv_columns(w_qkv[layer]) for layer in range(1, LAYERS)],
            *[copies(w_out[layer]) for layer in range(1, LAYERS)],
            *[joint_columns(shared_gate_up[layer]) for layer in range(1, LAYERS)],
        )
        rows = team_turn(rows.reshape(TEAM_SIZE * width, -1), member)
        rows = rows.reshape(TEAM_SIZE * width, -1)
        more_edges = [(LAYERS - 1) * qkv_width]
        for size in (D, joint_width):
            more_edges.append(more_edges[-1] + (LAYERS - 1) * size)
        more_rows = jnp.concatenate(
            [rows, *[padded_rows(shared_down[layer]) for layer in range(1, LAYERS)]], axis=1
        )
    first_rows = dp_rows(first_rows)
    weights = split_small(first_rows[:, qkv_width:])
    weights[0]["qkv"] = first_rows[:, :qkv_width]

    stream = x_in
    rows = from_team(x_in)
    grad_rows = from_team(cotangent)
    feeds = []
    for layer in range(LAYERS):
        mine = weights[layer]
        *pieces, team = qkv_step(
            rows,
            layer > 0,
            mine["gain_one"],
            mine["qkv"],
            (),
            context,
        )
        if layer == 0:
            at, held_rows, edges = 0, main_rows, [0, D, D + joint_width]
        else:
            at, held_rows, edges = layer - 1, more_rows, more_edges
        columns = [
            held_rows[:, low + at * size : low + (at + 1) * size]
            for low, size in zip(edges, (D, joint_width, D))
        ]
        after = grad_rows[1:] if layer == last else []
        if layer > 0:
            after = [*after, mine["out"], feeds[0]["other"]]
        at_heads = to_heads(pieces, context)
        if layer == 0:
            mine["out"] = dp_rows(later(columns[0], at_heads[min(2, len(at_heads) - 1)]))
        back, attended = attention_forward(at_heads, after, context, stretch)
        if layer > 0:
            mine["joint"] = dp_rows(later(columns[1], attended[1]))
        if layer == 0 and LAYERS > 1:
            more_rows = z_gather(later(more_rows, attended[1]))
        middle, normed_ffn, gates, outgoing, mixed = feed_step(
            back,
            stream,
            mine["out"],
            mine["gain_two"],
            mine["router"],
            cotangent if layer == last else None,
            [mine["joint"]] if layer > 0 else [],
            context,
        )
        if layer == 0:
            mine["joint"] = dp_rows(later(columns[1], normed_ffn))
        down_padded = dp_rows(later(columns[2], normed_ffn))
        mine["down"] = down_rows(down_padded)
        arrived = send_rows(outgoing, split_count)
        other = swap(arrived)
        ffn_rows = from_team(normed_ffn)
        def branch(after):
            return shared_step(
                ffn_rows,
                grad_rows if layer == last else None,
                mine["joint"],
                mine["down"],
                True,
                after,
                context,
            )

        if layer == last:
            shared = branch([])
        returned = run_expert(
            layer,
            joint,
            down,
            (arrived, 0),
            (arrived, 1) if layer == last else None,
            True,
            [shared[0]] if layer == last else [*ffn_rows[1:], mine["joint"]],
        )
        if layer < last:
            shared = branch([returned])
        if layer == 0:
            for i in range(1, LAYERS):
                columns = more_rows[:, (i - 1) * qkv_width : i * qkv_width]
                weights[i]["qkv"] = dp_rows(later(columns, returned))
        returned = return_rows(returned, split_count)
        feed = dict(
            stream=stream,
            team=team,
            attended=attended,
            middle=middle,
            normed_ffn=normed_ffn,
            gates=gates,
            mixed=mixed,
            arrived=arrived,
            other=other,
            ffn_rows=ffn_rows,
        )
        feeds.append(feed)
        parts = to_team(shared[:4])
        if layer < last:
            stream, feed["gap"], normed = layer_end_step(
                returned, feed, parts, weights[layer + 1]["gain_one"], [weights[layer + 1]["qkv"]], context
            )
            rows = from_team(normed)
            low = more_edges[0] + layer * D
            weights[layer + 1]["out"] = dp_rows(later(more_rows[:, low : low + D], normed))

    upstream = cotangent
    terms = None
    unit = FF // lax.axis_size(ALL)
    feed_parts, head_parts = [None] * LAYERS, [None] * LAYERS
    for layer in reversed(range(LAYERS)):
        feed, mine = feeds[layer], weights[layer]
        arrived, other = feed["arrived"], feed["other"]
        if layer == last:
            grads, other_grads = (arrived, 1), (other, 1)
            shared_parts = shared_grads(shared, [parts[2]], context)
            output, middle_grad, attn_grad, head_grads, small = feed_back_step(
                returned,
                feed,
                upstream,
                parts,
                [],
                mine,
                True,
                [shared_parts[1], shared_parts[3]],
                context,
            )
        else:
            arrived_grad = send_rows(outgoing_grads, split_count)
            grads, other_grads = (arrived_grad, 0), (swap(arrived_grad), 0)
            grad_rows = from_team(upstream_rows)
            waiting = [(own, swap(rows)) for own, rows in waiting]
            shared = shared_step(
                feed["ffn_rows"],
                grad_rows,
                mine["joint"],
                mine["down"],
                False,
                [],
                context,
            )
            returned = run_expert(
                layer,
                joint,
                down,
                (arrived, 0),
                (arrived_grad, 0),
                False,
                [shared[0], *[rows for _, rows in waiting]],
            )
            terms = expert_grads(
                *rest_of_terms, terms, [returned, other_grads[0]], context
            )
            returned = return_rows(returned, split_count)
            parts = to_team(shared[:4])
            shared_parts = shared_grads(shared, [parts[2]], context)
            waiting = [(own, later(rows, parts[1])) for own, rows in waiting]
            waiting_sum = z_sum(beside([*waiting, *waited]))
            middle_grad, attn_grad, head_grads, small = feed_back_step(
                returned,
                feed,
                upstream,
                parts,
                [feed["gap"]],
                mine,
                False,
                [shared_parts[1], shared_parts[3], terms[1]],
                context,
            )
        out_own, out_other = out_grads_step(feed["mixed"], attn_grad, context)
        joint_arrived, down_arrived = swap(shared_parts[1]), swap(shared_parts[3])
        out_arrived = swap(out_other)
        at_heads = grads_to_heads(head_grads, context)
        halves = [(shared_parts[0], later(joint_arrived, at_heads))]
        if layer == 0:
            halves.append((shared_parts[2], down_arrived))
        shared_sum = z_sum(beside(halves))
        pieces, token = attention_backward(
            at_heads,
            feed["attended"],
            [],
            context,
        )
        held = ((arrived, 0), grads), ((other, 0), other_grads)
        terms = expert_grads(layer, 0, *held, joint, down, terms, [token], context)
        results = qkv_back_step(
            pieces,
            mine["qkv"],
            feed["team"],
            mine["gain_one"],
            small,
            layer > 0,
            [shared_sum, out_arrived, terms[1]] + ([down_arrived] if layer > 0 else [waiting_sum]),
            context,
        )
        normed_parts, packed = to_team(results[:4]), results[4:]
        if layer > 0:
            waiting = [packed]
            waited = [(out_own, out_arrived), (shared_parts[2], down_arrived)]
            upstream, upstream_rows, outgoing_grads = layer_start_step(
                feed["stream"], middle_grad, mine["gain_one"], normed_parts, feeds[layer - 1], context
            )
            rest_of_terms = (layer, 1, *held, joint, down)
        else:
            (upstream_rows,) = layer_start_step(
                feed["stream"], middle_grad, mine["gain_one"], normed_parts, None, context
            )
            total = lax.axis_size(ALL)
            first_sum = exchange(packed[0].reshape(total, D // total, -1), ALL)
            out_sum = z_sum(beside([(out_own, later(out_arrived, packed[0]))]))
        if layer < last:
            edge = waiting_sum.shape[1] - 2 * D
            head_parts[layer + 1] = team_pieces(waiting_sum[:, :edge], member)
            feed_parts[layer + 1][1] = team_pieces(waiting_sum[:, edge : edge + D], member)
            feed_parts[layer + 1][2] = waiting_sum[:unit, edge + D :]
        feed_parts[layer] = [
            team_pieces(shared_sum[:, :joint_width], member),
            None,
            shared_sum[:unit, joint_width:] if layer == 0 else None,
        ]
        if layer == 0:
            early = [packed[0], *feed_parts[0][0][1:]]
            for later_layer in range(1, LAYERS):
                early += head_parts[later_layer][1:]
                early += feed_parts[later_layer][0][1:] + feed_parts[later_layer][1][1:]
            terms = expert_grads(layer, 1, *held, joint, down, terms, early, context)
            feed_parts[0][1] = team_pieces(later(out_sum, terms[1]), member)
    joint_sum, out_sum, down_sum = run_kernel(
        feed_end_kernel,
        [
            context["place"],
            *[piece for pieces, _, _ in feed_parts for piece in pieces],
            *[piece for _, pieces, _ in feed_parts for piece in pieces],
            *[rows for _, _, rows in feed_parts],
        ],
        [
            ((LAYERS, width, 2 * FF), F32),
            ((LAYERS, width, D), F32),
            ((LAYERS, unit, D), F32),
        ],
        [((TEAM_SIZE, width, joint_width), F32)],
        name="feed_end",
    )
    qkv_sum, small_sum = run_kernel(
        qkv_end_kernel,
        [context["place"], first_sum, *[piece for pieces in head_parts[1:] for piece in pieces]],
        [((LAYERS, width, 3 * D), F32), ((LAYERS, width, 64), F32)],
        [((TEAM_SIZE, width, first_sum.shape[2]), F32)],
        name="qkv_end",
    )
    dense = (
        small_sum[:, :, 0],
        qkv_sum,
        out_sum,
        small_sum[:, :, 1],
        small_sum[:, :, 2 : 2 + EXPERTS],
        joint_sum,
        down_sum,
    )
    return (output, upstream_rows, dense, terms)


def query_spans(block_row, group, part, parts):
    length = block_row.shape[0]
    limit = jnp.sum((block_row[None, :] <= block_row[:, None]).astype(jnp.int32), axis=1)
    tiles = length // QUERY_TILE // parts
    base = part * tiles
    ends = lax.dynamic_slice_in_dim(limit.reshape(-1, QUERY_TILE), base, tiles, 0)
    full = ends[:, 0] // group
    some = (ends[:, -1] + group - 1) // group
    base = jnp.full((1,), base, jnp.int32)
    return (full, some, base, limit[None, :], tiles, parts)


def local(
    x_in,
    block_ids,
    expert_ids,
    cotangent,
    gain_attn,
    w_qkv,
    w_out,
    gain_ffn,
    w_router,
    shared_gate_up,
    shared_down,
    expert_gate_up,
    expert_down,
):
    stretch = x_in.shape[1]
    group = TEAM_SIZE * stretch
    deep = lax.axis_size("z")
    parts = max(1, deep // TEAM_SIZE)
    at = lax.axis_index("z")
    member = lax.axis_index("core") * lax.axis_size("ulysses") + lax.axis_index("ulysses")
    half_size = HEAD // 2
    spacing = 10000.0 ** (-jnp.arange(half_size).astype(F32) * 2.0 / HEAD)
    positions = (at * group + jnp.arange(group, dtype=jnp.int32)).astype(F32)
    angles = spacing[:, None] * positions[None, :]
    part = at % parts
    slots = route_slots(expert_ids[0])
    place = [member, at, lax.axis_index("core"), lax.axis_index("dp")]
    context = dict(
        member=member,
        place=jnp.stack(place).astype(jnp.int32),
        cosine=jnp.cos(angles),
        sine=jnp.sin(angles),
        ids=expert_ids[0],
        slots=slots,
        turned_slots=slots.T,
        parts=parts,
        part=part,
        deep=deep,
        split_count=deep * TEAM_SIZE // EXPERTS,
        spans=query_spans(block_ids[0], group, part, parts),
    )
    output, grad_x, dense, terms = layers(
        x_in[0],
        cotangent[0],
        gain_attn,
        w_qkv,
        w_out,
        gain_ffn,
        w_router,
        shared_gate_up,
        shared_down,
        expert_gate_up,
        expert_down,
        context,
    )
    return (output[None], grad_x[None], *dense, *terms)


def solution(mesh):
    dp, blk, ulysses = mesh.devices.shape
    grid = Mesh(mesh.devices.reshape(dp, blk // 2, 2, ulysses), ALL)
    rows = P("dp", SEQ, None)
    in_specs = (
        rows,
        P("dp", None),
        rows,
        rows,
        P(None, ALL),
        P(None, ALL, None),
        P(None, ALL, None),
        P(None, ALL),
        P(None, ALL, None),
        P(None, ALL, None),
        P(None, ALL, None),
        P(None, SEQ, None, None),
        P(None, SEQ, None, None),
    )
    out_specs = (
        rows,
        rows,
        P(None, ALL),
        P(None, ALL, None),
        P(None, ALL, None),
        P(None, ALL),
        P(None, ALL, None),
        P(None, ALL, None),
        P(None, ALL, None),
        P(None, SEQ, None, None),
        P(None, SEQ, None, None),
    )
    return jax.shard_map(local, mesh=grid, in_specs=in_specs, out_specs=out_specs, check_vma=False)
```

```python
import functools
import math

import jax
import jax.numpy as jnp
from jax import lax
from jax.experimental import pallas as pl
from jax.experimental.pallas import tpu as pltpu
from jax.sharding import Mesh
from jax.sharding import PartitionSpec as P

D = 768
HEADS = 12
HEAD = 64
FF = 2048
EXPERTS = 16
LAYERS = 2
MOST = 21
SLOTS = -(-MOST // 8) * 8
TEAM_SIZE = 4
TEAM_HEADS = HEADS // TEAM_SIZE

ALL = ("dp", "z", "core", "ulysses")
SEQ = ("z", "core", "ulysses")
TEAM = ("core", "ulysses")
REST = ("dp", "z")

NORM_EPS = 1e-06
NEG_BIG = -1e30
PRECISE = lax.Precision.HIGHEST
F32 = jnp.float32
BF16 = jnp.bfloat16
QUERY_TILE = 256
MIB = 1024 * 1024


def vmem(size):
    return pltpu.CompilerParams(vmem_limit_bytes=61 * MIB)


def cost(flops, moved, steps=0):
    return pl.CostEstimate(flops=flops, bytes_accessed=moved, transcendentals=steps)


def contract(left, right, left_dim, right_dim):
    return lax.dot_general(
        left, right, (((left_dim,), (right_dim,)), ((), ())), preferred_element_type=F32
    )


def exchange(rows, axes):
    return lax.all_to_all(rows, axes, split_axis=0, concat_axis=0, tiled=True)


SWAP = [(0, 1), (1, 0)]


def from_member(rows, turn):
    if turn == 1:
        return lax.ppermute(rows, "ulysses", SWAP)
    if turn == 2:
        return lax.ppermute(rows, "core", SWAP)
    return lax.ppermute(rows, TEAM, [(i, 3 - i) for i in range(4)])


def team_gather(rows):
    return jnp.stack([rows] + [from_member(rows, turn) for turn in (1, 2, 3)])


def in_order(stacked, member):
    turns = [jnp.equal(member, i) for i in range(4)]
    pieces = []
    for k in range(4):
        piece = stacked[k ^ 3]
        for i in range(3):
            piece = jnp.where(turns[i], stacked[k ^ i], piece)
        pieces.append(piece)
    return jnp.stack(pieces)


def team_sum(parts):
    total = parts[0].astype(F32)
    for turn in (1, 2, 3):
        total = total + from_member(parts[turn].astype(BF16), turn).astype(F32)
    return total


def rms_factor(stream):
    return lax.rsqrt(jnp.mean(stream * stream, axis=-1, keepdims=True) + NORM_EPS)


def norm_back(stream, gain, factor, upstream):
    weighted = upstream * gain
    inner_mean = jnp.mean(weighted * stream, axis=-1, keepdims=True)
    grad_stream = factor * weighted - stream * factor * factor * factor * inner_mean
    grad_gain = jnp.sum(upstream * stream * factor, axis=0)
    return (grad_stream, grad_gain)


def attention_kernel(full_ref, some_ref, base_ref, rows_ref, limit_ref, out_ref, wide_ref, log_ref, keys):
    span = rows_ref.shape[2]
    step = pl.program_id(0)
    per_block = span // QUERY_TILE

    @pl.when(step == 0)
    def _():
        for s in range(rows_ref.shape[0]):
            keys[s] = rows_ref[s, HEAD : 2 * HEAD, :].T

    tile = base_ref[0] + step
    lanes = pl.ds(pl.multiple_of((tile % per_block) * QUERY_TILE, QUERY_TILE), QUERY_TILE)
    queries = rows_ref[tile // per_block, 0:HEAD, lanes] * BF16(HEAD**-0.5)
    limit = limit_ref[...]
    key_index = lax.broadcasted_iota(jnp.int32, (span, QUERY_TILE), 0)

    def sweep(s, state, masked):
        highest, total, running = state
        scores = jnp.dot(keys[s], queries, preferred_element_type=F32)
        if masked:
            scores = jnp.where(key_index < limit - s * span, scores, NEG_BIG)
        raised = jnp.maximum(highest, jnp.max(scores, axis=0, keepdims=True))
        terms = jnp.exp(scores - raised)
        shrink = jnp.exp(highest - raised)
        total = total * shrink + jnp.sum(terms, axis=0, keepdims=True)
        running = running * shrink + jnp.dot(
            rows_ref[s, 2 * HEAD :, :], terms.astype(BF16), preferred_element_type=F32
        )
        return (raised, total, running)

    state = (
        jnp.full((1, QUERY_TILE), NEG_BIG, F32),
        jnp.zeros((1, QUERY_TILE), F32),
        jnp.zeros((HEAD, QUERY_TILE), F32),
    )
    state = lax.fori_loop(0, full_ref[step], lambda s, c: sweep(s, c, False), state)
    state = lax.fori_loop(full_ref[step], some_ref[step], lambda s, c: sweep(s, c, True), state)
    highest, total, running = state
    result = running / total
    log_ref[...] = highest + jnp.log(total)
    wide_ref[...] = result
    stretch = out_ref.shape[2]
    for i in range(QUERY_TILE // stretch):
        out_ref[i] = result[:, i * stretch : (i + 1) * stretch].astype(BF16)


def attention_back_kernel(
    full_ref, some_ref, base_ref, rows_ref, limit_ref, grad_ref, wide_ref, log_ref, *refs
):
    out_ref, keys, values, key_sum, value_sum = refs[-5:]
    span = rows_ref.shape[2]
    blocks = rows_ref.shape[0]
    step = pl.program_id(0)
    per_block = span // QUERY_TILE

    @pl.when(step == 0)
    def _():
        for s in range(blocks):
            keys[s] = rows_ref[s, HEAD : 2 * HEAD, :].T
            values[s] = rows_ref[s, 2 * HEAD :, :].T
        key_sum[...] = jnp.zeros_like(key_sum)
        value_sum[...] = jnp.zeros_like(value_sum)
        out_ref[...] = jnp.zeros_like(out_ref)

    tile = base_ref[0] + step
    lanes = pl.ds(pl.multiple_of((tile % per_block) * QUERY_TILE, QUERY_TILE), QUERY_TILE)
    queries = rows_ref[tile // per_block, 0:HEAD, lanes] * BF16(HEAD**-0.5)
    limit = limit_ref[...]
    key_index = lax.broadcasted_iota(jnp.int32, (span, QUERY_TILE), 0)
    grads = jnp.concatenate([grad_ref[i] for i in range(grad_ref.shape[0])], axis=1)
    delta = jnp.sum(grads.astype(F32) * wide_ref[...], axis=0, keepdims=True)
    logs = log_ref[...]

    def sweep(s, query_grad, masked):
        scores = jnp.dot(keys[s], queries, preferred_element_type=F32)
        probs = jnp.exp(scores - logs)
        if masked:
            probs = jnp.where(key_index < limit - s * span, probs, 0.0)
        prob_grad = jnp.dot(values[s], grads, preferred_element_type=F32)
        score_grad = (probs * (prob_grad - delta)).astype(BF16)
        value_sum[s] += contract(grads, probs.astype(BF16), 1, 1)
        key_sum[s] += contract(queries, score_grad, 1, 1)
        return query_grad + jnp.dot(
            rows_ref[s, HEAD : 2 * HEAD, :], score_grad, preferred_element_type=F32
        )

    query_grad = jnp.zeros((HEAD, QUERY_TILE), F32)
    query_grad = lax.fori_loop(0, full_ref[step], lambda s, c: sweep(s, c, False), query_grad)
    query_grad = lax.fori_loop(
        full_ref[step], some_ref[step], lambda s, c: sweep(s, c, True), query_grad
    )
    out_ref[tile // per_block, 0:HEAD, lanes] = (query_grad * HEAD**-0.5).astype(BF16)

    @pl.when(step == pl.num_programs(0) - 1)
    def _():
        out_ref[:, HEAD : 2 * HEAD, :] = key_sum[...].astype(BF16)
        out_ref[:, 2 * HEAD :, :] = value_sum[...].astype(BF16)


def fixed_attention_kernel(place_ref, *refs):
    rows_ref, out_ref, wide_ref, log_ref, keys, values = refs[-6:]
    blocks, _, span = rows_ref.shape
    pieces, limit_ref = refs[:blocks], refs[blocks]
    for turn in range(blocks):
        rows_ref[lax.rem(place_ref[1] + blocks - turn, blocks)] = pieces[turn][...]
    length = blocks * span
    stretch = out_ref.shape[2]
    for s in range(blocks):
        keys[s * span : (s + 1) * span, :] = rows_ref[s, HEAD : 2 * HEAD, :].T
        values[:, s * span : (s + 1) * span] = rows_ref[s, 2 * HEAD :, :]
    key_index = lax.broadcasted_iota(jnp.int32, (2 * QUERY_TILE, QUERY_TILE), 0)
    for tile in range(length // QUERY_TILE):
        start = tile * QUERY_TILE
        end = min(start + 2 * QUERY_TILE, length)
        lanes = slice(start % span, start % span + QUERY_TILE)
        queries = rows_ref[start // span, 0:HEAD, lanes] * BF16(HEAD**-0.5)
        scores = jnp.dot(keys[start:end, :], queries, preferred_element_type=F32)
        limit = limit_ref[:, start : start + QUERY_TILE] - start
        scores = jnp.where(key_index[: end - start] < limit, scores, NEG_BIG)
        highest = jnp.max(scores, axis=0, keepdims=True)
        if start > 0:
            before = jnp.dot(keys[:start, :], queries, preferred_element_type=F32)
            highest = jnp.maximum(highest, jnp.max(before, axis=0, keepdims=True))
        terms = jnp.exp(scores - highest)
        total = jnp.sum(terms, axis=0, keepdims=True)
        result = jnp.dot(values[:, start:end], terms.astype(BF16), preferred_element_type=F32)
        if start > 0:
            terms = jnp.exp(before - highest)
            total = total + jnp.sum(terms, axis=0, keepdims=True)
            result = result + jnp.dot(
                values[:, :start], terms.astype(BF16), preferred_element_type=F32
            )
        result = result / total
        log_ref[:, start : start + QUERY_TILE] = highest + jnp.log(total)
        wide_ref[:, start : start + QUERY_TILE] = result
        for i in range(QUERY_TILE // stretch):
            out_ref[start // stretch + i] = result[:, i * stretch : (i + 1) * stretch].astype(BF16)


def fixed_attention_back_kernel(place_ref, rows_ref, limit_ref, grad_ref, wide_ref, log_ref, *refs):
    blocks, _, span = rows_ref.shape
    out_ref, keys, values, key_sum, value_sum = refs[-5:]
    outs = refs[-5 - blocks : -5]
    length = blocks * span
    stretch = grad_ref.shape[2]
    for s in range(blocks):
        keys[s * span : (s + 1) * span, :] = rows_ref[s, HEAD : 2 * HEAD, :].T
        values[s * span : (s + 1) * span, :] = rows_ref[s, 2 * HEAD :, :].T
    key_sum[...] = jnp.zeros_like(key_sum)
    value_sum[...] = jnp.zeros_like(value_sum)
    key_index = lax.broadcasted_iota(jnp.int32, (2 * QUERY_TILE, QUERY_TILE), 0)
    for tile in range(length // QUERY_TILE):
        start = tile * QUERY_TILE
        end = min(start + 2 * QUERY_TILE, length)
        lanes = slice(start % span, start % span + QUERY_TILE)
        queries = rows_ref[start // span, 0:HEAD, lanes] * BF16(HEAD**-0.5)
        pieces = QUERY_TILE // stretch
        grads = jnp.concatenate([grad_ref[tile * pieces + i] for i in range(pieces)], axis=1)
        wide = wide_ref[:, start : start + QUERY_TILE]
        delta = jnp.sum(grads.astype(F32) * wide, axis=0, keepdims=True)
        logs = log_ref[:, start : start + QUERY_TILE]
        limit = limit_ref[:, start : start + QUERY_TILE] - start
        query_grad = jnp.zeros((HEAD, QUERY_TILE), F32)
        for low, high in ((0, start), (start, end)):
            if low == high:
                continue
            scores = jnp.dot(keys[low:high, :], queries, preferred_element_type=F32)
            probs = jnp.exp(scores - logs)
            if low == start:
                probs = jnp.where(key_index[: high - low] < limit, probs, 0.0)
            prob_grad = jnp.dot(values[low:high, :], grads, preferred_element_type=F32)
            score_grad = (probs * (prob_grad - delta)).astype(BF16)
            value_sum[:, low:high] += contract(grads, probs.astype(BF16), 1, 1)
            key_sum[:, low:high] += contract(queries, score_grad, 1, 1)
            query_grad = query_grad + contract(keys[low:high, :], score_grad, 0, 0)
        out_ref[start // span, 0:HEAD, lanes] = (query_grad * HEAD**-0.5).astype(BF16)
    for s in range(blocks):
        out_ref[s, HEAD : 2 * HEAD, :] = key_sum[:, s * span : (s + 1) * span].astype(BF16)
        out_ref[s, 2 * HEAD :, :] = value_sum[:, s * span : (s + 1) * span].astype(BF16)
    for turn in range(blocks):
        outs[turn][...] = out_ref[lax.rem(place_ref[1] + turn, blocks)]


def at_once(shape):
    return pl.BlockSpec(shape, lambda step: (0,) * len(shape))


ANYWHERE = pl.BlockSpec(memory_space=pl.ANY)
IN_SMEM = pl.BlockSpec(memory_space=pltpu.SMEM)


def fixed_attention(pieces, limit, place, stretch, after):
    blocks = len(pieces)
    features, span = pieces[0].shape
    length = blocks * span
    return pl.pallas_call(
        fixed_attention_kernel,
        grid=(1,),
        in_specs=[IN_SMEM, *[at_once(array.shape) for array in (*pieces, limit)]]
        + [ANYWHERE] * len(after),
        out_specs=[
            at_once((blocks, features, span)),
            at_once((length // stretch, HEAD, stretch)),
            at_once((HEAD, length)),
            at_once((1, length)),
        ],
        out_shape=[
            jax.ShapeDtypeStruct((blocks, features, span), BF16),
            jax.ShapeDtypeStruct((length // stretch, HEAD, stretch), BF16),
            jax.ShapeDtypeStruct((HEAD, length), F32),
            jax.ShapeDtypeStruct((1, length), F32),
        ],
        scratch_shapes=[pltpu.VMEM((length, HEAD), BF16), pltpu.VMEM((HEAD, length), BF16)],
        compiler_params=vmem(16 * MIB),
        cost_estimate=cost(features * length * length // 48, features * length * 4, length * length),
        name="attend",
    )(place, *pieces, limit, *after)


def fixed_attention_back(rows, limit, grads, wide, logs, place, later_than):
    blocks, features, span = rows.shape
    length = blocks * span
    return pl.pallas_call(
        fixed_attention_back_kernel,
        grid=(1,),
        in_specs=[
            IN_SMEM,
            *[at_once(array.shape) for array in (rows, limit, grads, wide, logs)],
        ]
        + [ANYWHERE] * len(later_than),
        out_specs=[at_once((features, span))] * blocks,
        out_shape=[jax.ShapeDtypeStruct((features, span), BF16)] * blocks,
        scratch_shapes=[
            pltpu.VMEM(rows.shape, BF16),
            pltpu.VMEM((length, HEAD), BF16),
            pltpu.VMEM((length, HEAD), BF16),
            pltpu.VMEM((HEAD, length), F32),
            pltpu.VMEM((HEAD, length), F32),
        ],
        compiler_params=vmem(20 * MIB),
        cost_estimate=cost(rows.size * length // 16, rows.size * 4, length * length),
        name="attend_back",
    )(place, rows, limit, grads, wide, logs, *later_than)


def whole(shape):
    return pl.BlockSpec(shape, lambda step, *_: (0,) * len(shape))


def tile_at(step, full, some, base):
    return (0, base[0] + step)


def attention(rows, spans, stretch):
    full, some, base, limit, tiles, parts = spans
    blocks, _, span = rows.shape
    length = tiles * QUERY_TILE
    return pl.pallas_call(
        attention_kernel,
        grid_spec=pltpu.PrefetchScalarGridSpec(
            num_scalar_prefetch=3,
            grid=(tiles,),
            in_specs=[whole(rows.shape), pl.BlockSpec((1, QUERY_TILE), tile_at)],
            out_specs=[
                pl.BlockSpec((QUERY_TILE // stretch, HEAD, stretch), lambda step, *_: (step, 0, 0)),
                pl.BlockSpec((HEAD, QUERY_TILE), lambda step, *_: (0, step)),
                pl.BlockSpec((1, QUERY_TILE), lambda step, *_: (0, step)),
            ],
            scratch_shapes=[pltpu.VMEM((blocks, span, HEAD), BF16)],
        ),
        out_shape=[
            jax.ShapeDtypeStruct((length // stretch, HEAD, stretch), BF16),
            jax.ShapeDtypeStruct((HEAD, length), F32),
            jax.ShapeDtypeStruct((1, length), F32),
        ],
        compiler_params=vmem(52 * MIB),
        cost_estimate=cost(rows.size * length // 48, rows.size * 4, length * length),
        name="attend",
    )(full, some, base, rows, limit)


def attention_back(rows, spans, grads, wide, logs, later_than):
    full, some, base, limit, tiles, parts = spans
    blocks, _, span = rows.shape
    stretch = grads.shape[2]
    return pl.pallas_call(
        attention_back_kernel,
        grid_spec=pltpu.PrefetchScalarGridSpec(
            num_scalar_prefetch=3,
            grid=(tiles,),
            in_specs=[
                whole(rows.shape),
                pl.BlockSpec((1, QUERY_TILE), tile_at),
                pl.BlockSpec((QUERY_TILE // stretch, HEAD, stretch), lambda step, *_: (step, 0, 0)),
                pl.BlockSpec((HEAD, QUERY_TILE), lambda step, *_: (0, step)),
                pl.BlockSpec((1, QUERY_TILE), lambda step, *_: (0, step)),
                *[pl.BlockSpec(memory_space=pl.ANY)] * len(later_than),
            ],
            out_specs=whole(rows.shape),
            scratch_shapes=[
                pltpu.VMEM((blocks, span, HEAD), BF16),
                pltpu.VMEM((blocks, span, HEAD), BF16),
                pltpu.VMEM((blocks, HEAD, span), F32),
                pltpu.VMEM((blocks, HEAD, span), F32),
            ],
        ),
        out_shape=jax.ShapeDtypeStruct(rows.shape, BF16),
        compiler_params=vmem(52 * MIB),
        cost_estimate=cost(rows.size * tiles * QUERY_TILE // 16, rows.size * 4, rows.size),
        name="attend_back",
    )(full, some, base, rows, limit, grads, wide, logs, *later_than)


def run_kernel(kernel, operands, outputs, scratch=(), after=(), flops=0, name=None, room=6):
    moved = sum(array.size * array.dtype.itemsize for array in operands)
    size = 2 * moved
    for times, arrays in ((2, outputs), (1, scratch)):
        for shape, dtype in arrays:
            size += times * math.prod(shape) * jnp.dtype(dtype).itemsize
    given, kept = len(operands), len(operands) + len(after)
    return pl.pallas_call(
        lambda *refs: kernel(*refs[:given], *refs[kept:]),
        grid=(1,),
        in_specs=[IN_SMEM, *[at_once(array.shape) for array in operands[1:]]]
        + [ANYWHERE] * len(after),
        out_specs=[at_once(shape) for shape, _ in outputs],
        out_shape=[jax.ShapeDtypeStruct(shape, dtype) for shape, dtype in outputs],
        scratch_shapes=[pltpu.VMEM(shape, dtype) for shape, dtype in scratch],
        compiler_params=vmem(room * MIB + size),
        cost_estimate=cost(flops, moved),
        name=name,
    )(*operands, *after)


def rows_at(index, size):
    return pl.ds(pl.multiple_of(index * size, size), size)


def qkv_kernel(fixed, normed, place_ref, *refs):
    rows_refs, (gain_ref, weight_ref, cosine_ref, sine_ref) = refs[:4], refs[4:8]
    pieces, team, heads = refs[8:-2], refs[-2], refs[-1]
    member = place_ref[0]
    stretch = rows_refs[0].shape[0]
    half = HEAD // 2
    for turn in range(4):
        rows = rows_refs[turn][...]
        if not normed:
            wide = rows.astype(F32)
            rows = (wide * rms_factor(wide) * gain_ref[...]).astype(BF16)
        team[rows_at(member ^ turn, stretch), :] = rows
    projected = contract(weight_ref[...], team[...], 0, 1)
    cosine, sine = cosine_ref[...], sine_ref[...]
    for head in range(TEAM_HEADS):
        for part in range(3):
            at = (head * 3 + part) * HEAD
            first, second = projected[at : at + half], projected[at + half : at + HEAD]
            if part < 2:
                first, second = (
                    first * cosine - second * sine,
                    second * cosine + first * sine,
                )
            heads[head, part * HEAD : part * HEAD + half] = first.astype(BF16)
            heads[head, part * HEAD + half : (part + 1) * HEAD] = second.astype(BF16)
    for turn, piece in enumerate(pieces):
        head = turn
        if fixed:
            head = lax.rem(place_ref[1] + turn, len(pieces)) - place_ref[2]
            head = jnp.clip(head, 0, TEAM_HEADS - 1)
        piece[...] = heads[head]


def qkv_step(rows, normed, gain, weight, after, context):
    group = TEAM_SIZE * rows[0].shape[0]
    fixed = context["parts"] == 1
    return run_kernel(
        functools.partial(qkv_kernel, fixed, normed),
        [context["place"], *rows, gain, weight, context["cosine"], context["sine"]],
        [((3 * HEAD, group), BF16)] * (context["deep"] if fixed else TEAM_HEADS)
        + [((group, D), BF16)],
        [((TEAM_HEADS, 3 * HEAD, group), BF16)],
        after,
        flops=2 * group * D * weight.shape[1],
        name="qkv",
    )


def qkv_back_kernel(fixed, halves, place_ref, *refs):
    count = len(refs) - (16 if halves else 15)
    grads, refs = refs[:count], refs[count:]
    weight_ref, cosine_ref, sine_ref, team_ref, gain_ref, small_ref = refs[:6]
    outs, (stacked, turned, parts, packed) = refs[6:-4], refs[-4:]
    half = HEAD // 2
    stretch = outs[0].shape[0]
    for turn in range(count):
        stacked[turn] = grads[turn][...]
    cosine, sine = cosine_ref[...], sine_ref[...]
    for head in range(TEAM_HEADS):
        at = head
        if fixed:
            at = lax.rem(place_ref[1] - head - place_ref[2] + 2 * count, count)
        rows = stacked[at].astype(F32)
        for part in range(3):
            low = part * HEAD
            first, second = rows[low : low + half], rows[low + half : low + HEAD]
            if part < 2:
                first, second = (
                    first * cosine + second * sine,
                    second * cosine - first * sine,
                )
            low += head * 3 * HEAD
            turned[low : low + half] = first.astype(BF16)
            turned[low + half : low + HEAD] = second.astype(BF16)
    projected_grad = turned[...].T
    normed_grad = contract(projected_grad, weight_ref[...], 1, 1)
    parts[...] = normed_grad.astype(BF16)
    for turn in range(4):
        outs[turn][...] = parts[rows_at(place_ref[0] ^ turn, stretch), :]
    team = team_ref[...]
    edge = projected_grad.shape[1]
    packed[:, :edge] = contract(team, projected_grad, 0, 0).astype(BF16)
    gain_grad = jnp.sum(normed_grad * team.astype(F32), axis=0, keepdims=True) / gain_ref[...]
    small = small_ref[...]
    lane = lax.broadcasted_iota(jnp.int32, small.shape, 1)
    small = jnp.where(lane == 0, jnp.broadcast_to(gain_grad, (128, D)).T, small)
    packed[:, edge:] = small[:, : packed.shape[1] - edge].astype(BF16)
    if halves:
        outs[4][...] = packed[rows_at(place_ref[3], D // 2), :]
        outs[5][...] = packed[rows_at(1 - place_ref[3], D // 2), :]
    else:
        outs[4][...] = packed[...]


def qkv_back_step(grads, weight, team, gain, small, halves, after, context):
    group = team.shape[0]
    width = weight.shape[1] + 64
    packed = [((D // 2, width), BF16)] * 2 if halves else [((D, width), BF16)]
    return run_kernel(
        functools.partial(qkv_back_kernel, context["parts"] == 1, halves),
        [
            context["place"],
            *grads,
            weight,
            context["cosine"],
            context["sine"],
            team,
            gain,
            small,
        ],
        [((group // TEAM_SIZE, D), BF16)] * TEAM_SIZE + packed,
        [
            ((len(grads), 3 * HEAD, group), BF16),
            ((weight.shape[1], group), BF16),
            ((group, D), BF16),
            ((D, width), BF16),
        ],
        after,
        flops=4 * group * D * weight.shape[1],
        name="qkv_back",
    )


def head_slot(head, fixed):
    member = head // TEAM_HEADS
    return (head % TEAM_HEADS + (member // 2 if fixed else 0)) * TEAM_SIZE + member


def chosen(ids_ref, choice):
    ids = ids_ref[:, choice : choice + 1]
    return lax.broadcasted_iota(jnp.int32, (ids.shape[0], 128), 1) == ids + 2


def row_table(slots_ref, choice):
    slots = slots_ref[:, choice : choice + 1]
    index = lax.broadcasted_iota(jnp.int32, (slots.shape[0], EXPERTS * SLOTS), 1)
    return jnp.where(index == slots, 1.0, 0.0).astype(BF16)


def slot_table(turned_ref, choice):
    slots = turned_ref[choice : choice + 1, :]
    index = lax.broadcasted_iota(jnp.int32, (EXPERTS * SLOTS, slots.shape[1]), 0)
    return jnp.where(index == slots, 1.0, 0.0).astype(BF16)


def slots_of_grads(turned_ref, gates, upstream):
    terms = [
        jnp.dot(
            slot_table(turned_ref, c),
            (gates[:, c : c + 1] * upstream).astype(BF16),
            preferred_element_type=F32,
        )
        for c in range(2)
    ]
    return (terms[0] + terms[1]).astype(BF16)


def feed_kernel(fixed, last, place_ref, *refs):
    back_ref, stream_ref, weight_ref, gain_ref, router_ref, ids_ref, turned_ref = refs[:7]
    middle_ref, normed_ref, gates_ref, out_ref, mixed_ref = refs[-5:]
    for head in range(HEADS):
        mixed_ref[head * HEAD : (head + 1) * HEAD, :] = back_ref[head_slot(head, fixed)]
    middle = stream_ref[...].astype(F32) + contract(mixed_ref[...], weight_ref[...], 0, 0)
    normed = (middle * rms_factor(middle) * gain_ref[...]).astype(BF16)
    middle_ref[...] = middle
    normed_ref[...] = normed
    table = slot_table(turned_ref, 0) + slot_table(turned_ref, 1)
    out_ref[:, :D] = jnp.dot(table, normed, preferred_element_type=F32).astype(BF16)
    logits = jnp.dot(normed, router_ref[...], preferred_element_type=F32)
    picked = [
        jnp.sum(jnp.where(chosen(ids_ref, c), logits, 0.0), axis=1, keepdims=True)
        for c in range(2)
    ]
    highest = jnp.maximum(picked[0], picked[1])
    powers = [jnp.exp(pick - highest) for pick in picked]
    total = powers[0] + powers[1]
    gates = jnp.concatenate([powers[0] / total, powers[1] / total], axis=1)
    gates_ref[...] = gates
    if last:
        out_ref[:, D:] = slots_of_grads(turned_ref, gates, refs[7][...].astype(F32))


def feed_step(back, stream, out_weight, gain, router, upstream, after, context):
    stretch = stream.shape[0]
    last = upstream is not None
    operands = [
        context["place"],
        back,
        stream,
        out_weight,
        gain,
        router,
        context["ids"],
        context["turned_slots"],
    ]
    return run_kernel(
        functools.partial(feed_kernel, context["parts"] == 1, last),
        operands + ([upstream] if last else []),
        [
            ((stretch, D), F32),
            ((stretch, D), BF16),
            ((stretch, 2), F32),
            ((EXPERTS * SLOTS, 2 * D if last else D), BF16),
            ((D, stretch), BF16),
        ],
        (),
        after,
        flops=4 * stretch * D * D,
        name="feed",
    )


def add_up(parts):
    total = parts[0][...].astype(F32)
    for part in parts[1:]:
        total = total + part[...].astype(F32)
    return total


def layer_end_kernel(place_ref, *refs):
    returned_ref, middle_ref, gates_ref, slots_ref, gain_ref = refs[:5]
    parts = refs[5:9]
    stream_ref, gap_ref, normed_ref = refs[-3:]
    choices = [
        jnp.dot(row_table(slots_ref, c), returned_ref[...], preferred_element_type=F32)
        for c in range(2)
    ]
    gates = gates_ref[...]
    stream = middle_ref[...] + add_up(parts) + gates[:, 0:1] * choices[0]
    stream = stream + gates[:, 1:2] * choices[1]
    stream_ref[...] = stream
    gap_ref[...] = choices[0] - choices[1]
    normed_ref[...] = (stream * rms_factor(stream) * gain_ref[...]).astype(BF16)


def layer_end_step(returned, feed, parts, next_gain, after, context):
    shape = feed["middle"].shape
    return run_kernel(
        layer_end_kernel,
        [
            context["place"],
            returned,
            feed["middle"],
            feed["gates"],
            context["slots"],
            next_gain,
            *parts,
        ],
        [(shape, F32), (shape, F32), (shape, BF16)],
        (),
        after,
        flops=4 * shape[0] * D * returned.shape[0],
        name="layer_end",
    )


def feed_back_kernel(fixed, last, place_ref, *refs):
    (
        returned_ref,
        middle_ref,
        normed_ref,
        gates_ref,
        slots_ref,
        ids_ref,
        upstream_ref,
        gain_ref,
        router_ref,
        weight_ref,
    ) = refs[:10]
    parts = refs[10:14]
    outs = refs[-4:]
    tables = [row_table(slots_ref, c) for c in range(2)]
    gates = gates_ref[...]
    middle = middle_ref[...]
    upstream = upstream_ref[...].astype(F32)
    if last:
        choices = [
            jnp.dot(table, returned_ref[:, :D], preferred_element_type=F32) for table in tables
        ]
        gap = choices[0] - choices[1]
        sums = add_up(parts)
        output = middle + sums[:, :D] + gates[:, 0:1] * choices[0]
        refs[-5][...] = (output + gates[:, 1:2] * choices[1]).astype(BF16)
        grad_rows, shared_grad = returned_ref[:, D:], sums[:, D:]
    else:
        gap = refs[14][...]
        grad_rows, shared_grad = returned_ref[...], add_up(parts)
    lead = gates[:, 0:1] * gates[:, 1:2] * jnp.sum(gap * upstream, axis=1, keepdims=True)
    logit_grad = jnp.where(chosen(ids_ref, 0), lead, 0.0) - jnp.where(
        chosen(ids_ref, 1), lead, 0.0
    )
    high = logit_grad.astype(BF16)
    low = (logit_grad - high.astype(F32)).astype(BF16)
    router = router_ref[...]
    normed_grad = (
        shared_grad
        + contract(high, router, 1, 1)
        + contract(low, router, 1, 1)
        + jnp.dot(tables[0] + tables[1], grad_rows, preferred_element_type=F32)
    )
    factor = rms_factor(middle)
    norm_grad, _ = norm_back(middle, gain_ref[...], factor, normed_grad)
    middle_grad = upstream + norm_grad
    attn_grad = middle_grad.astype(BF16)
    middle_grad_ref, attn_ref, heads_ref, small_ref = outs
    middle_grad_ref[...] = middle_grad
    attn_ref[...] = attn_grad
    mixed_grad = contract(weight_ref[...], attn_grad, 1, 1).astype(BF16)
    used = set()
    for head in range(HEADS):
        slot = head_slot(head, fixed)
        used.add(slot)
        heads_ref[slot] = mixed_grad[head * HEAD : (head + 1) * HEAD]
    for slot in range(heads_ref.shape[0]):
        if slot not in used:
            heads_ref[slot] = jnp.zeros_like(heads_ref[slot])
    gain_grad = jnp.sum(normed_grad * middle * factor, axis=0, keepdims=True)
    normed = normed_ref[...]
    small = contract(normed, high, 0, 0) + contract(normed, low, 0, 0)
    lane = lax.broadcasted_iota(jnp.int32, small.shape, 1)
    small_ref[...] = jnp.where(lane == 1, jnp.broadcast_to(gain_grad, (128, D)).T, small)


def feed_back_step(returned, feed, upstream, parts, others, weights, last, after, context):
    stretch = feed["middle"].shape[0]
    shape = (stretch, D)
    return run_kernel(
        functools.partial(feed_back_kernel, context["parts"] == 1, last),
        [
            context["place"],
            returned,
            feed["middle"],
            feed["normed_ffn"],
            feed["gates"],
            context["slots"],
            context["ids"],
            upstream,
            weights["gain_two"],
            weights["router"],
            weights["out"],
            *parts,
            *others,
        ],
        ([(shape, BF16)] if last else [])
        + [
            (shape, F32),
            (shape, BF16),
            ((TEAM_SIZE * TEAM_SIZE, HEAD, stretch), BF16),
            ((D, 128), F32),
        ],
        (),
        after,
        flops=4 * stretch * D * D,
        name="feed_back",
    )


def layer_start_kernel(more, place_ref, *refs):
    stream_ref, middle_grad_ref, gain_ref = refs[:3]
    parts = refs[3:7]
    stream = stream_ref[...].astype(F32)
    norm_grad, _ = norm_back(stream, gain_ref[...], rms_factor(stream), add_up(parts))
    upstream = middle_grad_ref[...] + norm_grad
    if more:
        gates_ref, turned_ref, wide_ref, out_ref = refs[7:9] + refs[-3:-2] + refs[-1:]
        wide_ref[...] = upstream
        refs[-2][...] = upstream.astype(BF16)
        out_ref[...] = slots_of_grads(turned_ref, gates_ref[...], upstream)
    else:
        refs[-1][...] = upstream.astype(BF16)


def layer_start_step(stream, middle_grad, gain, parts, feed, context):
    shape = stream.shape
    more = feed is not None
    return run_kernel(
        functools.partial(layer_start_kernel, more),
        [
            context["place"],
            stream,
            middle_grad,
            gain,
            *parts,
            *([feed["gates"], context["turned_slots"]] if more else []),
        ],
        [(shape, F32), (shape, BF16), ((EXPERTS * SLOTS, D), BF16)] if more else [(shape, BF16)],
        flops=4 * shape[0] * D * EXPERTS * SLOTS if more else 0,
        name="layer_start",
    )


def shared_grads_kernel(unit, place_ref, *refs):
    team_ref, joint_ref, hidden_ref, grads_ref = refs[:4]
    joint_outs, down_outs = refs[4:6], refs[6:8]
    half = D // 2
    units = hidden_ref.shape[1] // 2
    for place, dp in enumerate((place_ref[3], 1 - place_ref[3])):
        joint_outs[place][...] = contract(
            team_ref[:, rows_at(dp, half)], joint_ref[...], 0, 0
        ).astype(BF16)
        down = contract(hidden_ref[:, rows_at(dp, units)], grads_ref[...], 0, 0).astype(BF16)
        out = down_outs[place]
        for block in range(units // unit):
            low, high = block * unit, (block + 1) * unit
            at, end = block * half * unit // units, (block + 1) * half * unit // units
            out[at : at + unit] = down[low:high]
            out[at + unit : end] = jnp.zeros((end - at - unit, D), BF16)


def shared_grads_step(team, joint_grad, hidden, grad_team, after, context):
    return run_kernel(
        functools.partial(shared_grads_kernel, FF // lax.axis_size(ALL)),
        [context["place"], team, joint_grad, hidden, grad_team],
        [((D // 2, joint_grad.shape[1]), BF16)] * 2 + [((D // 2, D), BF16)] * 2,
        (),
        after,
        flops=2 * team.shape[0] * D * (joint_grad.shape[1] + D),
        name="shared_grads",
    )


def shared_grads(shared, after, context):
    team, grads, hidden, joint_grad = shared[-4:]
    return shared_grads_step(team, joint_grad, hidden, grads, after, context)


def out_grads_kernel(place_ref, mixed_ref, attn_ref, own_ref, other_ref):
    for out, dp in zip((own_ref, other_ref), (place_ref[3], 1 - place_ref[3])):
        out[...] = jnp.dot(
            mixed_ref[rows_at(dp, D // 2), :], attn_ref[...], preferred_element_type=F32
        ).astype(BF16)


def out_grads_step(mixed, attn_grad, after, context):
    return run_kernel(
        out_grads_kernel,
        [context["place"], mixed, attn_grad],
        [((D // 2, D), BF16)] * 2,
        (),
        after,
        flops=2 * mixed.shape[1] * D * D,
        name="out_grads",
    )


def feed_end_kernel(place_ref, *refs):
    layers_count = (len(refs) - 4) // 9
    pieces = refs[: 4 * layers_count]
    out_pieces = refs[4 * layers_count : 8 * layers_count]
    downs = refs[8 * layers_count : 9 * layers_count]
    joint_out, out_out, down_out, columns = refs[-4:]
    width = joint_out.shape[1]
    joint_width = pieces[0].shape[1]
    unit = down_out.shape[1]
    rest = joint_width // (2 * unit)
    for layer in range(layers_count):
        total = None
        for turn in range(4):
            columns[place_ref[0] ^ turn] = pieces[4 * layer + turn][...].astype(F32)
            part = out_pieces[4 * layer + turn][...].astype(F32)
            total = part if total is None else total + part
        out_out[layer] = total
        for member in range(4):
            rows = columns[member]
            for part in range(2):
                for block in range(rest):
                    low = (part * rest + block) * unit
                    at = part * (joint_out.shape[2] // 2) + (block * 4 + member) * unit
                    joint_out[layer, :, at : at + unit] = rows[:, low : low + unit]
        down_out[layer] = downs[layer][...].astype(F32)


def qkv_end_kernel(place_ref, *refs):
    pieces = refs[:-3]
    qkv_out, small_out, columns = refs[-3:]
    edge = TEAM_HEADS * 3 * HEAD
    for layer in range(qkv_out.shape[0]):
        small = None
        for turn in range(4):
            piece = pieces[4 * layer + turn][...].astype(F32)
            columns[place_ref[0] ^ turn] = piece
            part = piece[:, edge:]
            small = part if small is None else small + part
        small_out[layer] = small
        for member in range(4):
            rows = columns[member]
            for head in range(TEAM_HEADS):
                for part in range(3):
                    low = (head * 3 + part) * HEAD
                    at = part * D + (member * TEAM_HEADS + head) * HEAD
                    qkv_out[layer, :, at : at + HEAD] = rows[:, low : low + HEAD]


def logistic(values):
    return 0.5 * jnp.tanh(0.5 * values) + 0.5


def swiglu_back(gate_pre, up_pre, hidden_grad):
    sigmoid_gate = logistic(gate_pre)
    silu_gate = gate_pre * sigmoid_gate
    gate_grad = hidden_grad * up_pre * (sigmoid_gate + silu_gate * (1.0 - sigmoid_gate))
    up_grad = hidden_grad * silu_gate
    return (gate_grad.astype(BF16), up_grad.astype(BF16))


def swiglu(gate_pre, up_pre):
    return (gate_pre * logistic(gate_pre) * up_pre).astype(BF16)


def expert_kernel(forward, backward, *refs):
    inputs = 1 + backward
    rows_ref, grads_ref = refs[0], refs[inputs - 1]
    gate_ref, up_ref, down_ref, out_ref, total = refs[inputs:]
    step = pl.program_id(0)
    rows = rows_ref[...]
    gate, up, down = gate_ref[0, 0], up_ref[0, 0], down_ref[0, 0]
    gate_pre = jnp.dot(rows, gate, preferred_element_type=F32)
    up_pre = jnp.dot(rows, up, preferred_element_type=F32)
    terms = []
    if forward:
        terms.append(jnp.dot(swiglu(gate_pre, up_pre), down, preferred_element_type=F32))
    if backward:
        hidden_grad = contract(grads_ref[...], down, 1, 1).astype(BF16).astype(F32)
        gate_grad, up_grad = swiglu_back(gate_pre, up_pre, hidden_grad)
        terms.append(contract(gate_grad, gate, 1, 1) + contract(up_grad, up, 1, 1))

    @pl.when(step == 0)
    def _():
        for i, term in enumerate(terms):
            total[:, i * D : (i + 1) * D] = term

    @pl.when(step > 0)
    def _():
        for i, term in enumerate(terms):
            total[:, i * D : (i + 1) * D] += term

    @pl.when(step == pl.num_programs(0) - 1)
    def _():
        out_ref[...] = total[...].astype(BF16)


def run_expert(layer, joint, down, rows, grads, forward, after=()):
    half = joint.shape[3] // 2
    chunk = min(512, half)
    chunks = half // chunk
    given = [rows] + ([grads] if grads is not None else [])
    count = rows[0].shape[0]
    width = D * (int(forward) + int(grads is not None))
    drop = len(given) + 3
    body = functools.partial(expert_kernel, forward, grads is not None)
    return pl.pallas_call(
        lambda *refs: body(*refs[:drop], *refs[drop + len(after) :]),
        grid=(chunks,),
        in_specs=[
            *[pl.BlockSpec((count, D), lambda i, at=at: (0, at)) for _, at in given],
            pl.BlockSpec((1, 1, D, chunk), lambda i: (layer, 0, 0, i)),
            pl.BlockSpec((1, 1, D, chunk), lambda i: (layer, 0, 0, chunks + i)),
            pl.BlockSpec((1, 1, chunk, D), lambda i: (layer, 0, i, 0)),
            *[ANYWHERE] * len(after),
        ],
        out_specs=pl.BlockSpec((count, width), lambda i: (0, 0)),
        out_shape=jax.ShapeDtypeStruct((count, width), BF16),
        scratch_shapes=[pltpu.VMEM((count, width), F32)],
        compiler_params=vmem(
            4 * len(given) * count * D + 12 * D * chunk + 8 * count * width + 32 * count * chunk
        ),
        cost_estimate=cost(
            2 * count * D * half * (2 + int(forward) + 3 * int(grads is not None)),
            6 * D * half + 4 * count * width,
            count * half,
        ),
        name="expert_forward" if grads is None else "expert_both" if forward else "expert_back",
    )(*[array for array, _ in given], joint, joint, down, *after)


def expert_grad_kernel(place_ref, own_rows, own_grads, other_rows, other_grads, gate_ref, up_ref, down_ref, *refs):
    joint_out, down_out, rows_all, grads_all, turned, hold = refs[-6:]
    count = own_rows.shape[0]

    @pl.when((pl.program_id(0) == 0) & (pl.program_id(1) == 0))
    def _():
        own = rows_at(place_ref[3], count)
        other = rows_at(1 - place_ref[3], count)
        rows_all[own, :] = own_rows[...]
        rows_all[other, :] = other_rows[...]
        grads_all[own, :] = own_grads[...]
        grads_all[other, :] = other_grads[...]
        turned[...] = rows_all[...].T

    @pl.when(pl.program_id(1) == 0)
    def _():
        rows = rows_all[...]
        grads = grads_all[...]
        gate_pre = jnp.dot(rows, gate_ref[0, 0], preferred_element_type=F32)
        up_pre = jnp.dot(rows, up_ref[0, 0], preferred_element_type=F32)
        hidden_grad = contract(grads, down_ref[0, 0], 1, 1).astype(BF16).astype(F32)
        gate_grad, up_grad = swiglu_back(gate_pre, up_pre, hidden_grad)
        hold[...] = up_grad
        down_out[0, 0] = contract(swiglu(gate_pre, up_pre), grads, 0, 0)
        joint_out[0, 0] = jnp.dot(turned[...], gate_grad, preferred_element_type=F32)

    @pl.when(pl.program_id(1) == 1)
    def _():
        joint_out[0, 0] = jnp.dot(turned[...], hold[...], preferred_element_type=F32)


def expert_grads(layer, quarters, own, other, joint, down, before, later_than, context):
    half = joint.shape[3] // 2
    given = [*own, *other]
    count = given[0][0].shape[0]
    chunk = min(512 if count <= 512 else 128, half // 4)
    chunks = half // chunk
    first, steps = [quarter * chunks // 4 for quarter in quarters]
    in_specs = [
        IN_SMEM,
        *[pl.BlockSpec((count, D), lambda i, h, at=at: (0, at)) for _, at in given],
        pl.BlockSpec((1, 1, D, chunk), lambda i, h: (layer, 0, 0, first + i)),
        pl.BlockSpec((1, 1, D, chunk), lambda i, h: (layer, 0, 0, chunks + first + i)),
        pl.BlockSpec((1, 1, chunk, D), lambda i, h: (layer, 0, first + i, 0)),
    ]
    operands = [context["place"]] + [array for array, _ in given] + [joint, joint, down]
    aliases = {}
    if before is not None:
        aliases = {len(operands): 0, len(operands) + 1: 1}
        operands += list(before)
    operands += later_than
    in_specs += [ANYWHERE] * (len(operands) - len(in_specs))
    return pl.pallas_call(
        expert_grad_kernel,
        grid=(steps, 2),
        in_specs=in_specs,
        out_specs=[
            pl.BlockSpec((1, 1, D, chunk), lambda i, h: (layer, 0, 0, h * chunks + first + i)),
            pl.BlockSpec((1, 1, chunk, D), lambda i, h: (layer, 0, first + i, 0)),
        ],
        out_shape=[
            jax.ShapeDtypeStruct(joint.shape, F32),
            jax.ShapeDtypeStruct(down.shape, F32),
        ],
        scratch_shapes=[
            pltpu.VMEM((2 * count, D), BF16),
            pltpu.VMEM((2 * count, D), BF16),
            pltpu.VMEM((D, 2 * count), BF16),
            pltpu.VMEM((2 * count, chunk), BF16),
        ],
        input_output_aliases=aliases,
        compiler_params=vmem(30 * count * D + 28 * D * chunk + 56 * count * chunk),
        cost_estimate=cost(
            24 * count * D * chunk * steps, 18 * D * chunk * steps, 2 * count * chunk * steps
        ),
        name="expert_grads",
    )(*operands)


def nothing(*refs):
    pass


def later(rows, *others):
    return pl.pallas_call(
        nothing,
        in_specs=[pl.BlockSpec(memory_space=pl.ANY)] * (1 + len(others)),
        out_specs=pl.BlockSpec(memory_space=pl.ANY),
        out_shape=jax.ShapeDtypeStruct(rows.shape, rows.dtype),
        input_output_aliases={0: 0},
        name="later",
    )(rows, *others)


def route_slots(route_ids):
    stretch_rows = route_ids.shape[0]
    experts_row = jnp.arange(EXPERTS, dtype=jnp.int32)
    route_hits = (route_ids[:, :, None] == experts_row[None, None, :]).astype(jnp.int32)
    running = jnp.cumsum(route_hits.reshape(2 * stretch_rows, EXPERTS), axis=0) - 1
    running = running.reshape(stretch_rows, 2, EXPERTS)
    return route_ids * SLOTS + jnp.sum(route_hits * running, axis=2)


def send_rows(outgoing, split_count):
    width = outgoing.shape[1]
    outgoing = outgoing.reshape(EXPERTS, SLOTS, width)
    if split_count > 1:
        outgoing = jnp.repeat(outgoing, split_count, axis=0)
    return exchange(outgoing, SEQ).reshape(-1, width)


def return_rows(rows, split_count):
    width = rows.shape[1]
    returned = exchange(rows.reshape(-1, SLOTS, width), SEQ)
    if split_count > 1:
        returned = (
            returned.reshape(EXPERTS, split_count, SLOTS, width).astype(F32).sum(axis=1)
        ).astype(BF16)
    return returned.reshape(EXPERTS * SLOTS, width)


def shared_kernel(forward, backward, place_ref, *refs):
    rows_refs, refs = refs[:4], refs[4:]
    if backward:
        grads_refs, refs = refs[:4], refs[4:]
    joint_ref, down_ref = refs[:2]
    parts, outs = refs[2:6], refs[6:]
    stretch = rows_refs[0].shape[0]
    team = jnp.concatenate([ref[...] for ref in rows_refs], axis=0)
    joint, down = joint_ref[...], down_ref[...]
    half = joint.shape[1] // 2
    pre = jnp.dot(team, joint, preferred_element_type=F32)
    gate_pre, up_pre = pre[:, :half], pre[:, half:]
    hidden = swiglu(gate_pre, up_pre)
    results = []
    if forward:
        results.append(jnp.dot(hidden, down, preferred_element_type=F32))
    if backward:
        grads = jnp.concatenate([ref[...] for ref in grads_refs], axis=0)
        hidden_grad = contract(grads, down, 1, 1).astype(BF16).astype(F32)
        gate_grad, up_grad = swiglu_back(gate_pre, up_pre, hidden_grad)
        joint_grad = jnp.concatenate([gate_grad, up_grad], axis=1)
        results.append(contract(joint_grad, joint, 1, 1))
        team_out, grads_out, hidden_out, joint_out = outs
        team_out[...] = team
        grads_out[...] = grads
        hidden_out[...] = hidden
        joint_out[...] = joint_grad
    for place, result in enumerate(results):
        for turn in range(4):
            parts[turn][:, place * D : (place + 1) * D] = result[
                turn * stretch : (turn + 1) * stretch
            ].astype(BF16)


def shared_step(rows, grads, joint, down, forward, after, context):
    stretch = rows[0].shape[0]
    group = TEAM_SIZE * stretch
    backward = grads is not None
    outputs = [((stretch, D * (int(forward) + int(backward))), BF16)] * 4
    if backward:
        outputs += [
            ((group, D), BF16),
            ((group, D), BF16),
            ((group, down.shape[0]), BF16),
            ((group, joint.shape[1]), BF16),
        ]
    return run_kernel(
        functools.partial(shared_kernel, forward, backward),
        [context["place"], *rows, *(grads if backward else []), joint, down],
        outputs,
        (),
        after,
        flops=2 * group * joint.size * (3 if backward else 1),
        name="shared",
        room=16,
    )


def z_turn(pieces, out):
    count = len(pieces)
    arrived = [pieces[0]]
    for turn in range(1, count):
        pairs = []
        for z in range(count):
            for core in range(2):
                to = (z + turn) % count
                if 0 <= (to if out else z) - core < TEAM_HEADS:
                    pairs.append((z * 2 + core, to * 2 + core))
        arrived.append(lax.ppermute(pieces[turn], ("z", "core"), pairs))
    return arrived


def to_heads(pieces, context):
    parts = context["parts"]
    if parts == 1:
        return z_turn(pieces, True)
    heads = jnp.stack([*pieces, jnp.zeros_like(pieces[0])])
    return [exchange(jnp.repeat(heads, parts, axis=0), "z")]


def attention_forward(arrived, after, context, stretch):
    parts = context["parts"]
    if parts == 1:
        rows, attended, wide, logs = fixed_attention(
            arrived, context["spans"][3], context["place"], stretch, after
        )
        return (exchange(attended, SEQ), (rows, wide, logs))
    (rows,) = arrived
    attended, wide, logs = attention(rows, context["spans"], stretch)
    count = context["deep"] * TEAM_SIZE
    attended = lax.dynamic_update_slice_in_dim(
        jnp.zeros((count, HEAD, stretch), BF16), attended, context["part"] * (count // parts), 0
    )
    back = exchange(attended, SEQ).reshape(TEAM_SIZE, parts, TEAM_SIZE, HEAD, stretch)
    back = back.astype(F32).sum(axis=1).astype(BF16)
    return (back.reshape(-1, HEAD, stretch), (rows, wide, logs))


def grads_to_heads(head_grads, context):
    parts = context["parts"]
    if parts > 1:
        stretch = head_grads.shape[2]
        head_grads = head_grads.reshape(TEAM_SIZE, TEAM_SIZE, HEAD, stretch)
        head_grads = jnp.repeat(head_grads, parts, axis=0).reshape(-1, HEAD, stretch)
    return exchange(head_grads, SEQ)


def attention_backward(grads, saved, after, context):
    parts = context["parts"]
    rows, wide, logs = saved
    if parts == 1:
        pieces = fixed_attention_back(
            rows, context["spans"][3], grads, wide, logs, context["place"], after
        )
        return (z_turn(pieces, False), pieces[0])
    count = grads.shape[0] // parts
    grads = lax.dynamic_slice_in_dim(grads, context["part"] * count, count, 0)
    rows_grad = attention_back(rows, context["spans"], grads, wide, logs, after)
    back = exchange(rows_grad, "z")
    back = back.reshape((TEAM_SIZE, parts) + back.shape[1:]).astype(F32).sum(axis=1).astype(BF16)
    return ([back[i] for i in range(TEAM_HEADS)], rows_grad)


def team_pieces(rows, member):
    pieces = rows.reshape(TEAM_SIZE, -1, rows.shape[1])
    parts = [lax.dynamic_index_in_dim(pieces, member ^ k, 0, keepdims=False) for k in range(4)]
    return [parts[0]] + [from_member(parts[k], k) for k in (1, 2, 3)]


def team_turn(rows, member):
    return in_order(jnp.stack(team_pieces(rows, member)), member)


def swap(rows):
    return lax.ppermute(rows, "dp", SWAP)


def beside(pairs):
    return jnp.concatenate(
        [(own.astype(F32) + other.astype(F32)).astype(BF16) for own, other in pairs], axis=1
    )


def z_sum(rows):
    return lax.psum_scatter(rows, "z", scatter_dimension=0, tiled=True)


def z_sum_direct(rows):
    count = lax.axis_size("z")
    if count > 4:
        return z_sum(rows)
    at = lax.axis_index("z")
    blocks = rows.reshape(count, -1, rows.shape[1])
    total = lax.dynamic_index_in_dim(blocks, at, 0, keepdims=False).astype(F32)
    for turn in range(1, count):
        block = lax.dynamic_index_in_dim(blocks, (at + turn) % count, 0, keepdims=False)
        block = lax.ppermute(block, "z", [(i, (i + turn) % count) for i in range(count)])
        total = total + block.astype(F32)
    return total.astype(BF16)


def to_team(parts):
    return [parts[0]] + [from_member(parts[k], k) for k in (1, 2, 3)]


def from_team(rows):
    return [rows] + [from_member(rows, k) for k in (1, 2, 3)]


def spread(rows, axes):
    count = lax.axis_size(axes)
    copies = jnp.broadcast_to(rows[None], (count,) + rows.shape)
    return exchange(copies, axes).reshape((-1,) + rows.shape[1:])


def dp_rows(rows):
    other = lax.ppermute(rows, "dp", SWAP)
    first = lax.axis_index("dp") == 0
    return jnp.concatenate([jnp.where(first, rows, other), jnp.where(first, other, rows)], axis=0)


def small_weights(gain_attn, gain_ffn, w_router):
    small = jnp.concatenate([gain_attn[:, :, None], gain_ffn[:, :, None], w_router], axis=2)
    small = small.transpose(1, 0, 2).reshape(gain_attn.shape[1], -1)
    return jnp.broadcast_to(small[None], (TEAM_SIZE,) + small.shape)


def split_small(smalls):
    weights = []
    for layer in range(LAYERS):
        part = smalls[:, layer * (2 + EXPERTS) : (layer + 1) * (2 + EXPERTS)]
        gains = part[:, :2].astype(F32).T
        weights.append(
            dict(
                gain_one=gains[0:1],
                gain_two=gains[1:2],
                router=jnp.pad(part, ((0, 0), (0, 128 - part.shape[1]))),
            )
        )
    return weights


def qkv_columns(w_qkv):
    width = w_qkv.shape[0]
    blocks = w_qkv.reshape(width, 3, TEAM_SIZE, TEAM_HEADS, HEAD)
    return blocks.transpose(2, 0, 3, 1, 4).reshape(TEAM_SIZE, width, -1)


def joint_columns(shared_gate_up):
    total = lax.axis_size(ALL)
    width = shared_gate_up.shape[0]
    blocks = shared_gate_up.reshape(width, 2, total // TEAM_SIZE, TEAM_SIZE, FF // total)
    return blocks.transpose(3, 0, 1, 2, 4).reshape(TEAM_SIZE, width, -1)


def padded_rows(shared_down):
    total = lax.axis_size(ALL)
    return jnp.pad(shared_down, ((0, TEAM_SIZE * D // total - shared_down.shape[0]), (0, 0)))


def down_rows(padded):
    total = lax.axis_size(ALL)
    return padded.reshape(total // TEAM_SIZE, -1, D)[:, : FF // total].reshape(-1, D)


def folded(w_out):
    return w_out.reshape(TEAM_SIZE * w_out.shape[0], -1)


def out_rows(rows, member):
    width = D // lax.axis_size(ALL)
    rows = dp_rows(rows.reshape(-1, D))
    rows = in_order(jnp.stack(from_team(rows)), member)
    return rows.reshape(TEAM_SIZE, -1, width, D).transpose(1, 0, 2, 3).reshape(D, D)


def side_by_side(*arrays):
    return jnp.concatenate(arrays, axis=2)


def copies(rows):
    return jnp.broadcast_to(rows[None], (TEAM_SIZE,) + rows.shape)


def z_gather(rows):
    return lax.all_gather(rows, "z", axis=0, tiled=True)


def rest_gather(rows):
    return lax.all_gather(rows, REST, axis=0, tiled=True)


def dp_gather(rows, edges, token):
    parts = []
    for low, high in zip(edges, edges[1:]):
        token = dp_rows(later(rows[:, low:high], token))
        parts.append(token)
    return parts


def layers(
    x_in,
    cotangent,
    gain_attn,
    w_qkv,
    w_out,
    gain_ffn,
    w_router,
    shared_gate_up,
    shared_down,
    joint,
    down,
    context,
):
    split_count = context["split_count"]
    member = context["member"]
    stretch = x_in.shape[0]
    last = LAYERS - 1

    width = w_qkv.shape[1]
    qkv_width, joint_width = 3 * D // TEAM_SIZE, 2 * FF // TEAM_SIZE
    small = small_weights(gain_attn, gain_ffn, w_router)
    rows = side_by_side(qkv_columns(w_qkv[0]), small).reshape(TEAM_SIZE * width, -1)
    rows = team_turn(rows, member).reshape(TEAM_SIZE * width, -1)
    first_rows = spread(rows, "z")
    rows = exchange(joint_columns(shared_gate_up[0]), TEAM).reshape(TEAM_SIZE * width, -1)
    main_rows = jnp.concatenate([folded(w_out[0]), rows, padded_rows(shared_down[0])], axis=1)
    main_rows = z_gather(later(main_rows, first_rows))
    if LAYERS > 1:
        rows = side_by_side(
            *[qkv_columns(w_qkv[layer]) for layer in range(1, LAYERS)],
            *[joint_columns(shared_gate_up[layer]) for layer in range(1, LAYERS)],
        )
        rows = team_turn(rows.reshape(TEAM_SIZE * width, -1), member)
        rows = rows.reshape(TEAM_SIZE * width, -1)
        edge = (LAYERS - 1) * qkv_width
        more_edges = [edge]
        for size in (D // TEAM_SIZE, joint_width):
            more_edges.append(more_edges[-1] + (LAYERS - 1) * size)
        more_rows = jnp.concatenate(
            [
                rows[:, :edge],
                *[folded(w_out[layer]) for layer in range(1, LAYERS)],
                rows[:, edge:],
                *[padded_rows(shared_down[layer]) for layer in range(1, LAYERS)],
            ],
            axis=1,
        )
    first_rows = dp_rows(first_rows)
    weights = split_small(first_rows[:, qkv_width:])
    weights[0]["qkv"] = first_rows[:, :qkv_width]

    stream = x_in
    rows = from_team(x_in)
    grad_rows = from_team(cotangent)
    feeds = []
    for layer in range(LAYERS):
        mine = weights[layer]
        *pieces, team = qkv_step(
            rows,
            layer > 0,
            mine["gain_one"],
            mine["qkv"],
            (),
            context,
        )
        if layer == 0:
            at, held_rows = 0, main_rows
            edges = [0, D // TEAM_SIZE, D // TEAM_SIZE + joint_width]
        else:
            at, held_rows, edges = layer - 1, more_rows, more_edges
        columns = [
            held_rows[:, low + at * size : low + (at + 1) * size]
            for low, size in zip(edges, (D // TEAM_SIZE, joint_width, D))
        ]
        after = grad_rows[1:] if layer == last else []
        if layer > 0:
            after = [*after, feeds[0]["other"]]
        mine["out"] = out_rows(later(columns[0], pieces[0]), member)
        at_heads = to_heads(pieces, context)
        back, attended = attention_forward(at_heads, after, context, stretch)
        if layer > 0:
            mine["joint"] = dp_rows(later(columns[1], attended[1]))
        if layer == 0 and LAYERS > 1:
            more_rows = z_gather(later(more_rows, attended[1]))
        middle, normed_ffn, gates, outgoing, mixed = feed_step(
            back,
            stream,
            mine["out"],
            mine["gain_two"],
            mine["router"],
            cotangent if layer == last else None,
            [mine["joint"]] if layer > 0 else [],
            context,
        )
        if layer == 0:
            mine["joint"] = dp_rows(later(columns[1], normed_ffn))
        down_padded = dp_rows(later(columns[2], normed_ffn))
        mine["down"] = down_rows(down_padded)
        arrived = send_rows(outgoing, split_count)
        other = swap(arrived)
        ffn_rows = from_team(normed_ffn)
        def branch(after):
            return shared_step(
                ffn_rows,
                grad_rows if layer == last else None,
                mine["joint"],
                mine["down"],
                True,
                after,
                context,
            )

        if layer == last:
            shared = branch([])
        returned = run_expert(
            layer,
            joint,
            down,
            (arrived, 0),
            (arrived, 1) if layer == last else None,
            True,
            [shared[0]] if layer == last else [*ffn_rows[1:], mine["joint"]],
        )
        if layer < last:
            shared = branch([returned])
        if layer == 0:
            for i in range(1, LAYERS):
                columns = more_rows[:, (i - 1) * qkv_width : i * qkv_width]
                weights[i]["qkv"] = dp_rows(later(columns, returned))
        returned = return_rows(returned, split_count)
        feed = dict(
            stream=stream,
            team=team,
            attended=attended,
            middle=middle,
            normed_ffn=normed_ffn,
            gates=gates,
            mixed=mixed,
            arrived=arrived,
            other=other,
            ffn_rows=ffn_rows,
        )
        feeds.append(feed)
        parts = to_team(shared[:4])
        if layer < last:
            stream, feed["gap"], normed = layer_end_step(
                returned, feed, parts, weights[layer + 1]["gain_one"], [weights[layer + 1]["qkv"]], context
            )
            rows = from_team(normed)

    upstream = cotangent
    terms = None
    unit = FF // lax.axis_size(ALL)
    feed_parts, head_parts = [None] * LAYERS, [None] * LAYERS
    for layer in reversed(range(LAYERS)):
        feed, mine = feeds[layer], weights[layer]
        arrived, other = feed["arrived"], feed["other"]
        if layer == last:
            grads, other_grads = (arrived, 1), (other, 1)
            shared_parts = shared_grads(shared, [parts[2]], context)
            output, middle_grad, attn_grad, head_grads, small = feed_back_step(
                returned,
                feed,
                upstream,
                parts,
                [],
                mine,
                True,
                [shared_parts[1], shared_parts[3]],
                context,
            )
        else:
            arrived_grad = send_rows(outgoing_grads, split_count)
            grads, other_grads = (arrived_grad, 0), (swap(arrived_grad), 0)
            grad_rows = from_team(upstream_rows)
            waited = [(waited[0][0], later(waited[0][1], grad_rows[2])), *waited[1:]]
            waited_sum = z_sum(beside(waited))
            waiting = [(own, swap(rows)) for own, rows in waiting]
            shared = shared_step(
                feed["ffn_rows"],
                grad_rows,
                mine["joint"],
                mine["down"],
                False,
                [terms[1]],
                context,
            )
            returned = run_expert(
                layer,
                joint,
                down,
                (arrived, 0),
                (arrived_grad, 0),
                False,
                [shared[0], *[rows for _, rows in waiting]],
            )
            returned = return_rows(returned, split_count)
            parts = to_team(shared[:4])
            shared_parts = shared_grads(shared, [parts[2], other_grads[0]], context)
            waiting = [(own, later(rows, parts[1], waited_sum)) for own, rows in waiting]
            waiting_sum = z_sum(beside(waiting))
            middle_grad, attn_grad, head_grads, small = feed_back_step(
                returned,
                feed,
                upstream,
                parts,
                [feed["gap"]],
                mine,
                False,
                [shared_parts[1], shared_parts[3], waited_sum],
                context,
            )
            terms = expert_grads(*rest_of_terms, terms, [attn_grad, other_grads[0]], context)
        joint_arrived, down_arrived = swap(shared_parts[1]), swap(shared_parts[3])
        at_heads = grads_to_heads(head_grads, context)
        if layer == 0:
            out_own, out_other = out_grads_step(feed["mixed"], attn_grad, [], context)
            out_arrived = swap(out_other)
            halves = [(shared_parts[0], later(joint_arrived, out_other))]
            shared_sum = z_sum(beside([*halves, (shared_parts[2], down_arrived)]))
        pieces, token = attention_backward(
            at_heads,
            feed["attended"],
            [waiting_sum, joint_arrived, down_arrived, terms[1]] if layer < last else [],
            context,
        )
        if layer > 0:
            out_own, out_other = out_grads_step(
                feed["mixed"], attn_grad, [pieces[min(1, len(pieces) - 1)]], context
            )
            out_arrived = swap(out_other)
        held = ((arrived, 0), grads), ((other, 0), other_grads)
        terms = expert_grads(layer, (0, 2), *held, joint, down, terms, [token], context)
        results = qkv_back_step(
            pieces,
            mine["qkv"],
            feed["team"],
            mine["gain_one"],
            small,
            True,
            [terms[1]] + ([down_arrived, joint_arrived] if layer > 0 else [out_arrived]),
            context,
        )
        normed_parts, packed = to_team(results[:4]), results[4:]
        if layer > 0:
            waiting = [packed]
            waited = [
                (out_own, out_arrived),
                (shared_parts[2], down_arrived),
                (shared_parts[0], joint_arrived),
            ]
            upstream, upstream_rows, outgoing_grads = layer_start_step(
                feed["stream"], middle_grad, mine["gain_one"], normed_parts, feeds[layer - 1], context
            )
            terms = expert_grads(
                layer, (2, 1), *held, joint, down, terms, [outgoing_grads], context
            )
            rest_of_terms = (layer, (3, 1), *held, joint, down)
        else:
            (upstream_rows,) = layer_start_step(
                feed["stream"], middle_grad, mine["gain_one"], normed_parts, None, context
            )
            qkv_arrived = swap(packed[1])
            out_sum = z_sum(beside([(out_own, later(out_arrived, packed[0]))]))
        if layer < last:
            head_parts[layer + 1] = team_pieces(waiting_sum, member)
            feed_parts[layer + 1][1] = team_pieces(waited_sum[:, :D], member)
            feed_parts[layer + 1][2] = waited_sum[:unit, D : 2 * D]
            feed_parts[layer + 1][0] = team_pieces(waited_sum[:, 2 * D :], member)
        feed_parts[layer] = [None] * 3
        if layer == 0:
            feed_parts[0][0] = team_pieces(shared_sum[:, :joint_width], member)
            feed_parts[0][2] = shared_sum[:unit, joint_width:]
        if layer == 0:
            terms = expert_grads(
                layer, (2, 2), *held, joint, down, terms, [packed[0], shared_sum], context
            )
            early = later(qkv_arrived, terms[1], *normed_parts[1:])
            qkv_sum = z_sum_direct(beside([(packed[0], early)]))
            head_parts[0] = team_pieces(qkv_sum, member)
            feed_parts[0][1] = team_pieces(later(out_sum, terms[1]), member)
    joint_sum, out_sum, down_sum = run_kernel(
        feed_end_kernel,
        [
            context["place"],
            *[piece for pieces, _, _ in feed_parts for piece in pieces],
            *[piece for _, pieces, _ in feed_parts for piece in pieces],
            *[rows for _, _, rows in feed_parts],
        ],
        [
            ((LAYERS, width, 2 * FF), F32),
            ((LAYERS, width, D), F32),
            ((LAYERS, unit, D), F32),
        ],
        [((TEAM_SIZE, width, joint_width), F32)],
        name="feed_end",
    )
    qkv_sum, small_sum = run_kernel(
        qkv_end_kernel,
        [context["place"], *[piece for pieces in head_parts for piece in pieces]],
        [((LAYERS, width, 3 * D), F32), ((LAYERS, width, 64), F32)],
        [((TEAM_SIZE, width, qkv_width + 64), F32)],
        name="qkv_end",
    )
    dense = (
        small_sum[:, :, 0],
        qkv_sum,
        out_sum,
        small_sum[:, :, 1],
        small_sum[:, :, 2 : 2 + EXPERTS],
        joint_sum,
        down_sum,
    )
    return (output, upstream_rows, dense, terms)


def query_spans(block_row, group, part, parts):
    length = block_row.shape[0]
    limit = jnp.sum((block_row[None, :] <= block_row[:, None]).astype(jnp.int32), axis=1)
    tiles = length // QUERY_TILE // parts
    base = part * tiles
    ends = lax.dynamic_slice_in_dim(limit.reshape(-1, QUERY_TILE), base, tiles, 0)
    full = ends[:, 0] // group
    some = (ends[:, -1] + group - 1) // group
    base = jnp.full((1,), base, jnp.int32)
    return (full, some, base, limit[None, :], tiles, parts)


def local(
    x_in,
    block_ids,
    expert_ids,
    cotangent,
    gain_attn,
    w_qkv,
    w_out,
    gain_ffn,
    w_router,
    shared_gate_up,
    shared_down,
    expert_gate_up,
    expert_down,
):
    stretch = x_in.shape[1]
    group = TEAM_SIZE * stretch
    deep = lax.axis_size("z")
    parts = max(1, deep // TEAM_SIZE)
    at = lax.axis_index("z")
    member = lax.axis_index("core") * lax.axis_size("ulysses") + lax.axis_index("ulysses")
    half_size = HEAD // 2
    spacing = 10000.0 ** (-jnp.arange(half_size).astype(F32) * 2.0 / HEAD)
    positions = (at * group + jnp.arange(group, dtype=jnp.int32)).astype(F32)
    angles = spacing[:, None] * positions[None, :]
    part = at % parts
    slots = route_slots(expert_ids[0])
    place = [member, at, lax.axis_index("core"), lax.axis_index("dp")]
    context = dict(
        member=member,
        place=jnp.stack(place).astype(jnp.int32),
        cosine=jnp.cos(angles),
        sine=jnp.sin(angles),
        ids=expert_ids[0],
        slots=slots,
        turned_slots=slots.T,
        parts=parts,
        part=part,
        deep=deep,
        split_count=deep * TEAM_SIZE // EXPERTS,
        spans=query_spans(block_ids[0], group, part, parts),
    )
    output, grad_x, dense, terms = layers(
        x_in[0],
        cotangent[0],
        gain_attn,
        w_qkv,
        w_out,
        gain_ffn,
        w_router,
        shared_gate_up,
        shared_down,
        expert_gate_up,
        expert_down,
        context,
    )
    return (output[None], grad_x[None], *dense, *terms)


def solution(mesh):
    dp, blk, ulysses = mesh.devices.shape
    grid = Mesh(mesh.devices.reshape(dp, blk // 2, 2, ulysses), ALL)
    rows = P("dp", SEQ, None)
    in_specs = (
        rows,
        P("dp", None),
        rows,
        rows,
        P(None, ALL),
        P(None, ALL, None),
        P(None, ALL, None),
        P(None, ALL),
        P(None, ALL, None),
        P(None, ALL, None),
        P(None, ALL, None),
        P(None, SEQ, None, None),
        P(None, SEQ, None, None),
    )
    out_specs = (
        rows,
        rows,
        P(None, ALL),
        P(None, ALL, None),
        P(None, ALL, None),
        P(None, ALL),
        P(None, ALL, None),
        P(None, ALL, None),
        P(None, ALL, None),
        P(None, SEQ, None, None),
        P(None, SEQ, None, None),
    )
    return jax.shard_map(local, mesh=grid, in_specs=in_specs, out_specs=out_specs, check_vma=False)
```

```python
import functools
import math

import jax
import jax.numpy as jnp
from jax import lax
from jax.experimental import pallas as pl
from jax.experimental.pallas import tpu as pltpu
from jax.sharding import Mesh
from jax.sharding import PartitionSpec as P

D = 768
HEADS = 12
HEAD = 64
FF = 2048
EXPERTS = 16
LAYERS = 2
MOST = 21
SLOTS = -(-MOST // 8) * 8
TEAM_SIZE = 4
TEAM_HEADS = HEADS // TEAM_SIZE

ALL = ("dp", "z", "core", "ulysses")
SEQ = ("z", "core", "ulysses")
TEAM = ("core", "ulysses")
REST = ("dp", "z")

NORM_EPS = 1e-06
NEG_BIG = -1e30
PRECISE = lax.Precision.HIGHEST
F32 = jnp.float32
BF16 = jnp.bfloat16
QUERY_TILE = 256
MIB = 1024 * 1024


def vmem(size):
    return pltpu.CompilerParams(vmem_limit_bytes=61 * MIB)


def cost(flops, moved, steps=0):
    return pl.CostEstimate(flops=flops, bytes_accessed=moved, transcendentals=steps)


def contract(left, right, left_dim, right_dim):
    return lax.dot_general(
        left, right, (((left_dim,), (right_dim,)), ((), ())), preferred_element_type=F32
    )


def exchange(rows, axes):
    return lax.all_to_all(rows, axes, split_axis=0, concat_axis=0, tiled=True)


SWAP = [(0, 1), (1, 0)]


def from_member(rows, turn):
    if turn == 1:
        return lax.ppermute(rows, "ulysses", SWAP)
    if turn == 2:
        return lax.ppermute(rows, "core", SWAP)
    return lax.ppermute(rows, TEAM, [(i, 3 - i) for i in range(4)])


def team_gather(rows):
    return jnp.stack([rows] + [from_member(rows, turn) for turn in (1, 2, 3)])


def in_order(stacked, member):
    turns = [jnp.equal(member, i) for i in range(4)]
    pieces = []
    for k in range(4):
        piece = stacked[k ^ 3]
        for i in range(3):
            piece = jnp.where(turns[i], stacked[k ^ i], piece)
        pieces.append(piece)
    return jnp.stack(pieces)


def team_sum(parts):
    total = parts[0].astype(F32)
    for turn in (1, 2, 3):
        total = total + from_member(parts[turn].astype(BF16), turn).astype(F32)
    return total


def rms_factor(stream):
    return lax.rsqrt(jnp.mean(stream * stream, axis=-1, keepdims=True) + NORM_EPS)


def norm_back(stream, gain, factor, upstream):
    weighted = upstream * gain
    inner_mean = jnp.mean(weighted * stream, axis=-1, keepdims=True)
    grad_stream = factor * weighted - stream * factor * factor * factor * inner_mean
    grad_gain = jnp.sum(upstream * stream * factor, axis=0)
    return (grad_stream, grad_gain)


def attention_kernel(full_ref, some_ref, base_ref, rows_ref, limit_ref, out_ref, wide_ref, log_ref, keys):
    span = rows_ref.shape[2]
    step = pl.program_id(0)
    per_block = span // QUERY_TILE

    @pl.when(step == 0)
    def _():
        for s in range(rows_ref.shape[0]):
            keys[s] = rows_ref[s, HEAD : 2 * HEAD, :].T

    tile = base_ref[0] + step
    lanes = pl.ds(pl.multiple_of((tile % per_block) * QUERY_TILE, QUERY_TILE), QUERY_TILE)
    queries = rows_ref[tile // per_block, 0:HEAD, lanes] * BF16(HEAD**-0.5)
    limit = limit_ref[...]
    key_index = lax.broadcasted_iota(jnp.int32, (span, QUERY_TILE), 0)

    def sweep(s, state, masked):
        highest, total, running = state
        scores = jnp.dot(keys[s], queries, preferred_element_type=F32)
        if masked:
            scores = jnp.where(key_index < limit - s * span, scores, NEG_BIG)
        raised = jnp.maximum(highest, jnp.max(scores, axis=0, keepdims=True))
        terms = jnp.exp(scores - raised)
        shrink = jnp.exp(highest - raised)
        total = total * shrink + jnp.sum(terms, axis=0, keepdims=True)
        running = running * shrink + jnp.dot(
            rows_ref[s, 2 * HEAD :, :], terms.astype(BF16), preferred_element_type=F32
        )
        return (raised, total, running)

    state = (
        jnp.full((1, QUERY_TILE), NEG_BIG, F32),
        jnp.zeros((1, QUERY_TILE), F32),
        jnp.zeros((HEAD, QUERY_TILE), F32),
    )
    state = lax.fori_loop(0, full_ref[step], lambda s, c: sweep(s, c, False), state)
    state = lax.fori_loop(full_ref[step], some_ref[step], lambda s, c: sweep(s, c, True), state)
    highest, total, running = state
    result = running / total
    log_ref[...] = highest + jnp.log(total)
    wide_ref[...] = result
    stretch = out_ref.shape[2]
    for i in range(QUERY_TILE // stretch):
        out_ref[i] = result[:, i * stretch : (i + 1) * stretch].astype(BF16)


def attention_back_kernel(
    full_ref, some_ref, base_ref, rows_ref, limit_ref, grad_ref, wide_ref, log_ref, *refs
):
    out_ref, keys, values, key_sum, value_sum = refs[-5:]
    span = rows_ref.shape[2]
    blocks = rows_ref.shape[0]
    step = pl.program_id(0)
    per_block = span // QUERY_TILE

    @pl.when(step == 0)
    def _():
        for s in range(blocks):
            keys[s] = rows_ref[s, HEAD : 2 * HEAD, :].T
            values[s] = rows_ref[s, 2 * HEAD :, :].T
        key_sum[...] = jnp.zeros_like(key_sum)
        value_sum[...] = jnp.zeros_like(value_sum)
        out_ref[...] = jnp.zeros_like(out_ref)

    tile = base_ref[0] + step
    lanes = pl.ds(pl.multiple_of((tile % per_block) * QUERY_TILE, QUERY_TILE), QUERY_TILE)
    queries = rows_ref[tile // per_block, 0:HEAD, lanes] * BF16(HEAD**-0.5)
    limit = limit_ref[...]
    key_index = lax.broadcasted_iota(jnp.int32, (span, QUERY_TILE), 0)
    grads = jnp.concatenate([grad_ref[i] for i in range(grad_ref.shape[0])], axis=1)
    delta = jnp.sum(grads.astype(F32) * wide_ref[...], axis=0, keepdims=True)
    logs = log_ref[...]

    def sweep(s, query_grad, masked):
        scores = jnp.dot(keys[s], queries, preferred_element_type=F32)
        probs = jnp.exp(scores - logs)
        if masked:
            probs = jnp.where(key_index < limit - s * span, probs, 0.0)
        prob_grad = jnp.dot(values[s], grads, preferred_element_type=F32)
        score_grad = (probs * (prob_grad - delta)).astype(BF16)
        value_sum[s] += contract(grads, probs.astype(BF16), 1, 1)
        key_sum[s] += contract(queries, score_grad, 1, 1)
        return query_grad + jnp.dot(
            rows_ref[s, HEAD : 2 * HEAD, :], score_grad, preferred_element_type=F32
        )

    query_grad = jnp.zeros((HEAD, QUERY_TILE), F32)
    query_grad = lax.fori_loop(0, full_ref[step], lambda s, c: sweep(s, c, False), query_grad)
    query_grad = lax.fori_loop(
        full_ref[step], some_ref[step], lambda s, c: sweep(s, c, True), query_grad
    )
    out_ref[tile // per_block, 0:HEAD, lanes] = (query_grad * HEAD**-0.5).astype(BF16)

    @pl.when(step == pl.num_programs(0) - 1)
    def _():
        out_ref[:, HEAD : 2 * HEAD, :] = key_sum[...].astype(BF16)
        out_ref[:, 2 * HEAD :, :] = value_sum[...].astype(BF16)


def fixed_attention_kernel(place_ref, *refs):
    rows_ref, out_ref, wide_ref, log_ref, keys, values = refs[-6:]
    blocks, _, span = rows_ref.shape
    pieces, limit_ref = refs[:blocks], refs[blocks]
    for turn in range(blocks):
        rows_ref[lax.rem(place_ref[1] + blocks - turn, blocks)] = pieces[turn][...]
    length = blocks * span
    stretch = out_ref.shape[2]
    for s in range(blocks):
        keys[s * span : (s + 1) * span, :] = rows_ref[s, HEAD : 2 * HEAD, :].T
        values[:, s * span : (s + 1) * span] = rows_ref[s, 2 * HEAD :, :]
    key_index = lax.broadcasted_iota(jnp.int32, (2 * QUERY_TILE, QUERY_TILE), 0)
    for tile in range(length // QUERY_TILE):
        start = tile * QUERY_TILE
        end = min(start + 2 * QUERY_TILE, length)
        lanes = slice(start % span, start % span + QUERY_TILE)
        queries = rows_ref[start // span, 0:HEAD, lanes] * BF16(HEAD**-0.5)
        scores = jnp.dot(keys[start:end, :], queries, preferred_element_type=F32)
        limit = limit_ref[:, start : start + QUERY_TILE] - start
        scores = jnp.where(key_index[: end - start] < limit, scores, NEG_BIG)
        highest = jnp.max(scores, axis=0, keepdims=True)
        if start > 0:
            before = jnp.dot(keys[:start, :], queries, preferred_element_type=F32)
            highest = jnp.maximum(highest, jnp.max(before, axis=0, keepdims=True))
        terms = jnp.exp(scores - highest)
        total = jnp.sum(terms, axis=0, keepdims=True)
        result = jnp.dot(values[:, start:end], terms.astype(BF16), preferred_element_type=F32)
        if start > 0:
            terms = jnp.exp(before - highest)
            total = total + jnp.sum(terms, axis=0, keepdims=True)
            result = result + jnp.dot(
                values[:, :start], terms.astype(BF16), preferred_element_type=F32
            )
        result = result / total
        log_ref[:, start : start + QUERY_TILE] = highest + jnp.log(total)
        wide_ref[:, start : start + QUERY_TILE] = result
        for i in range(QUERY_TILE // stretch):
            out_ref[start // stretch + i] = result[:, i * stretch : (i + 1) * stretch].astype(BF16)


def fixed_attention_back_kernel(place_ref, rows_ref, limit_ref, grad_ref, wide_ref, log_ref, *refs):
    blocks, _, span = rows_ref.shape
    out_ref, keys, values, key_sum, value_sum = refs[-5:]
    outs = refs[-5 - blocks : -5]
    length = blocks * span
    stretch = grad_ref.shape[2]
    for s in range(blocks):
        keys[s * span : (s + 1) * span, :] = rows_ref[s, HEAD : 2 * HEAD, :].T
        values[s * span : (s + 1) * span, :] = rows_ref[s, 2 * HEAD :, :].T
    key_sum[...] = jnp.zeros_like(key_sum)
    value_sum[...] = jnp.zeros_like(value_sum)
    key_index = lax.broadcasted_iota(jnp.int32, (2 * QUERY_TILE, QUERY_TILE), 0)
    for tile in range(length // QUERY_TILE):
        start = tile * QUERY_TILE
        end = min(start + 2 * QUERY_TILE, length)
        lanes = slice(start % span, start % span + QUERY_TILE)
        queries = rows_ref[start // span, 0:HEAD, lanes] * BF16(HEAD**-0.5)
        pieces = QUERY_TILE // stretch
        grads = jnp.concatenate([grad_ref[tile * pieces + i] for i in range(pieces)], axis=1)
        wide = wide_ref[:, start : start + QUERY_TILE]
        delta = jnp.sum(grads.astype(F32) * wide, axis=0, keepdims=True)
        logs = log_ref[:, start : start + QUERY_TILE]
        limit = limit_ref[:, start : start + QUERY_TILE] - start
        query_grad = jnp.zeros((HEAD, QUERY_TILE), F32)
        for low, high in ((0, start), (start, end)):
            if low == high:
                continue
            scores = jnp.dot(keys[low:high, :], queries, preferred_element_type=F32)
            probs = jnp.exp(scores - logs)
            if low == start:
                probs = jnp.where(key_index[: high - low] < limit, probs, 0.0)
            prob_grad = jnp.dot(values[low:high, :], grads, preferred_element_type=F32)
            score_grad = (probs * (prob_grad - delta)).astype(BF16)
            value_sum[:, low:high] += contract(grads, probs.astype(BF16), 1, 1)
            key_sum[:, low:high] += contract(queries, score_grad, 1, 1)
            query_grad = query_grad + contract(keys[low:high, :], score_grad, 0, 0)
        out_ref[start // span, 0:HEAD, lanes] = (query_grad * HEAD**-0.5).astype(BF16)
    for s in range(blocks):
        out_ref[s, HEAD : 2 * HEAD, :] = key_sum[:, s * span : (s + 1) * span].astype(BF16)
        out_ref[s, 2 * HEAD :, :] = value_sum[:, s * span : (s + 1) * span].astype(BF16)
    for turn in range(blocks):
        outs[turn][...] = out_ref[lax.rem(place_ref[1] + turn, blocks)]


def at_once(shape):
    return pl.BlockSpec(shape, lambda step: (0,) * len(shape))


ANYWHERE = pl.BlockSpec(memory_space=pl.ANY)
IN_SMEM = pl.BlockSpec(memory_space=pltpu.SMEM)


def fixed_attention(pieces, limit, place, stretch, after):
    blocks = len(pieces)
    features, span = pieces[0].shape
    length = blocks * span
    return pl.pallas_call(
        fixed_attention_kernel,
        grid=(1,),
        in_specs=[IN_SMEM, *[at_once(array.shape) for array in (*pieces, limit)]]
        + [ANYWHERE] * len(after),
        out_specs=[
            at_once((blocks, features, span)),
            at_once((length // stretch, HEAD, stretch)),
            at_once((HEAD, length)),
            at_once((1, length)),
        ],
        out_shape=[
            jax.ShapeDtypeStruct((blocks, features, span), BF16),
            jax.ShapeDtypeStruct((length // stretch, HEAD, stretch), BF16),
            jax.ShapeDtypeStruct((HEAD, length), F32),
            jax.ShapeDtypeStruct((1, length), F32),
        ],
        scratch_shapes=[pltpu.VMEM((length, HEAD), BF16), pltpu.VMEM((HEAD, length), BF16)],
        compiler_params=vmem(16 * MIB),
        cost_estimate=cost(features * length * length // 48, features * length * 4, length * length),
        name="attend",
    )(place, *pieces, limit, *after)


def fixed_attention_back(rows, limit, grads, wide, logs, place, later_than):
    blocks, features, span = rows.shape
    length = blocks * span
    return pl.pallas_call(
        fixed_attention_back_kernel,
        grid=(1,),
        in_specs=[
            IN_SMEM,
            *[at_once(array.shape) for array in (rows, limit, grads, wide, logs)],
        ]
        + [ANYWHERE] * len(later_than),
        out_specs=[at_once((features, span))] * blocks,
        out_shape=[jax.ShapeDtypeStruct((features, span), BF16)] * blocks,
        scratch_shapes=[
            pltpu.VMEM(rows.shape, BF16),
            pltpu.VMEM((length, HEAD), BF16),
            pltpu.VMEM((length, HEAD), BF16),
            pltpu.VMEM((HEAD, length), F32),
            pltpu.VMEM((HEAD, length), F32),
        ],
        compiler_params=vmem(20 * MIB),
        cost_estimate=cost(rows.size * length // 16, rows.size * 4, length * length),
        name="attend_back",
    )(place, rows, limit, grads, wide, logs, *later_than)


def whole(shape):
    return pl.BlockSpec(shape, lambda step, *_: (0,) * len(shape))


def tile_at(step, full, some, base):
    return (0, base[0] + step)


def attention(rows, spans, stretch):
    full, some, base, limit, tiles, parts = spans
    blocks, _, span = rows.shape
    length = tiles * QUERY_TILE
    return pl.pallas_call(
        attention_kernel,
        grid_spec=pltpu.PrefetchScalarGridSpec(
            num_scalar_prefetch=3,
            grid=(tiles,),
            in_specs=[whole(rows.shape), pl.BlockSpec((1, QUERY_TILE), tile_at)],
            out_specs=[
                pl.BlockSpec((QUERY_TILE // stretch, HEAD, stretch), lambda step, *_: (step, 0, 0)),
                pl.BlockSpec((HEAD, QUERY_TILE), lambda step, *_: (0, step)),
                pl.BlockSpec((1, QUERY_TILE), lambda step, *_: (0, step)),
            ],
            scratch_shapes=[pltpu.VMEM((blocks, span, HEAD), BF16)],
        ),
        out_shape=[
            jax.ShapeDtypeStruct((length // stretch, HEAD, stretch), BF16),
            jax.ShapeDtypeStruct((HEAD, length), F32),
            jax.ShapeDtypeStruct((1, length), F32),
        ],
        compiler_params=vmem(52 * MIB),
        cost_estimate=cost(rows.size * length // 48, rows.size * 4, length * length),
        name="attend",
    )(full, some, base, rows, limit)


def attention_back(rows, spans, grads, wide, logs, later_than):
    full, some, base, limit, tiles, parts = spans
    blocks, _, span = rows.shape
    stretch = grads.shape[2]
    return pl.pallas_call(
        attention_back_kernel,
        grid_spec=pltpu.PrefetchScalarGridSpec(
            num_scalar_prefetch=3,
            grid=(tiles,),
            in_specs=[
                whole(rows.shape),
                pl.BlockSpec((1, QUERY_TILE), tile_at),
                pl.BlockSpec((QUERY_TILE // stretch, HEAD, stretch), lambda step, *_: (step, 0, 0)),
                pl.BlockSpec((HEAD, QUERY_TILE), lambda step, *_: (0, step)),
                pl.BlockSpec((1, QUERY_TILE), lambda step, *_: (0, step)),
                *[pl.BlockSpec(memory_space=pl.ANY)] * len(later_than),
            ],
            out_specs=whole(rows.shape),
            scratch_shapes=[
                pltpu.VMEM((blocks, span, HEAD), BF16),
                pltpu.VMEM((blocks, span, HEAD), BF16),
                pltpu.VMEM((blocks, HEAD, span), F32),
                pltpu.VMEM((blocks, HEAD, span), F32),
            ],
        ),
        out_shape=jax.ShapeDtypeStruct(rows.shape, BF16),
        compiler_params=vmem(52 * MIB),
        cost_estimate=cost(rows.size * tiles * QUERY_TILE // 16, rows.size * 4, rows.size),
        name="attend_back",
    )(full, some, base, rows, limit, grads, wide, logs, *later_than)


def run_kernel(kernel, operands, outputs, scratch=(), after=(), flops=0, name=None, room=6):
    moved = sum(array.size * array.dtype.itemsize for array in operands)
    size = 2 * moved
    for times, arrays in ((2, outputs), (1, scratch)):
        for shape, dtype in arrays:
            size += times * math.prod(shape) * jnp.dtype(dtype).itemsize
    given, kept = len(operands), len(operands) + len(after)
    return pl.pallas_call(
        lambda *refs: kernel(*refs[:given], *refs[kept:]),
        grid=(1,),
        in_specs=[IN_SMEM, *[at_once(array.shape) for array in operands[1:]]]
        + [ANYWHERE] * len(after),
        out_specs=[at_once(shape) for shape, _ in outputs],
        out_shape=[jax.ShapeDtypeStruct(shape, dtype) for shape, dtype in outputs],
        scratch_shapes=[pltpu.VMEM(shape, dtype) for shape, dtype in scratch],
        compiler_params=vmem(room * MIB + size),
        cost_estimate=cost(flops, moved),
        name=name,
    )(*operands, *after)


def rows_at(index, size):
    return pl.ds(pl.multiple_of(index * size, size), size)


def qkv_kernel(fixed, normed, place_ref, *refs):
    rows_refs, (gain_ref, weight_ref, cosine_ref, sine_ref) = refs[:4], refs[4:8]
    pieces, team, heads = refs[8:-2], refs[-2], refs[-1]
    member = place_ref[0]
    stretch = rows_refs[0].shape[0]
    half = HEAD // 2
    for turn in range(4):
        rows = rows_refs[turn][...]
        if not normed:
            wide = rows.astype(F32)
            rows = (wide * rms_factor(wide) * gain_ref[...]).astype(BF16)
        team[rows_at(member ^ turn, stretch), :] = rows
    projected = contract(weight_ref[...], team[...], 0, 1)
    cosine, sine = cosine_ref[...], sine_ref[...]
    for head in range(TEAM_HEADS):
        for part in range(3):
            at = (head * 3 + part) * HEAD
            first, second = projected[at : at + half], projected[at + half : at + HEAD]
            if part < 2:
                first, second = (
                    first * cosine - second * sine,
                    second * cosine + first * sine,
                )
            heads[head, part * HEAD : part * HEAD + half] = first.astype(BF16)
            heads[head, part * HEAD + half : (part + 1) * HEAD] = second.astype(BF16)
    for turn, piece in enumerate(pieces):
        head = turn
        if fixed:
            head = lax.rem(place_ref[1] + turn, len(pieces)) - place_ref[2]
            head = jnp.clip(head, 0, TEAM_HEADS - 1)
        piece[...] = heads[head]


def qkv_step(rows, normed, gain, weight, after, context):
    group = TEAM_SIZE * rows[0].shape[0]
    fixed = context["parts"] == 1
    return run_kernel(
        functools.partial(qkv_kernel, fixed, normed),
        [context["place"], *rows, gain, weight, context["cosine"], context["sine"]],
        [((3 * HEAD, group), BF16)] * (context["deep"] if fixed else TEAM_HEADS)
        + [((group, D), BF16)],
        [((TEAM_HEADS, 3 * HEAD, group), BF16)],
        after,
        flops=2 * group * D * weight.shape[1],
        name="qkv",
    )


def qkv_back_kernel(fixed, halves, place_ref, *refs):
    count = len(refs) - (16 if halves else 15)
    grads, refs = refs[:count], refs[count:]
    weight_ref, cosine_ref, sine_ref, team_ref, gain_ref, small_ref = refs[:6]
    outs, (stacked, turned, parts, packed) = refs[6:-4], refs[-4:]
    half = HEAD // 2
    stretch = outs[0].shape[0]
    for turn in range(count):
        stacked[turn] = grads[turn][...]
    cosine, sine = cosine_ref[...], sine_ref[...]
    for head in range(TEAM_HEADS):
        at = head
        if fixed:
            at = lax.rem(place_ref[1] - head - place_ref[2] + 2 * count, count)
        rows = stacked[at].astype(F32)
        for part in range(3):
            low = part * HEAD
            first, second = rows[low : low + half], rows[low + half : low + HEAD]
            if part < 2:
                first, second = (
                    first * cosine + second * sine,
                    second * cosine - first * sine,
                )
            low += head * 3 * HEAD
            turned[low : low + half] = first.astype(BF16)
            turned[low + half : low + HEAD] = second.astype(BF16)
    projected_grad = turned[...].T
    normed_grad = contract(projected_grad, weight_ref[...], 1, 1)
    parts[...] = normed_grad.astype(BF16)
    for turn in range(4):
        outs[turn][...] = parts[rows_at(place_ref[0] ^ turn, stretch), :]
    team = team_ref[...]
    edge = projected_grad.shape[1]
    packed[:, :edge] = contract(team, projected_grad, 0, 0).astype(BF16)
    gain_grad = jnp.sum(normed_grad * team.astype(F32), axis=0, keepdims=True) / gain_ref[...]
    small = small_ref[...]
    lane = lax.broadcasted_iota(jnp.int32, small.shape, 1)
    small = jnp.where(lane == 0, jnp.broadcast_to(gain_grad, (128, D)).T, small)
    packed[:, edge:] = small[:, : packed.shape[1] - edge].astype(BF16)
    if halves:
        outs[4][...] = packed[rows_at(place_ref[3], D // 2), :]
        outs[5][...] = packed[rows_at(1 - place_ref[3], D // 2), :]
    else:
        outs[4][...] = packed[...]


def qkv_back_step(grads, weight, team, gain, small, halves, after, context):
    group = team.shape[0]
    width = weight.shape[1] + 64
    packed = [((D // 2, width), BF16)] * 2 if halves else [((D, width), BF16)]
    return run_kernel(
        functools.partial(qkv_back_kernel, context["parts"] == 1, halves),
        [
            context["place"],
            *grads,
            weight,
            context["cosine"],
            context["sine"],
            team,
            gain,
            small,
        ],
        [((group // TEAM_SIZE, D), BF16)] * TEAM_SIZE + packed,
        [
            ((len(grads), 3 * HEAD, group), BF16),
            ((weight.shape[1], group), BF16),
            ((group, D), BF16),
            ((D, width), BF16),
        ],
        after,
        flops=4 * group * D * weight.shape[1],
        name="qkv_back",
    )


def head_slot(head, fixed):
    member = head // TEAM_HEADS
    return (head % TEAM_HEADS + (member // 2 if fixed else 0)) * TEAM_SIZE + member


def chosen(ids_ref, choice):
    ids = ids_ref[:, choice : choice + 1]
    return lax.broadcasted_iota(jnp.int32, (ids.shape[0], 128), 1) == ids + 2


def row_table(slots_ref, choice):
    slots = slots_ref[:, choice : choice + 1]
    index = lax.broadcasted_iota(jnp.int32, (slots.shape[0], EXPERTS * SLOTS), 1)
    return jnp.where(index == slots, 1.0, 0.0).astype(BF16)


def slot_table(turned_ref, choice):
    slots = turned_ref[choice : choice + 1, :]
    index = lax.broadcasted_iota(jnp.int32, (EXPERTS * SLOTS, slots.shape[1]), 0)
    return jnp.where(index == slots, 1.0, 0.0).astype(BF16)


def slots_of_grads(turned_ref, gates, upstream):
    terms = [
        jnp.dot(
            slot_table(turned_ref, c),
            (gates[:, c : c + 1] * upstream).astype(BF16),
            preferred_element_type=F32,
        )
        for c in range(2)
    ]
    return (terms[0] + terms[1]).astype(BF16)


def feed_kernel(fixed, last, place_ref, *refs):
    back_ref, stream_ref, weight_ref, gain_ref, router_ref, ids_ref, turned_ref = refs[:7]
    middle_ref, normed_ref, gates_ref, out_ref, mixed_ref = refs[-5:]
    for head in range(HEADS):
        mixed_ref[head * HEAD : (head + 1) * HEAD, :] = back_ref[head_slot(head, fixed)]
    middle = stream_ref[...].astype(F32) + contract(mixed_ref[...], weight_ref[...], 0, 0)
    normed = (middle * rms_factor(middle) * gain_ref[...]).astype(BF16)
    middle_ref[...] = middle
    normed_ref[...] = normed
    table = slot_table(turned_ref, 0) + slot_table(turned_ref, 1)
    out_ref[:, :D] = jnp.dot(table, normed, preferred_element_type=F32).astype(BF16)
    logits = jnp.dot(normed, router_ref[...], preferred_element_type=F32)
    picked = [
        jnp.sum(jnp.where(chosen(ids_ref, c), logits, 0.0), axis=1, keepdims=True)
        for c in range(2)
    ]
    highest = jnp.maximum(picked[0], picked[1])
    powers = [jnp.exp(pick - highest) for pick in picked]
    total = powers[0] + powers[1]
    gates = jnp.concatenate([powers[0] / total, powers[1] / total], axis=1)
    gates_ref[...] = gates
    if last:
        out_ref[:, D:] = slots_of_grads(turned_ref, gates, refs[7][...].astype(F32))


def feed_step(back, stream, out_weight, gain, router, upstream, after, context):
    stretch = stream.shape[0]
    last = upstream is not None
    operands = [
        context["place"],
        back,
        stream,
        out_weight,
        gain,
        router,
        context["ids"],
        context["turned_slots"],
    ]
    return run_kernel(
        functools.partial(feed_kernel, context["parts"] == 1, last),
        operands + ([upstream] if last else []),
        [
            ((stretch, D), F32),
            ((stretch, D), BF16),
            ((stretch, 2), F32),
            ((EXPERTS * SLOTS, 2 * D if last else D), BF16),
            ((D, stretch), BF16),
        ],
        (),
        after,
        flops=4 * stretch * D * D,
        name="feed",
    )


def add_up(parts):
    total = parts[0][...].astype(F32)
    for part in parts[1:]:
        total = total + part[...].astype(F32)
    return total


def layer_end_kernel(place_ref, *refs):
    returned_ref, middle_ref, gates_ref, slots_ref, gain_ref = refs[:5]
    parts = refs[5:9]
    stream_ref, gap_ref, normed_ref = refs[-3:]
    choices = [
        jnp.dot(row_table(slots_ref, c), returned_ref[...], preferred_element_type=F32)
        for c in range(2)
    ]
    gates = gates_ref[...]
    stream = middle_ref[...] + add_up(parts) + gates[:, 0:1] * choices[0]
    stream = stream + gates[:, 1:2] * choices[1]
    stream_ref[...] = stream
    gap_ref[...] = choices[0] - choices[1]
    normed_ref[...] = (stream * rms_factor(stream) * gain_ref[...]).astype(BF16)


def layer_end_step(returned, feed, parts, next_gain, after, context):
    shape = feed["middle"].shape
    return run_kernel(
        layer_end_kernel,
        [
            context["place"],
            returned,
            feed["middle"],
            feed["gates"],
            context["slots"],
            next_gain,
            *parts,
        ],
        [(shape, F32), (shape, F32), (shape, BF16)],
        (),
        after,
        flops=4 * shape[0] * D * returned.shape[0],
        name="layer_end",
    )


def feed_back_kernel(fixed, last, place_ref, *refs):
    (
        returned_ref,
        middle_ref,
        normed_ref,
        gates_ref,
        slots_ref,
        ids_ref,
        upstream_ref,
        gain_ref,
        router_ref,
        weight_ref,
    ) = refs[:10]
    parts = refs[10:14]
    outs = refs[-4:]
    tables = [row_table(slots_ref, c) for c in range(2)]
    gates = gates_ref[...]
    middle = middle_ref[...]
    upstream = upstream_ref[...].astype(F32)
    if last:
        choices = [
            jnp.dot(table, returned_ref[:, :D], preferred_element_type=F32) for table in tables
        ]
        gap = choices[0] - choices[1]
        sums = add_up(parts)
        output = middle + sums[:, :D] + gates[:, 0:1] * choices[0]
        refs[-5][...] = (output + gates[:, 1:2] * choices[1]).astype(BF16)
        grad_rows, shared_grad = returned_ref[:, D:], sums[:, D:]
    else:
        gap = refs[14][...]
        grad_rows, shared_grad = returned_ref[...], add_up(parts)
    lead = gates[:, 0:1] * gates[:, 1:2] * jnp.sum(gap * upstream, axis=1, keepdims=True)
    logit_grad = jnp.where(chosen(ids_ref, 0), lead, 0.0) - jnp.where(
        chosen(ids_ref, 1), lead, 0.0
    )
    high = logit_grad.astype(BF16)
    low = (logit_grad - high.astype(F32)).astype(BF16)
    router = router_ref[...]
    normed_grad = (
        shared_grad
        + contract(high, router, 1, 1)
        + contract(low, router, 1, 1)
        + jnp.dot(tables[0] + tables[1], grad_rows, preferred_element_type=F32)
    )
    factor = rms_factor(middle)
    norm_grad, _ = norm_back(middle, gain_ref[...], factor, normed_grad)
    middle_grad = upstream + norm_grad
    attn_grad = middle_grad.astype(BF16)
    middle_grad_ref, attn_ref, heads_ref, small_ref = outs
    middle_grad_ref[...] = middle_grad
    attn_ref[...] = attn_grad
    mixed_grad = contract(weight_ref[...], attn_grad, 1, 1).astype(BF16)
    used = set()
    for head in range(HEADS):
        slot = head_slot(head, fixed)
        used.add(slot)
        heads_ref[slot] = mixed_grad[head * HEAD : (head + 1) * HEAD]
    for slot in range(heads_ref.shape[0]):
        if slot not in used:
            heads_ref[slot] = jnp.zeros_like(heads_ref[slot])
    gain_grad = jnp.sum(normed_grad * middle * factor, axis=0, keepdims=True)
    normed = normed_ref[...]
    small = contract(normed, high, 0, 0) + contract(normed, low, 0, 0)
    lane = lax.broadcasted_iota(jnp.int32, small.shape, 1)
    small_ref[...] = jnp.where(lane == 1, jnp.broadcast_to(gain_grad, (128, D)).T, small)


def feed_back_step(returned, feed, upstream, parts, others, weights, last, after, context):
    stretch = feed["middle"].shape[0]
    shape = (stretch, D)
    return run_kernel(
        functools.partial(feed_back_kernel, context["parts"] == 1, last),
        [
            context["place"],
            returned,
            feed["middle"],
            feed["normed_ffn"],
            feed["gates"],
            context["slots"],
            context["ids"],
            upstream,
            weights["gain_two"],
            weights["router"],
            weights["out"],
            *parts,
            *others,
        ],
        ([(shape, BF16)] if last else [])
        + [
            (shape, F32),
            (shape, BF16),
            ((TEAM_SIZE * TEAM_SIZE, HEAD, stretch), BF16),
            ((D, 128), F32),
        ],
        (),
        after,
        flops=4 * stretch * D * D,
        name="feed_back",
    )


def layer_start_kernel(more, place_ref, *refs):
    stream_ref, middle_grad_ref, gain_ref = refs[:3]
    parts = refs[3:7]
    stream = stream_ref[...].astype(F32)
    norm_grad, _ = norm_back(stream, gain_ref[...], rms_factor(stream), add_up(parts))
    upstream = middle_grad_ref[...] + norm_grad
    if more:
        gates_ref, turned_ref, wide_ref, out_ref = refs[7:9] + refs[-3:-2] + refs[-1:]
        wide_ref[...] = upstream
        refs[-2][...] = upstream.astype(BF16)
        out_ref[...] = slots_of_grads(turned_ref, gates_ref[...], upstream)
    else:
        refs[-1][...] = upstream.astype(BF16)


def layer_start_step(stream, middle_grad, gain, parts, feed, context):
    shape = stream.shape
    more = feed is not None
    return run_kernel(
        functools.partial(layer_start_kernel, more),
        [
            context["place"],
            stream,
            middle_grad,
            gain,
            *parts,
            *([feed["gates"], context["turned_slots"]] if more else []),
        ],
        [(shape, F32), (shape, BF16), ((EXPERTS * SLOTS, D), BF16)] if more else [(shape, BF16)],
        flops=4 * shape[0] * D * EXPERTS * SLOTS if more else 0,
        name="layer_start",
    )


def shared_grads_kernel(place_ref, *refs):
    team_ref, joint_ref, hidden_ref, grads_ref = refs[:4]
    joint_outs, down_outs = refs[4:6], refs[6:8]
    half = D // 2
    units = hidden_ref.shape[1] // 2
    for place, dp in enumerate((place_ref[3], 1 - place_ref[3])):
        joint_outs[place][...] = contract(
            team_ref[:, rows_at(dp, half)], joint_ref[...], 0, 0
        ).astype(BF16)
        down = contract(hidden_ref[:, rows_at(dp, units)], grads_ref[...], 0, 0).astype(BF16)
        down_outs[place][...] = down


def shared_grads_step(team, joint_grad, hidden, grad_team, after, context):
    return run_kernel(
        shared_grads_kernel,
        [context["place"], team, joint_grad, hidden, grad_team],
        [((D // 2, joint_grad.shape[1]), BF16)] * 2
        + [((hidden.shape[1] // 2, D), BF16)] * 2,
        (),
        after,
        flops=2 * team.shape[0] * D * (joint_grad.shape[1] + D),
        name="shared_grads",
    )


def shared_grads(shared, after, context):
    team, grads, hidden, joint_grad = shared[-4:]
    *joints, own, other = shared_grads_step(team, joint_grad, hidden, grads, after, context)
    return [*joints, own.reshape(D // 2, -1), other.reshape(D // 2, -1)]


def out_grads_kernel(place_ref, mixed_ref, attn_ref, own_ref, other_ref):
    for out, dp in zip((own_ref, other_ref), (place_ref[3], 1 - place_ref[3])):
        out[...] = jnp.dot(
            mixed_ref[rows_at(dp, D // 2), :], attn_ref[...], preferred_element_type=F32
        ).astype(BF16)


def out_grads_step(mixed, attn_grad, after, context):
    return run_kernel(
        out_grads_kernel,
        [context["place"], mixed, attn_grad],
        [((D // 2, D), BF16)] * 2,
        (),
        after,
        flops=2 * mixed.shape[1] * D * D,
        name="out_grads",
    )


def feed_end_kernel(place_ref, *refs):
    layers_count = (len(refs) - 4) // 9
    pieces = refs[: 4 * layers_count]
    out_pieces = refs[4 * layers_count : 8 * layers_count]
    downs = refs[8 * layers_count : 9 * layers_count]
    joint_out, out_out, down_out, columns = refs[-4:]
    width = joint_out.shape[1]
    joint_width = pieces[0].shape[1]
    unit = down_out.shape[1]
    rest = joint_width // (2 * unit)
    for layer in range(layers_count):
        total = None
        for turn in range(4):
            columns[place_ref[0] ^ turn] = pieces[4 * layer + turn][...].astype(F32)
            part = out_pieces[4 * layer + turn][...].astype(F32)
            total = part if total is None else total + part
        out_out[layer] = total
        for member in range(4):
            rows = columns[member]
            for part in range(2):
                for block in range(rest):
                    low = (part * rest + block) * unit
                    at = part * (joint_out.shape[2] // 2) + (block * 4 + member) * unit
                    joint_out[layer, :, at : at + unit] = rows[:, low : low + unit]
        down_out[layer] = downs[layer][...].astype(F32)


def qkv_end_kernel(place_ref, *refs):
    pieces = refs[:-3]
    qkv_out, small_out, columns = refs[-3:]
    edge = TEAM_HEADS * 3 * HEAD
    for layer in range(qkv_out.shape[0]):
        small = None
        for turn in range(4):
            piece = pieces[4 * layer + turn][...].astype(F32)
            columns[place_ref[0] ^ turn] = piece
            part = piece[:, edge:]
            small = part if small is None else small + part
        small_out[layer] = small
        for member in range(4):
            rows = columns[member]
            for head in range(TEAM_HEADS):
                for part in range(3):
                    low = (head * 3 + part) * HEAD
                    at = part * D + (member * TEAM_HEADS + head) * HEAD
                    qkv_out[layer, :, at : at + HEAD] = rows[:, low : low + HEAD]


def logistic(values):
    return 0.5 * jnp.tanh(0.5 * values) + 0.5


def swiglu_back(gate_pre, up_pre, hidden_grad):
    sigmoid_gate = logistic(gate_pre)
    silu_gate = gate_pre * sigmoid_gate
    gate_grad = hidden_grad * up_pre * (sigmoid_gate + silu_gate * (1.0 - sigmoid_gate))
    up_grad = hidden_grad * silu_gate
    return (gate_grad.astype(BF16), up_grad.astype(BF16))


def swiglu(gate_pre, up_pre):
    return (gate_pre * logistic(gate_pre) * up_pre).astype(BF16)


def expert_kernel(forward, backward, *refs):
    inputs = 1 + backward
    rows_ref, grads_ref = refs[0], refs[inputs - 1]
    gate_ref, up_ref, down_ref, out_ref, total = refs[inputs:]
    step = pl.program_id(0)
    rows = rows_ref[...]
    gate, up, down = gate_ref[0, 0], up_ref[0, 0], down_ref[0, 0]
    gate_pre = jnp.dot(rows, gate, preferred_element_type=F32)
    up_pre = jnp.dot(rows, up, preferred_element_type=F32)
    terms = []
    if forward:
        terms.append(jnp.dot(swiglu(gate_pre, up_pre), down, preferred_element_type=F32))
    if backward:
        hidden_grad = contract(grads_ref[...], down, 1, 1).astype(BF16).astype(F32)
        gate_grad, up_grad = swiglu_back(gate_pre, up_pre, hidden_grad)
        terms.append(contract(gate_grad, gate, 1, 1) + contract(up_grad, up, 1, 1))

    @pl.when(step == 0)
    def _():
        for i, term in enumerate(terms):
            total[:, i * D : (i + 1) * D] = term

    @pl.when(step > 0)
    def _():
        for i, term in enumerate(terms):
            total[:, i * D : (i + 1) * D] += term

    @pl.when(step == pl.num_programs(0) - 1)
    def _():
        out_ref[...] = total[...].astype(BF16)


def run_expert(layer, joint, down, rows, grads, forward, after=()):
    half = joint.shape[3] // 2
    chunk = min(512, half)
    chunks = half // chunk
    given = [rows] + ([grads] if grads is not None else [])
    count = rows[0].shape[0]
    width = D * (int(forward) + int(grads is not None))
    drop = len(given) + 3
    body = functools.partial(expert_kernel, forward, grads is not None)
    return pl.pallas_call(
        lambda *refs: body(*refs[:drop], *refs[drop + len(after) :]),
        grid=(chunks,),
        in_specs=[
            *[pl.BlockSpec((count, D), lambda i, at=at: (0, at)) for _, at in given],
            pl.BlockSpec((1, 1, D, chunk), lambda i: (layer, 0, 0, i)),
            pl.BlockSpec((1, 1, D, chunk), lambda i: (layer, 0, 0, chunks + i)),
            pl.BlockSpec((1, 1, chunk, D), lambda i: (layer, 0, i, 0)),
            *[ANYWHERE] * len(after),
        ],
        out_specs=pl.BlockSpec((count, width), lambda i: (0, 0)),
        out_shape=jax.ShapeDtypeStruct((count, width), BF16),
        scratch_shapes=[pltpu.VMEM((count, width), F32)],
        compiler_params=vmem(
            4 * len(given) * count * D + 12 * D * chunk + 8 * count * width + 32 * count * chunk
        ),
        cost_estimate=cost(
            2 * count * D * half * (2 + int(forward) + 3 * int(grads is not None)),
            6 * D * half + 4 * count * width,
            count * half,
        ),
        name="expert_forward" if grads is None else "expert_both" if forward else "expert_back",
    )(*[array for array, _ in given], joint, joint, down, *after)


def expert_grad_kernel(place_ref, own_rows, own_grads, other_rows, other_grads, gate_ref, up_ref, down_ref, *refs):
    joint_out, down_out, rows_all, grads_all, turned, hold = refs[-6:]
    count = own_rows.shape[0]

    @pl.when((pl.program_id(0) == 0) & (pl.program_id(1) == 0))
    def _():
        own = rows_at(place_ref[3], count)
        other = rows_at(1 - place_ref[3], count)
        rows_all[own, :] = own_rows[...]
        rows_all[other, :] = other_rows[...]
        grads_all[own, :] = own_grads[...]
        grads_all[other, :] = other_grads[...]
        turned[...] = rows_all[...].T

    @pl.when(pl.program_id(1) == 0)
    def _():
        rows = rows_all[...]
        grads = grads_all[...]
        gate_pre = jnp.dot(rows, gate_ref[0, 0], preferred_element_type=F32)
        up_pre = jnp.dot(rows, up_ref[0, 0], preferred_element_type=F32)
        hidden_grad = contract(grads, down_ref[0, 0], 1, 1).astype(BF16).astype(F32)
        gate_grad, up_grad = swiglu_back(gate_pre, up_pre, hidden_grad)
        hold[...] = up_grad
        down_out[0, 0] = contract(swiglu(gate_pre, up_pre), grads, 0, 0)
        joint_out[0, 0] = jnp.dot(turned[...], gate_grad, preferred_element_type=F32)

    @pl.when(pl.program_id(1) == 1)
    def _():
        joint_out[0, 0] = jnp.dot(turned[...], hold[...], preferred_element_type=F32)


def expert_grads(layer, quarters, own, other, joint, down, before, later_than, context):
    half = joint.shape[3] // 2
    given = [*own, *other]
    count = given[0][0].shape[0]
    chunk = min(512 if count <= 512 else 128, half // 4)
    chunks = half // chunk
    first, steps = [quarter * chunks // 4 for quarter in quarters]
    in_specs = [
        IN_SMEM,
        *[pl.BlockSpec((count, D), lambda i, h, at=at: (0, at)) for _, at in given],
        pl.BlockSpec((1, 1, D, chunk), lambda i, h: (layer, 0, 0, first + i)),
        pl.BlockSpec((1, 1, D, chunk), lambda i, h: (layer, 0, 0, chunks + first + i)),
        pl.BlockSpec((1, 1, chunk, D), lambda i, h: (layer, 0, first + i, 0)),
    ]
    operands = [context["place"]] + [array for array, _ in given] + [joint, joint, down]
    aliases = {}
    if before is not None:
        aliases = {len(operands): 0, len(operands) + 1: 1}
        operands += list(before)
    operands += later_than
    in_specs += [ANYWHERE] * (len(operands) - len(in_specs))
    return pl.pallas_call(
        expert_grad_kernel,
        grid=(steps, 2),
        in_specs=in_specs,
        out_specs=[
            pl.BlockSpec((1, 1, D, chunk), lambda i, h: (layer, 0, 0, h * chunks + first + i)),
            pl.BlockSpec((1, 1, chunk, D), lambda i, h: (layer, 0, first + i, 0)),
        ],
        out_shape=[
            jax.ShapeDtypeStruct(joint.shape, F32),
            jax.ShapeDtypeStruct(down.shape, F32),
        ],
        scratch_shapes=[
            pltpu.VMEM((2 * count, D), BF16),
            pltpu.VMEM((2 * count, D), BF16),
            pltpu.VMEM((D, 2 * count), BF16),
            pltpu.VMEM((2 * count, chunk), BF16),
        ],
        input_output_aliases=aliases,
        compiler_params=vmem(30 * count * D + 28 * D * chunk + 56 * count * chunk),
        cost_estimate=cost(
            24 * count * D * chunk * steps, 18 * D * chunk * steps, 2 * count * chunk * steps
        ),
        name="expert_grads",
    )(*operands)


def nothing(*refs):
    pass


def later(rows, *others):
    return pl.pallas_call(
        nothing,
        in_specs=[pl.BlockSpec(memory_space=pl.ANY)] * (1 + len(others)),
        out_specs=pl.BlockSpec(memory_space=pl.ANY),
        out_shape=jax.ShapeDtypeStruct(rows.shape, rows.dtype),
        input_output_aliases={0: 0},
        name="later",
    )(rows, *others)


def route_slots(route_ids):
    stretch_rows = route_ids.shape[0]
    experts_row = jnp.arange(EXPERTS, dtype=jnp.int32)
    route_hits = (route_ids[:, :, None] == experts_row[None, None, :]).astype(jnp.int32)
    running = jnp.cumsum(route_hits.reshape(2 * stretch_rows, EXPERTS), axis=0) - 1
    running = running.reshape(stretch_rows, 2, EXPERTS)
    return route_ids * SLOTS + jnp.sum(route_hits * running, axis=2)


def send_rows(outgoing, split_count):
    width = outgoing.shape[1]
    outgoing = outgoing.reshape(EXPERTS, SLOTS, width)
    if split_count > 1:
        outgoing = jnp.repeat(outgoing, split_count, axis=0)
    return exchange(outgoing, SEQ).reshape(-1, width)


def return_rows(rows, split_count):
    width = rows.shape[1]
    returned = exchange(rows.reshape(-1, SLOTS, width), SEQ)
    if split_count > 1:
        returned = (
            returned.reshape(EXPERTS, split_count, SLOTS, width).astype(F32).sum(axis=1)
        ).astype(BF16)
    return returned.reshape(EXPERTS * SLOTS, width)


def shared_kernel(forward, backward, place_ref, *refs):
    rows_refs, refs = refs[:4], refs[4:]
    if backward:
        grads_refs, refs = refs[:4], refs[4:]
    joint_ref, down_ref = refs[:2]
    parts, outs = refs[2:6], refs[6:]
    stretch = rows_refs[0].shape[0]
    team = jnp.concatenate([ref[...] for ref in rows_refs], axis=0)
    joint, down = joint_ref[...], down_ref[...]
    half = joint.shape[1] // 2
    pre = jnp.dot(team, joint, preferred_element_type=F32)
    gate_pre, up_pre = pre[:, :half], pre[:, half:]
    hidden = swiglu(gate_pre, up_pre)
    results = []
    if forward:
        results.append(jnp.dot(hidden, down, preferred_element_type=F32))
    if backward:
        grads = jnp.concatenate([ref[...] for ref in grads_refs], axis=0)
        hidden_grad = contract(grads, down, 1, 1).astype(BF16).astype(F32)
        gate_grad, up_grad = swiglu_back(gate_pre, up_pre, hidden_grad)
        joint_grad = jnp.concatenate([gate_grad, up_grad], axis=1)
        results.append(contract(joint_grad, joint, 1, 1))
        team_out, grads_out, hidden_out, joint_out = outs
        team_out[...] = team
        grads_out[...] = grads
        hidden_out[...] = hidden
        joint_out[...] = joint_grad
    for place, result in enumerate(results):
        for turn in range(4):
            parts[turn][:, place * D : (place + 1) * D] = result[
                turn * stretch : (turn + 1) * stretch
            ].astype(BF16)


def shared_step(rows, grads, joint, down, forward, after, context):
    stretch = rows[0].shape[0]
    group = TEAM_SIZE * stretch
    backward = grads is not None
    outputs = [((stretch, D * (int(forward) + int(backward))), BF16)] * 4
    if backward:
        outputs += [
            ((group, D), BF16),
            ((group, D), BF16),
            ((group, down.shape[0]), BF16),
            ((group, joint.shape[1]), BF16),
        ]
    return run_kernel(
        functools.partial(shared_kernel, forward, backward),
        [context["place"], *rows, *(grads if backward else []), joint, down],
        outputs,
        (),
        after,
        flops=2 * group * joint.size * (3 if backward else 1),
        name="shared",
        room=16,
    )


def z_turn(pieces, out):
    count = len(pieces)
    arrived = [pieces[0]]
    for turn in range(1, count):
        pairs = []
        for z in range(count):
            for core in range(2):
                to = (z + turn) % count
                if 0 <= (to if out else z) - core < TEAM_HEADS:
                    pairs.append((z * 2 + core, to * 2 + core))
        arrived.append(lax.ppermute(pieces[turn], ("z", "core"), pairs))
    return arrived


def to_heads(pieces, context):
    parts = context["parts"]
    if parts == 1:
        return z_turn(pieces, True)
    heads = jnp.stack([*pieces, jnp.zeros_like(pieces[0])])
    return [exchange(jnp.repeat(heads, parts, axis=0), "z")]


def attention_forward(arrived, after, context, stretch):
    parts = context["parts"]
    if parts == 1:
        rows, attended, wide, logs = fixed_attention(
            arrived, context["spans"][3], context["place"], stretch, after
        )
        return (exchange(attended, SEQ), (rows, wide, logs))
    (rows,) = arrived
    attended, wide, logs = attention(rows, context["spans"], stretch)
    count = context["deep"] * TEAM_SIZE
    attended = lax.dynamic_update_slice_in_dim(
        jnp.zeros((count, HEAD, stretch), BF16), attended, context["part"] * (count // parts), 0
    )
    back = exchange(attended, SEQ).reshape(TEAM_SIZE, parts, TEAM_SIZE, HEAD, stretch)
    back = back.astype(F32).sum(axis=1).astype(BF16)
    return (back.reshape(-1, HEAD, stretch), (rows, wide, logs))


def grads_to_heads(head_grads, context):
    parts = context["parts"]
    if parts > 1:
        stretch = head_grads.shape[2]
        head_grads = head_grads.reshape(TEAM_SIZE, TEAM_SIZE, HEAD, stretch)
        head_grads = jnp.repeat(head_grads, parts, axis=0).reshape(-1, HEAD, stretch)
    return exchange(head_grads, SEQ)


def attention_backward(grads, saved, after, context):
    parts = context["parts"]
    rows, wide, logs = saved
    if parts == 1:
        pieces = fixed_attention_back(
            rows, context["spans"][3], grads, wide, logs, context["place"], after
        )
        return (z_turn(pieces, False), pieces[0])
    count = grads.shape[0] // parts
    grads = lax.dynamic_slice_in_dim(grads, context["part"] * count, count, 0)
    rows_grad = attention_back(rows, context["spans"], grads, wide, logs, after)
    back = exchange(rows_grad, "z")
    back = back.reshape((TEAM_SIZE, parts) + back.shape[1:]).astype(F32).sum(axis=1).astype(BF16)
    return ([back[i] for i in range(TEAM_HEADS)], rows_grad)


def team_pieces(rows, member):
    pieces = rows.reshape(TEAM_SIZE, -1, rows.shape[1])
    parts = [lax.dynamic_index_in_dim(pieces, member ^ k, 0, keepdims=False) for k in range(4)]
    return [parts[0]] + [from_member(parts[k], k) for k in (1, 2, 3)]


def team_turn(rows, member):
    return in_order(jnp.stack(team_pieces(rows, member)), member)


def swap(rows):
    return lax.ppermute(rows, "dp", SWAP)


def beside(pairs):
    return jnp.concatenate(
        [(own.astype(F32) + other.astype(F32)).astype(BF16) for own, other in pairs], axis=1
    )


def z_sum(rows):
    return lax.psum_scatter(rows, "z", scatter_dimension=0, tiled=True)


def z_sum_direct(rows):
    count = lax.axis_size("z")
    if count > 4:
        return z_sum(rows)
    at = lax.axis_index("z")
    blocks = rows.reshape(count, -1, rows.shape[1])
    total = lax.dynamic_index_in_dim(blocks, at, 0, keepdims=False).astype(F32)
    for turn in range(1, count):
        block = lax.dynamic_index_in_dim(blocks, (at + turn) % count, 0, keepdims=False)
        block = lax.ppermute(block, "z", [(i, (i + turn) % count) for i in range(count)])
        total = total + block.astype(F32)
    return total.astype(BF16)


def to_team(parts):
    return [parts[0]] + [from_member(parts[k], k) for k in (1, 2, 3)]


def from_team(rows):
    return [rows] + [from_member(rows, k) for k in (1, 2, 3)]


def spread(rows, axes):
    count = lax.axis_size(axes)
    copies = jnp.broadcast_to(rows[None], (count,) + rows.shape)
    return exchange(copies, axes).reshape((-1,) + rows.shape[1:])


def dp_rows(rows):
    other = lax.ppermute(rows, "dp", SWAP)
    first = lax.axis_index("dp") == 0
    return jnp.concatenate([jnp.where(first, rows, other), jnp.where(first, other, rows)], axis=0)


def small_weights(gain_attn, gain_ffn, w_router):
    small = jnp.concatenate([gain_attn[:, :, None], gain_ffn[:, :, None], w_router], axis=2)
    small = small.transpose(1, 0, 2).reshape(gain_attn.shape[1], -1)
    return jnp.broadcast_to(small[None], (TEAM_SIZE,) + small.shape)


def split_small(smalls):
    weights = []
    for layer in range(LAYERS):
        part = smalls[:, layer * (2 + EXPERTS) : (layer + 1) * (2 + EXPERTS)]
        gains = part[:, :2].astype(F32).T
        weights.append(
            dict(
                gain_one=gains[0:1],
                gain_two=gains[1:2],
                router=jnp.pad(part, ((0, 0), (0, 128 - part.shape[1]))),
            )
        )
    return weights


def qkv_columns(w_qkv):
    width = w_qkv.shape[0]
    blocks = w_qkv.reshape(width, 3, TEAM_SIZE, TEAM_HEADS, HEAD)
    return blocks.transpose(2, 0, 3, 1, 4).reshape(TEAM_SIZE, width, -1)


def joint_columns(shared_gate_up):
    total = lax.axis_size(ALL)
    width = shared_gate_up.shape[0]
    blocks = shared_gate_up.reshape(width, 2, total // TEAM_SIZE, TEAM_SIZE, FF // total)
    return blocks.transpose(3, 0, 1, 2, 4).reshape(TEAM_SIZE, width, -1)


def down_rows(rows):
    return rows.reshape(-1, D)


def folded(w_out):
    return w_out.reshape(TEAM_SIZE * w_out.shape[0], -1)


def folded_down(shared_down):
    return shared_down.reshape(TEAM_SIZE * D // lax.axis_size(ALL), -1)


def out_rows(rows, member):
    width = D // lax.axis_size(ALL)
    rows = dp_rows(rows.reshape(-1, D))
    rows = in_order(jnp.stack(from_team(rows)), member)
    return rows.reshape(TEAM_SIZE, -1, width, D).transpose(1, 0, 2, 3).reshape(D, D)


def side_by_side(*arrays):
    return jnp.concatenate(arrays, axis=2)


def copies(rows):
    return jnp.broadcast_to(rows[None], (TEAM_SIZE,) + rows.shape)


def z_gather(rows):
    return lax.all_gather(rows, "z", axis=0, tiled=True)


def rest_gather(rows):
    return lax.all_gather(rows, REST, axis=0, tiled=True)


def dp_gather(rows, edges, token):
    parts = []
    for low, high in zip(edges, edges[1:]):
        token = dp_rows(later(rows[:, low:high], token))
        parts.append(token)
    return parts


def layers(
    x_in,
    cotangent,
    gain_attn,
    w_qkv,
    w_out,
    gain_ffn,
    w_router,
    shared_gate_up,
    shared_down,
    joint,
    down,
    context,
):
    split_count = context["split_count"]
    member = context["member"]
    stretch = x_in.shape[0]
    last = LAYERS - 1

    width = w_qkv.shape[1]
    qkv_width, joint_width = 3 * D // TEAM_SIZE, 2 * FF // TEAM_SIZE
    small = small_weights(gain_attn, gain_ffn, w_router)
    rows = side_by_side(qkv_columns(w_qkv[0]), small).reshape(TEAM_SIZE * width, -1)
    rows = team_turn(rows, member).reshape(TEAM_SIZE * width, -1)
    first_rows = spread(rows, "z")
    rows = exchange(joint_columns(shared_gate_up[0]), TEAM).reshape(TEAM_SIZE * width, -1)
    main_rows = jnp.concatenate([folded(w_out[0]), rows, folded_down(shared_down[0])], axis=1)
    main_rows = z_gather(later(main_rows, first_rows))
    if LAYERS > 1:
        rows = side_by_side(
            *[qkv_columns(w_qkv[layer]) for layer in range(1, LAYERS)],
            *[joint_columns(shared_gate_up[layer]) for layer in range(1, LAYERS)],
        )
        rows = team_turn(rows.reshape(TEAM_SIZE * width, -1), member)
        rows = rows.reshape(TEAM_SIZE * width, -1)
        edge = (LAYERS - 1) * qkv_width
        more_edges = [edge]
        for size in (D // TEAM_SIZE, joint_width):
            more_edges.append(more_edges[-1] + (LAYERS - 1) * size)
        more_rows = jnp.concatenate(
            [
                rows[:, :edge],
                *[folded(w_out[layer]) for layer in range(1, LAYERS)],
                rows[:, edge:],
                *[folded_down(shared_down[layer]) for layer in range(1, LAYERS)],
            ],
            axis=1,
        )
    first_rows = dp_rows(first_rows)
    weights = split_small(first_rows[:, qkv_width:])
    weights[0]["qkv"] = first_rows[:, :qkv_width]

    stream = x_in
    rows = from_team(x_in)
    grad_rows = from_team(cotangent)
    feeds = []
    for layer in range(LAYERS):
        mine = weights[layer]
        *pieces, team = qkv_step(
            rows,
            layer > 0,
            mine["gain_one"],
            mine["qkv"],
            (),
            context,
        )
        if layer == 0:
            at, held_rows = 0, main_rows
            edges = [0, D // TEAM_SIZE, D // TEAM_SIZE + joint_width]
        else:
            at, held_rows, edges = layer - 1, more_rows, more_edges
        columns = [
            held_rows[:, low + at * size : low + (at + 1) * size]
            for low, size in zip(edges, (D // TEAM_SIZE, joint_width, FF // TEAM_SIZE))
        ]
        after = grad_rows[1:] if layer == last else []
        if layer > 0:
            after = [*after, feeds[0]["other"]]
        mine["out"] = out_rows(later(columns[0], pieces[0]), member)
        at_heads = to_heads(pieces, context)
        back, attended = attention_forward(at_heads, after, context, stretch)
        if layer > 0:
            mine["joint"] = dp_rows(later(columns[1], attended[1]))
        if layer == 0 and LAYERS > 1:
            more_rows = z_gather(later(more_rows, attended[1]))
        middle, normed_ffn, gates, outgoing, mixed = feed_step(
            back,
            stream,
            mine["out"],
            mine["gain_two"],
            mine["router"],
            cotangent if layer == last else None,
            [mine["joint"]] if layer > 0 else [],
            context,
        )
        if layer == 0:
            mine["joint"] = dp_rows(later(columns[1], normed_ffn))
        down_padded = dp_rows(later(columns[2], normed_ffn))
        mine["down"] = down_rows(down_padded)
        arrived = send_rows(outgoing, split_count)
        other = swap(arrived)
        ffn_rows = from_team(normed_ffn)
        def branch(after):
            return shared_step(
                ffn_rows,
                grad_rows if layer == last else None,
                mine["joint"],
                mine["down"],
                True,
                after,
                context,
            )

        if layer == last:
            shared = branch([])
        returned = run_expert(
            layer,
            joint,
            down,
            (arrived, 0),
            (arrived, 1) if layer == last else None,
            True,
            [shared[0]] if layer == last else [*ffn_rows[1:], mine["joint"]],
        )
        if layer < last:
            shared = branch([returned])
        if layer == 0:
            for i in range(1, LAYERS):
                columns = more_rows[:, (i - 1) * qkv_width : i * qkv_width]
                weights[i]["qkv"] = dp_rows(later(columns, returned))
        returned = return_rows(returned, split_count)
        feed = dict(
            stream=stream,
            team=team,
            attended=attended,
            middle=middle,
            normed_ffn=normed_ffn,
            gates=gates,
            mixed=mixed,
            arrived=arrived,
            other=other,
            ffn_rows=ffn_rows,
        )
        feeds.append(feed)
        parts = to_team(shared[:4])
        if layer < last:
            stream, feed["gap"], normed = layer_end_step(
                returned, feed, parts, weights[layer + 1]["gain_one"], [weights[layer + 1]["qkv"]], context
            )
            rows = from_team(normed)

    upstream = cotangent
    terms = None
    unit = FF // lax.axis_size(ALL)
    feed_parts, head_parts = [None] * LAYERS, [None] * LAYERS
    for layer in reversed(range(LAYERS)):
        feed, mine = feeds[layer], weights[layer]
        arrived, other = feed["arrived"], feed["other"]
        if layer == last:
            grads, other_grads = (arrived, 1), (other, 1)
            shared_parts = shared_grads(shared, [parts[2]], context)
            output, middle_grad, attn_grad, head_grads, small = feed_back_step(
                returned,
                feed,
                upstream,
                parts,
                [],
                mine,
                True,
                [shared_parts[1], shared_parts[3]],
                context,
            )
        else:
            arrived_grad = send_rows(outgoing_grads, split_count)
            grads, other_grads = (arrived_grad, 0), (swap(arrived_grad), 0)
            grad_rows = from_team(upstream_rows)
            waited = [(waited[0][0], later(waited[0][1], grad_rows[2])), *waited[1:]]
            waited_sum = z_sum(beside(waited))
            waiting = [(own, swap(rows)) for own, rows in waiting]
            shared = shared_step(
                feed["ffn_rows"],
                grad_rows,
                mine["joint"],
                mine["down"],
                False,
                [terms[1]],
                context,
            )
            returned = run_expert(
                layer,
                joint,
                down,
                (arrived, 0),
                (arrived_grad, 0),
                False,
                [shared[0], *[rows for _, rows in waiting]],
            )
            returned = return_rows(returned, split_count)
            parts = to_team(shared[:4])
            shared_parts = shared_grads(shared, [parts[2], other_grads[0]], context)
            waiting = [(own, later(rows, parts[1], waited_sum)) for own, rows in waiting]
            waiting_sum = z_sum(beside(waiting))
            middle_grad, attn_grad, head_grads, small = feed_back_step(
                returned,
                feed,
                upstream,
                parts,
                [feed["gap"]],
                mine,
                False,
                [shared_parts[1], shared_parts[3], waited_sum],
                context,
            )
            terms = expert_grads(*rest_of_terms, terms, [attn_grad, other_grads[0]], context)
        joint_arrived, down_arrived = swap(shared_parts[1]), swap(shared_parts[3])
        at_heads = grads_to_heads(head_grads, context)
        if layer == 0:
            out_own, out_other = out_grads_step(feed["mixed"], attn_grad, [], context)
            out_arrived = swap(out_other)
            halves = [(shared_parts[0], later(joint_arrived, out_other))]
            shared_sum = z_sum(beside([*halves, (shared_parts[2], down_arrived)]))
        pieces, token = attention_backward(
            at_heads,
            feed["attended"],
            [waiting_sum, joint_arrived, down_arrived, terms[1]] if layer < last else [],
            context,
        )
        if layer > 0:
            out_own, out_other = out_grads_step(
                feed["mixed"], attn_grad, [pieces[min(1, len(pieces) - 1)]], context
            )
            out_arrived = swap(out_other)
        held = ((arrived, 0), grads), ((other, 0), other_grads)
        terms = expert_grads(layer, (0, 2), *held, joint, down, terms, [token], context)
        results = qkv_back_step(
            pieces,
            mine["qkv"],
            feed["team"],
            mine["gain_one"],
            small,
            True,
            [terms[1]] + ([down_arrived, joint_arrived] if layer > 0 else [out_arrived]),
            context,
        )
        normed_parts, packed = to_team(results[:4]), results[4:]
        if layer > 0:
            waiting = [packed]
            waited = [
                (out_own, out_arrived),
                (shared_parts[2], down_arrived),
                (shared_parts[0], joint_arrived),
            ]
            upstream, upstream_rows, outgoing_grads = layer_start_step(
                feed["stream"], middle_grad, mine["gain_one"], normed_parts, feeds[layer - 1], context
            )
            terms = expert_grads(
                layer, (2, 1), *held, joint, down, terms, [outgoing_grads], context
            )
            rest_of_terms = (layer, (3, 1), *held, joint, down)
        else:
            (upstream_rows,) = layer_start_step(
                feed["stream"], middle_grad, mine["gain_one"], normed_parts, None, context
            )
            qkv_arrived = swap(packed[1])
            out_sum = z_sum(beside([(out_own, later(out_arrived, packed[0]))]))
        if layer < last:
            head_parts[layer + 1] = team_pieces(waiting_sum, member)
            feed_parts[layer + 1][1] = team_pieces(waited_sum[:, :D], member)
            feed_parts[layer + 1][2] = waited_sum[:, D : D + FF // TEAM_SIZE].reshape(unit, D)
            feed_parts[layer + 1][0] = team_pieces(waited_sum[:, D + FF // TEAM_SIZE :], member)
        feed_parts[layer] = [None] * 3
        if layer == 0:
            feed_parts[0][0] = team_pieces(shared_sum[:, :joint_width], member)
            feed_parts[0][2] = shared_sum[:, joint_width:].reshape(unit, D)
        if layer == 0:
            terms = expert_grads(
                layer, (2, 2), *held, joint, down, terms, [packed[0], shared_sum], context
            )
            early = later(qkv_arrived, terms[1], *normed_parts[1:])
            qkv_sum = z_sum_direct(beside([(packed[0], early)]))
            head_parts[0] = team_pieces(qkv_sum, member)
            feed_parts[0][1] = team_pieces(later(out_sum, terms[1]), member)
    joint_sum, out_sum, down_sum = run_kernel(
        feed_end_kernel,
        [
            context["place"],
            *[piece for pieces, _, _ in feed_parts for piece in pieces],
            *[piece for _, pieces, _ in feed_parts for piece in pieces],
            *[rows for _, _, rows in feed_parts],
        ],
        [
            ((LAYERS, width, 2 * FF), F32),
            ((LAYERS, width, D), F32),
            ((LAYERS, unit, D), F32),
        ],
        [((TEAM_SIZE, width, joint_width), F32)],
        name="feed_end",
    )
    qkv_sum, small_sum = run_kernel(
        qkv_end_kernel,
        [context["place"], *[piece for pieces in head_parts for piece in pieces]],
        [((LAYERS, width, 3 * D), F32), ((LAYERS, width, 64), F32)],
        [((TEAM_SIZE, width, qkv_width + 64), F32)],
        name="qkv_end",
    )
    dense = (
        small_sum[:, :, 0],
        qkv_sum,
        out_sum,
        small_sum[:, :, 1],
        small_sum[:, :, 2 : 2 + EXPERTS],
        joint_sum,
        down_sum,
    )
    return (output, upstream_rows, dense, terms)


def query_spans(block_row, group, part, parts):
    length = block_row.shape[0]
    limit = jnp.sum((block_row[None, :] <= block_row[:, None]).astype(jnp.int32), axis=1)
    tiles = length // QUERY_TILE // parts
    base = part * tiles
    ends = lax.dynamic_slice_in_dim(limit.reshape(-1, QUERY_TILE), base, tiles, 0)
    full = ends[:, 0] // group
    some = (ends[:, -1] + group - 1) // group
    base = jnp.full((1,), base, jnp.int32)
    return (full, some, base, limit[None, :], tiles, parts)


def local(
    x_in,
    block_ids,
    expert_ids,
    cotangent,
    gain_attn,
    w_qkv,
    w_out,
    gain_ffn,
    w_router,
    shared_gate_up,
    shared_down,
    expert_gate_up,
    expert_down,
):
    stretch = x_in.shape[1]
    group = TEAM_SIZE * stretch
    deep = lax.axis_size("z")
    parts = max(1, deep // TEAM_SIZE)
    at = lax.axis_index("z")
    member = lax.axis_index("core") * lax.axis_size("ulysses") + lax.axis_index("ulysses")
    half_size = HEAD // 2
    spacing = 10000.0 ** (-jnp.arange(half_size).astype(F32) * 2.0 / HEAD)
    positions = (at * group + jnp.arange(group, dtype=jnp.int32)).astype(F32)
    angles = spacing[:, None] * positions[None, :]
    part = at % parts
    slots = route_slots(expert_ids[0])
    place = [member, at, lax.axis_index("core"), lax.axis_index("dp")]
    context = dict(
        member=member,
        place=jnp.stack(place).astype(jnp.int32),
        cosine=jnp.cos(angles),
        sine=jnp.sin(angles),
        ids=expert_ids[0],
        slots=slots,
        turned_slots=slots.T,
        parts=parts,
        part=part,
        deep=deep,
        split_count=deep * TEAM_SIZE // EXPERTS,
        spans=query_spans(block_ids[0], group, part, parts),
    )
    output, grad_x, dense, terms = layers(
        x_in[0],
        cotangent[0],
        gain_attn,
        w_qkv,
        w_out,
        gain_ffn,
        w_router,
        shared_gate_up,
        shared_down,
        expert_gate_up,
        expert_down,
        context,
    )
    return (output[None], grad_x[None], *dense, *terms)


def solution(mesh):
    dp, blk, ulysses = mesh.devices.shape
    grid = Mesh(mesh.devices.reshape(dp, blk // 2, 2, ulysses), ALL)
    rows = P("dp", SEQ, None)
    in_specs = (
        rows,
        P("dp", None),
        rows,
        rows,
        P(None, ALL),
        P(None, ALL, None),
        P(None, ALL, None),
        P(None, ALL),
        P(None, ALL, None),
        P(None, ALL, None),
        P(None, ALL, None),
        P(None, SEQ, None, None),
        P(None, SEQ, None, None),
    )
    out_specs = (
        rows,
        rows,
        P(None, ALL),
        P(None, ALL, None),
        P(None, ALL, None),
        P(None, ALL),
        P(None, ALL, None),
        P(None, ALL, None),
        P(None, ALL, None),
        P(None, SEQ, None, None),
        P(None, SEQ, None, None),
    )
    return jax.shard_map(local, mesh=grid, in_specs=in_specs, out_specs=out_specs, check_vma=False)
```
